128 devices in a mesh: blk: 8 (over z, core), leaf: 16 (over x, y).
Axes of the slice: x: 4, y: 4, z: 4, core: 2. Of those that a mesh axis runs over, the one named last changes fastest.
Arguments:
- modes: float32 [32768, 3, 256], P(('blk', 'leaf')), may hold values from -60 to 60
- stiffness: float32 [10, 3, 10, 3, 16384], P(None, None, None, None, ('blk', 'leaf')), may hold values from -0.5 to 3.5, as said below
- connect: int32 [10, 16384], P(None, ('blk', 'leaf')), may hold values from 0 to 767
- send_list: int32 [128, 4, 128], P(('blk', 'leaf')), may hold values from 0 to 255
- elem_count: int32 [128], P(('blk', 'leaf')), may hold values from 64 to 128, as said below
Outputs:
- q_panel: float32 [32768, 3, 512], P(('blk', 'leaf'))
- r_factor: float32 [512, 512], replicated
The draws below stay inside these ranges and needn't reach their ends.
Inputs may be any that keep to these rules, and one draw needn't show every extreme that they name: `elem_count`: the largest count equals 128. `stiffness`: symmetric under exchanging (k, c) with (l, c2).
All inputs are finite; a program needn't handle non-finite values.
Results may differ from the reference program's by a relative error of at most 0.0003.
Values sent between devices are 32-bit elements; how exact they have to be, the bound alone decides.
A program may use at most 128 MiB of HBM per device.

```python
import jax
import jax.numpy as jnp
from jax import lax

MODES = 256
NODE_DEV = 256
ELEM_DEV = 128
REACH = 2
MOST = 128
NODES = 32768
ELEMS = 16384
N_BLK = 8
N_LEAF = 16


def draw_modes(key, part):
    key = jax.random.fold_in(key, 11)
    key_base, key_cols = jax.random.split(key, 2)
    rise = jnp.arange(NODES, dtype=jnp.float32) / NODES
    col_scale = jnp.exp(jax.random.uniform(key_cols, (MODES,), jnp.float32, jnp.log(0.3), jnp.log(3.0)))
    base = jnp.clip(jax.random.normal(key_base, (NODES, 3, MODES), jnp.float32), -6.0, 6.0)
    values = base * (1.0 + 2.0 * rise)[:, None, None]
    return values * col_scale[None, None, :]


def draw_stiffness(key, part):
    key = jax.random.fold_in(key, 23)
    key_off, key_diag = jax.random.split(key)
    raw = jax.random.uniform(key_off, (10, 3, 10, 3, ELEMS), jnp.float32, -0.5, 0.5)
    sym = 0.5 * (raw + jnp.transpose(raw, (2, 3, 0, 1, 4)))
    diag = jnp.exp(jax.random.uniform(key_diag, (10, 3, ELEMS), jnp.float32, jnp.log(0.5), jnp.log(3.0)))
    node_eye = (jnp.arange(10)[:, None] == jnp.arange(10)[None, :]).astype(jnp.float32)
    comp_eye = (jnp.arange(3)[:, None] == jnp.arange(3)[None, :]).astype(jnp.float32)
    eye = node_eye[:, None, :, None, None] * comp_eye[None, :, None, :, None]
    return sym + eye * diag[:, :, None, None, :]


def draw_elem_count(key, part):
    key = jax.random.fold_in(key, 37)
    key_counts, key_full = jax.random.split(key)
    counts = jax.random.randint(key_counts, (N_BLK * N_LEAF,), ELEM_DEV // 2, ELEM_DEV + 1)
    fullest = jax.random.randint(key_full, (), 0, N_BLK * N_LEAF)
    return counts.at[fullest].set(ELEM_DEV).astype(jnp.int32)


def with_ends(array, rng, smallest, top_value):
    place = [jax.random.randint(jax.random.fold_in(rng, axis), (), 0, length) for axis, length in enumerate(array.shape)]
    main_axis = array.shape.index(max(array.shape))
    beside = place[:main_axis] + [(place[main_axis] + 1) % array.shape[main_axis]] + place[main_axis + 1:]
    return array.at[tuple(place)].set(smallest).at[tuple(beside)].set(top_value)


def setup_inputs(seed: int = 0) -> dict:
    streams_of = jax.random.split(jax.random.key(seed), 6)
    return {
        "modes": draw_modes(jax.random.fold_in(streams_of[5], 71), 0),
        "stiffness": draw_stiffness(jax.random.fold_in(streams_of[5], 71), 0),
        "connect": with_ends(jax.random.randint(streams_of[2], (10, ELEMS), 0, NODE_DEV + 2 * REACH * MOST), jax.random.fold_in(streams_of[2], 1), 0, (NODE_DEV + 2 * REACH * MOST) - 1).astype(jnp.int32),
        "send_list": with_ends(jax.random.randint(streams_of[3], (N_BLK * N_LEAF, 2 * REACH, MOST), 0, NODE_DEV), jax.random.fold_in(streams_of[3], 1), 0, NODE_DEV - 1).astype(jnp.int32),
        "elem_count": draw_elem_count(jax.random.fold_in(streams_of[5], 71), 0),
    }


def direction_offsets():
    steps = jnp.arange(2 * REACH, dtype=jnp.int32)
    return steps - REACH + (steps >= REACH).astype(jnp.int32)

def reference(modes, stiffness, connect, send_list, elem_count):
    device_total = N_BLK * N_LEAF
    mode_width = modes.shape[2]
    offsets = direction_offsets()
    padded = jnp.concatenate([modes, jnp.zeros((1, 3, mode_width), jnp.float32)], axis=0)
    stiff_all = jnp.zeros((NODES + 1, 3, mode_width), jnp.float32)

    def per_device(device, stiff_acc):
        senders = device - offsets
        valid = (senders >= 0) & (senders < device_total)
        clipped = jnp.clip(senders, 0, device_total - 1).astype(jnp.int32)
        shared = send_list[clipped, jnp.arange(2 * REACH, dtype=jnp.int32)]
        ghost_ids = jnp.where(valid[:, None], clipped[:, None] * NODE_DEV + shared, NODES).reshape(-1)
        own_ids = device * NODE_DEV + jnp.arange(NODE_DEV, dtype=jnp.int32)
        table_ids = jnp.concatenate([own_ids, ghost_ids.astype(jnp.int32)]).astype(jnp.int32)
        local_conn = lax.dynamic_slice_in_dim(connect, device * ELEM_DEV, ELEM_DEV, 1)
        blocks = lax.dynamic_slice_in_dim(stiffness, device * ELEM_DEV, ELEM_DEV, 4)
        positions = jnp.arange(ELEM_DEV, dtype=jnp.int32)
        blocks = jnp.where(positions < elem_count[device], blocks, 0.0)
        node_ids = table_ids[local_conn]
        gathered = padded[node_ids]
        product = jnp.einsum('kcldE,lEdm->kEcm', blocks, gathered, precision=lax.Precision.HIGHEST)
        return stiff_acc.at[node_ids].add(product)
    stiff_all = lax.fori_loop(0, device_total, per_device, stiff_all)[:NODES]
    panel = jnp.concatenate([modes, stiff_all], axis=2)
    columns = panel.shape[2]
    grouped = panel.reshape(device_total, 3 * NODE_DEV, columns)

    def add_gram(index, gram):
        part = grouped[index]
        return gram + jnp.einsum('rc,rd->cd', part, part, precision=lax.Precision.HIGHEST)
    gram = lax.fori_loop(0, device_total, add_gram, jnp.zeros((columns, columns), jnp.float32))
    lower = jnp.linalg.cholesky(gram)
    scale = jnp.sqrt(jnp.float32(3 * NODES))

    def solve_group(part):
        return jax.scipy.linalg.solve_triangular(lower, part.T, lower=True).T
    q_panel = lax.map(solve_group, grouped).reshape(NODES, 3, columns) * scale
    r_factor = lower.T / scale
    return (q_panel, r_factor)
```

```python
import functools

import jax
import jax.numpy as jnp
from jax import lax
from jax.experimental import pallas as pl
from jax.experimental.pallas import tpu as pltpu
from jax.sharding import PartitionSpec as P

HIGH = lax.Precision.HIGHEST
F32 = jnp.float32
BF16 = jnp.bfloat16
MESH = pl.DeviceIdType.MESH
VMEM = pl.BlockSpec(memory_space=pltpu.VMEM)
SMEM = pl.BlockSpec(memory_space=pltpu.SMEM)
LIMIT = 56 * 1024 * 1024


def dot(a, b, ca, cb, precision=None):
    return lax.dot_general(a, b, (((ca,), (cb,)), ((), ())), precision=precision, preferred_element_type=F32)


def split2(x):
    hi = x.astype(BF16)
    return hi, (x - hi.astype(F32)).astype(BF16)


def split3(x):
    hi = x.astype(BF16)
    rest = x - hi.astype(F32)
    mid = rest.astype(BF16)
    return hi, mid, (rest - mid.astype(F32)).astype(BF16)


def columns_of(rows, count):
    padded = jnp.concatenate([rows.astype(F32), jnp.zeros((16 - count, 128), F32)], axis=0)
    return padded.T


N_LEAF = 16
N_BLK = 8
CHUNK = 24


def greet(leaf, blk):
    barrier = pltpu.get_barrier_semaphore()
    for k in range(1, N_LEAF):
        pl.semaphore_signal(barrier, inc=1, device_id={"leaf": lax.rem(leaf + k, N_LEAF)}, device_id_type=MESH)
    for k in range(1, N_BLK):
        pl.semaphore_signal(barrier, inc=1, device_id={"blk": lax.rem(blk + k, N_BLK)}, device_id_type=MESH)
    return barrier


class Sum:
    def __init__(self, leaf, blk, local, near, far, total, leaf_sems, blk_sems):
        self.leaf, self.blk = leaf, blk
        self.local, self.near, self.far, self.total = local, near, far, total
        mine = pl.ds(pl.multiple_of(leaf * CHUNK, 8), CHUNK)
        self.mine = mine
        self.spread, self.cross, self.collect = [], [], []
        for k in range(1, N_LEAF):
            peer = lax.rem(leaf + k, N_LEAF)
            self.spread.append(pltpu.make_async_remote_copy(
                src_ref=local.at[pl.ds(pl.multiple_of(peer * CHUNK, 8), CHUNK)], dst_ref=near.at[k],
                send_sem=leaf_sems.at[0, k], recv_sem=leaf_sems.at[1, k], device_id={"leaf": peer}, device_id_type=MESH))
            self.collect.append(pltpu.make_async_remote_copy(
                src_ref=total.at[mine], dst_ref=total.at[mine],
                send_sem=leaf_sems.at[2, k], recv_sem=leaf_sems.at[3, k], device_id={"leaf": peer}, device_id_type=MESH))
        for k in range(1, N_BLK):
            peer = lax.rem(blk + k, N_BLK)
            self.cross.append(pltpu.make_async_remote_copy(
                src_ref=far.at[blk], dst_ref=far.at[blk],
                send_sem=blk_sems.at[0, k], recv_sem=blk_sems.at[1, k], device_id={"blk": peer}, device_id_type=MESH))

    def begin(self, top, low, bottom):
        self.local[0:128, :] = top
        self.local[128:256, :] = low
        self.local[256:384, :] = bottom
        for copy in self.spread:
            copy.start()

    def across(self):
        part = self.local[self.mine, :]
        for k, copy in enumerate(self.spread):
            copy.wait_recv()
            part = part + self.near[k + 1]
        self.far[self.blk] = part
        for copy in self.cross:
            copy.start()

    def gather(self):
        for copy in self.cross:
            copy.wait_recv()
        part = self.far[0]
        for b in range(1, N_BLK):
            part = part + self.far[b]
        self.total[self.mine, :] = part
        for copy in self.collect:
            copy.start()

    def end(self):
        for copy in self.collect:
            copy.wait_recv()

    def drain(self):
        for copy in self.spread + self.cross + self.collect:
            copy.wait_send()


def sum_scratch():
    return [
        pltpu.VMEM((384, 128), F32),
        pltpu.VMEM((N_LEAF, CHUNK, 128), F32),
        pltpu.VMEM((N_BLK, CHUNK, 128), F32),
        pltpu.VMEM((384, 128), F32),
        pltpu.SemaphoreType.DMA((4, N_LEAF)),
        pltpu.SemaphoreType.DMA((2, N_BLK)),
    ]


class AxisSum:
    def __init__(self, leaf, blk, local, along_x, part, along_y, far, total, sems, blk_sems):
        self.blk, self.local, self.part, self.total = blk, local, part, total
        self.along_x, self.along_y, self.far = along_x, along_y, far
        x, y = lax.div(leaf, 4), lax.rem(leaf, 4)
        wide, slim = 4 * CHUNK, CHUNK
        self.wide = pl.ds(pl.multiple_of(x * wide, 8), wide)
        self.slim = pl.ds(pl.multiple_of(y * slim, 8), slim)
        self.mine = pl.ds(pl.multiple_of(leaf * slim, 8), slim)
        self.stages = [[], [], [], [], []]

        def copy(stage, k, src, dst, sem, peer):
            self.stages[stage].append(pltpu.make_async_remote_copy(
                src_ref=src, dst_ref=dst, send_sem=sem.at[0, k], recv_sem=sem.at[1, k],
                device_id=peer, device_id_type=MESH))

        for k in range(1, 4):
            px, py = lax.rem(x + k, 4), lax.rem(y + k, 4)
            beside, above = {"leaf": px * 4 + y}, {"leaf": x * 4 + py}
            copy(0, k, local.at[pl.ds(pl.multiple_of(px * wide, 8), wide)], along_x.at[k], sems.at[0], beside)
            copy(1, k, part.at[pl.ds(pl.multiple_of(py * slim, 8), slim)], along_y.at[k], sems.at[1], above)
            copy(3, k, total.at[self.mine], total.at[self.mine], sems.at[2], above)
            copy(4, k, total.at[self.wide], total.at[self.wide], sems.at[3], beside)
        for k in range(1, N_BLK):
            copy(2, k, far.at[blk], far.at[blk], blk_sems, {"blk": lax.rem(blk + k, N_BLK)})

    def start(self, stage):
        for copy in self.stages[stage]:
            copy.start()

    def wait(self, stage):
        for copy in self.stages[stage]:
            copy.wait_recv()

    def begin(self, top, low, bottom):
        self.local[0:128, :] = top
        self.local[128:256, :] = low
        self.local[256:384, :] = bottom
        self.start(0)

    def second(self):
        self.wait(0)
        part = self.local[self.wide, :]
        for k in range(1, 4):
            part = part + self.along_x[k]
        self.part[...] = part
        self.start(1)

    def third(self):
        self.wait(1)
        part = self.part[self.slim, :]
        for k in range(1, 4):
            part = part + self.along_y[k]
        self.far[self.blk] = part
        self.start(2)

    def fourth(self):
        self.wait(2)
        part = self.far[0]
        for b in range(1, N_BLK):
            part = part + self.far[b]
        self.total[self.mine, :] = part
        self.start(3)

    def fifth(self):
        self.wait(3)
        self.start(4)

    def end(self):
        self.wait(4)

    def drain(self):
        for stage in self.stages:
            for copy in stage:
                copy.wait_send()


def axis_sum_scratch():
    return [
        pltpu.VMEM((384, 128), F32),
        pltpu.VMEM((4, 4 * CHUNK, 128), F32),
        pltpu.VMEM((4 * CHUNK, 128), F32),
        pltpu.VMEM((4, CHUNK, 128), F32),
        pltpu.VMEM((N_BLK, CHUNK, 128), F32),
        pltpu.VMEM((384, 128), F32),
        pltpu.SemaphoreType.DMA((4, 2, 4)),
        pltpu.SemaphoreType.DMA((2, N_BLK)),
    ]


SIDE = 256
BLOCK = 64


def unpack(packed):
    top, low, bottom = packed[0:128, :], packed[128:256, :], packed[256:384, :]
    return jnp.concatenate([jnp.concatenate([top, low.T], axis=1), jnp.concatenate([low, bottom], axis=1)], axis=0)


def factor_start(work, gram):
    work[:, 0:SIDE] = gram
    work[:, SIDE:] = (
        lax.broadcasted_iota(jnp.int32, (SIDE, SIDE), 0) == lax.broadcasted_iota(jnp.int32, (SIDE, SIDE), 1)
    ).astype(F32)


def factor(work, first, last):
    sub = lax.broadcasted_iota(jnp.int32, (8, 128), 0)
    for start in range(first, last, BLOCK):
        left = start // 128 * 128
        right = SIDE + -(-(start + BLOCK) // 128) * 128
        if start:
            update = dot(work[0:start, start : start + BLOCK], work[0:start, left:right], 0, 0, HIGH)
            work[start : start + BLOCK, left:right] = work[start : start + BLOCK, left:right] - update
        tiles = (right - left) // 128
        count = BLOCK // 8
        x = [[work[start + 8 * t : start + 8 * t + 8, left + 128 * i : left + 128 * (i + 1)] for i in range(tiles)]
             for t in range(count)]
        for p in range(count):
            tile, lane = divmod(start + 8 * p - left, 128)
            rest = range(p, count)
            col = [{t: jnp.broadcast_to(x[t][tile][:, lane + j : lane + j + 1], (8, 128)) for t in rest} for j in range(8)]
            entry = {(i, k): jnp.broadcast_to(col[k][p][i : i + 1, :], (8, 128)) for k in range(8) for i in range(k, 8)}
            for j in range(8):
                inverse = lax.rsqrt(entry[j, j])
                scaled = {k: entry[k, j] * inverse for k in range(j + 1, 8)}
                low = {t: col[j][t] * inverse for t in rest}
                for k in range(j + 1, 8):
                    for i in range(k, 8):
                        entry[i, k] = entry[i, k] - scaled[i] * scaled[k]
                    for t in rest:
                        col[k][t] = col[k][t] - low[t] * scaled[k]
                for i in range(tiles):
                    row = jnp.broadcast_to(x[p][i][j : j + 1, :], (8, 128)) * inverse
                    for t in rest:
                        moved = x[t][i] - low[t] * row
                        if t == p:
                            moved = jnp.where(sub > j, moved, jnp.where(sub == j, row, x[t][i]))
                        x[t][i] = moved
            for i in range(tiles):
                work[start + 8 * p : start + 8 * p + 8, left + 128 * i : left + 128 * (i + 1)] = x[p][i]


def upper(x):
    keep = lax.broadcasted_iota(jnp.int32, (SIDE, SIDE), 0) <= lax.broadcasted_iota(jnp.int32, (SIDE, SIDE), 1)
    return jnp.where(keep, x, 0.0)


TOTAL = N_LEAF * N_BLK
STEPS = (-1, 1)


class Exchange:
    def __init__(self, device, near, far, relay, near_to, far_to, sems):
        self.near_to, self.far_to = near_to, far_to
        self.direct, self.away, self.onward = [], [], []
        self.one, self.two, self.from_one, self.from_two = [], [], [], []
        self.between = (device >= 1) & (device < TOTAL - 1)
        for u, step in enumerate(STEPS):
            peer = lax.rem(device + step + TOTAL, TOTAL)
            there = (lax.div(peer, N_LEAF), lax.rem(peer, N_LEAF))

            def copy(kind, src, dst):
                return pltpu.make_async_remote_copy(
                    src_ref=src, dst_ref=dst, send_sem=sems.at[0, kind, u], recv_sem=sems.at[1, kind, u],
                    device_id=there, device_id_type=MESH)

            self.direct.append(copy(0, near[u], near_to[u]))
            self.away.append(copy(1, far[u], relay.at[u]))
            self.onward.append(copy(2, relay.at[u], far_to[u]))
            self.one.append(self.within(device + step))
            self.two.append(self.within(device + 2 * step))
            self.from_one.append(self.within(device - step))
            self.from_two.append(self.within(device - 2 * step))

    def within(self, device):
        return (device >= 0) & (device < TOTAL)

    def send_far(self):
        for u in range(2):
            pl.when(self.two[u])(self.away[u].start)

    def send_near(self):
        for u in range(2):
            pl.when(self.one[u])(self.direct[u].start)

    def forward(self):
        for u in range(2):
            @pl.when(self.between)
            def _():
                self.away[u].wait_recv()
                self.onward[u].start()

    def receive(self, arrives, copy, to):
        pl.when(arrives)(copy.wait_recv)

        @pl.when(jnp.logical_not(arrives))
        def _():
            to[...] = jnp.zeros(to.shape, F32)

    def receive_near(self):
        for u in range(2):
            self.receive(self.from_one[u], self.direct[u], self.near_to[u])

    def receive_far(self):
        for u in range(2):
            self.receive(self.from_two[u], self.onward[u], self.far_to[u])

    def drain(self):
        for u in range(2):
            pl.when(self.two[u])(self.away[u].wait_send)
            pl.when(self.one[u])(self.direct[u].wait_send)
            pl.when(self.between)(self.onward[u].wait_send)


STORED = (512, 256, 384, 640)
NEAR_OUT, FAR_OUT = (1, 2), (0, 3)
NEAR_BACK, FAR_BACK = (2, 1), (3, 0)


def main_kernel(count, modes, stiffness, connect, send, g22_out, low_out, rest_out, r_out, q_out,
                outgoing, table, relay, acc, incoming, relay_back, halo_sems, back_sems,
                ext_hi, ext_lo, pick, place, taken, blocks, matrix_hi, matrix_lo, product, stiff, work, *sums):
    leaf, blk = lax.axis_index("leaf"), lax.axis_index("blk")
    device = blk * N_LEAF + leaf
    barrier = greet(leaf, blk)

    def rows_of(ref, h, j):
        return ref.at[h, pl.ds(STORED[j], 128)]

    halo, back = [], []
    for h in range(2):
        halo.append(Exchange(
            device, [outgoing.at[h, j] for j in NEAR_OUT], [outgoing.at[h, j] for j in FAR_OUT], relay.at[h],
            [rows_of(table, h, j) for j in NEAR_OUT], [rows_of(table, h, j) for j in FAR_OUT], halo_sems.at[h]))
        back.append(Exchange(
            device, [rows_of(acc, h, j) for j in NEAR_BACK], [rows_of(acc, h, j) for j in FAR_BACK], relay_back.at[h],
            [incoming.at[h, j] for j in NEAR_BACK], [incoming.at[h, j] for j in FAR_BACK], back_sems.at[h]))
    greeted = N_LEAF + N_BLK - 2
    for u, step in enumerate(STEPS):
        peer = lax.rem(device + step + TOTAL, TOTAL)
        there = (lax.div(peer, N_LEAF), lax.rem(peer, N_LEAF))
        greeted = greeted + halo[0].from_one[u].astype(jnp.int32)

        @pl.when(halo[0].one[u])
        def _():
            pl.semaphore_signal(barrier, inc=1, device_id=there, device_id_type=MESH)

    first = AxisSum(leaf, blk, *sums[0:8])
    cross = AxisSum(leaf, blk, *sums[8:16])
    last = Sum(leaf, blk, *sums[16:22])

    chosen = send[...]
    columns = columns_of(chosen, 4)
    nodes = lax.broadcasted_iota(jnp.int32, (128, 256), 1).astype(F32)
    choosers = [(columns[:, j : j + 1] == nodes).astype(BF16) for j in range(4)]

    def prepare(h):
        wide = jnp.concatenate([modes[c, :, 128 * h : 128 * (h + 1)] for c in range(3)], axis=1)
        parts = split3(wide)
        for j in FAR_OUT + NEAR_OUT:
            outgoing[h, j] = sum(dot(choosers[j], part, 1, 0) for part in parts)
        table[h, 0:256, :] = wide
        ext_hi[h, 0:256, :], ext_lo[h, 0:256, :] = parts[0], parts[1]

    prepare(0)
    pl.semaphore_wait(barrier, greeted)
    halo[0].send_far()
    halo[0].send_near()
    prepare(1)
    gram = sum(dot(modes[c], modes[c], 0, 0, HIGH) for c in range(3))
    first.begin(gram[0:128, 0:128], gram[128:256, 0:128], gram[128:256, 128:256])

    conn = connect[...]
    columns = columns_of(conn, 10)

    def table_id(at):
        return jnp.where(at < 256, at, jnp.where(at < 512, at + 128, jnp.where(at < 640, at - 256, at)))

    lanes = table_id(lax.broadcasted_iota(jnp.int32, (128, 768), 1)).astype(F32)
    rows = table_id(lax.broadcasted_iota(jnp.int32, (768, 128), 0))
    for k in range(10):
        pick[128 * k : 128 * (k + 1), :] = (columns[:, k : k + 1] == lanes).astype(BF16)
        place[:, 128 * k : 128 * (k + 1)] = (rows == conn[k : k + 1, :]).astype(BF16)

    halo[0].forward()
    halo[1].send_far()
    halo[1].send_near()

    def gather(h, part):
        span = slice(256 * part, 256 * (part + 1))
        if part:
            ext_hi[h, span, :], ext_lo[h, span, :] = split2(table[h, span, :])

        def body(step, carry):
            at = pl.ds(pl.multiple_of(step * 320, 320), 320)
            picked = pick[at, span]
            found = dot(picked, ext_hi[h, span, :], 1, 0) + dot(picked, ext_lo[h, span, :], 1, 0)
            taken[h, at, :] = found if part == 0 else taken[h, at, :] + found
            return carry

        lax.fori_loop(0, 4, body, 0)

    gather(0, 0)
    gather(1, 0)
    first.second()

    live = lax.broadcasted_iota(jnp.int32, (30, 128), 1) < count[0]
    source = lax.broadcasted_iota(jnp.int32, (30, 256), 0)
    target = lax.broadcasted_iota(jnp.int32, (30, 256), 1)
    wanted = lax.rem(source, 3) * 10 + lax.div(source, 3)
    spread = (lax.shift_right_logical(target, 3) == wanted).astype(BF16)
    for k in range(10):
        for c in range(3):
            block = jnp.concatenate([stiffness[k, c, l] for l in range(10)], axis=0)
            hi, lo = split2(jnp.where(live, block, 0.0))
            blocks[10 * c + k] = dot(hi, spread, 0, 0) + dot(lo, spread, 0, 0)

    keep = lax.broadcasted_iota(jnp.int32, (8, 256), 0) == lax.rem(lax.broadcasted_iota(jnp.int32, (8, 256), 1), 8)

    def assemble(g, carry):
        at = pl.ds(pl.multiple_of(g * 8, 8), 8)
        matrix = jnp.concatenate([jnp.where(keep, blocks[n, at, :], 0.0) for n in range(30)], axis=0)
        matrix_hi[g], matrix_lo[g] = split2(matrix)
        return carry

    lax.fori_loop(0, 16, assemble, 0)
    first.third()

    def multiply(h):
        def group(g, carry):
            spans = [pl.ds(pl.multiple_of(128 * k + g * 8, 8), 8) for k in range(10)]
            vectors = jnp.concatenate(
                [taken[h, spans[l], 128 * d : 128 * (d + 1)] for d in range(3) for l in range(10)]
                + [jnp.zeros((16, 128), F32)],
                axis=0,
            )
            v_hi, v_lo = split2(vectors)
            m_hi, m_lo = matrix_hi[g], matrix_lo[g]
            result = dot(m_hi, v_hi, 1, 0) + (dot(m_hi, v_lo, 1, 0) + dot(m_lo, v_hi, 1, 0))
            for c in range(3):
                for k in range(10):
                    n = 10 * c + k
                    product[spans[k], 128 * c : 128 * (c + 1)] = result[8 * n : 8 * n + 8, :]
            return carry

        lax.fori_loop(0, 16, group, 0, unroll=2)
        return split2(product[...])

    def scatter(h, halves, span):
        where = place[span, :]
        acc[h, span, :] = dot(where, halves[0], 1, 0) + dot(where, halves[1], 1, 0)

    OWN, NEAR, FAR = slice(0, 256), slice(256, 512), slice(512, 768)

    halo[0].receive_near()
    gather(0, 1)
    halo[0].receive_far()
    gather(0, 2)
    first.fourth()
    halves = multiply(0)
    scatter(0, halves, FAR)
    back[0].send_far()
    halo[1].forward()
    scatter(0, halves, NEAR)
    back[0].send_near()
    scatter(0, halves, OWN)
    first.fifth()
    halo[1].receive_near()
    gather(1, 1)
    halo[1].receive_far()
    gather(1, 2)
    halves = multiply(1)
    scatter(1, halves, FAR)
    back[1].send_far()
    back[0].forward()
    scatter(1, halves, NEAR)
    back[1].send_near()
    scatter(1, halves, OWN)

    def against(a, b):
        spans = [slice(128 * c, 128 * (c + 1)) for c in range(3)]
        return sum(dot(acc[a, :, s], table[b, :, s], 0, 0, HIGH) for s in spans)

    cross.begin(against(0, 0), against(1, 0), against(1, 1))

    first.end()
    factor_start(work, unpack(first.total[...]))
    factor(work, 0, 64)
    cross.second()
    factor(work, 64, 128)
    back[1].forward()
    factor(work, 128, 192)
    cross.third()
    factor(work, 192, 256)
    r_out[...] = upper(work[:, 0:SIDE])
    inv = work[:, SIDE:]
    cross.fourth()
    for c in range(3):
        q_out[c] = dot(modes[c], inv, 1, 1, HIGH)

    rows = lax.broadcasted_iota(jnp.int32, (256, 128), 0)
    to_own = jnp.concatenate([(rows == chosen[j : j + 1, :]).astype(BF16) for j in range(4)], axis=1)

    def complete(h):
        back[h].receive_near()
        back[h].receive_far()
        parts = split3(jnp.concatenate([incoming[h, j] for j in range(4)], axis=0))
        whole = acc[h, OWN, :] + sum(dot(to_own, part, 1, 0) for part in parts)
        for c in range(3):
            stiff[c, :, 128 * h : 128 * (h + 1)] = whole[:, 128 * c : 128 * (c + 1)]

    complete(0)
    top = sum(dot(stiff[c, :, 0:128], stiff[c, :, 0:128], 0, 0, HIGH) for c in range(3))
    cross.fifth()
    complete(1)
    bottom = sum(dot(stiff[c, :, 128:256], stiff[c], 0, 0, HIGH) for c in range(3))
    last.begin(top, bottom[:, 0:128], bottom[:, 128:256])

    cross.end()
    low = dot(unpack(cross.total[...]), inv, 1, 1, HIGH)
    low_out[...] = low
    last.across()
    for c in range(3):
        rest_out[c] = stiff[c] - dot(q_out[c], low, 1, 1, HIGH)
    last.gather()
    for h in range(2):
        halo[h].drain()
        back[h].drain()
    first.drain()
    cross.drain()
    last.end()
    last.drain()
    g22_out[...] = last.total[...]


def up_to_last_gram(count, modes, stiffness, connect, send):
    square = jax.ShapeDtypeStruct((SIDE, SIDE), F32)
    tall = jax.ShapeDtypeStruct((3, 256, 256), F32)
    rows = pltpu.VMEM((2, 4, 128, 384), F32)
    table = pltpu.VMEM((2, 768, 384), F32)
    relay = pltpu.VMEM((2, 2, 128, 384), F32)
    sems = pltpu.SemaphoreType.DMA((2, 2, 3, 2))
    return pl.pallas_call(
        main_kernel,
        out_shape=[jax.ShapeDtypeStruct((384, 128), F32), square, tall, square, tall],
        in_specs=[SMEM] + [VMEM] * 4,
        out_specs=[VMEM] * 5,
        scratch_shapes=[
            rows, table, relay, table, rows, relay, sems, sems,
            pltpu.VMEM((2, 768, 384), BF16),
            pltpu.VMEM((2, 768, 384), BF16),
            pltpu.VMEM((1280, 768), BF16),
            pltpu.VMEM((768, 1280), BF16),
            pltpu.VMEM((2, 1280, 384), F32),
            pltpu.VMEM((30, 128, 256), F32),
            pltpu.VMEM((16, 240, 256), BF16),
            pltpu.VMEM((16, 240, 256), BF16),
            pltpu.VMEM((1280, 384), F32),
            pltpu.VMEM((3, 256, 256), F32),
            pltpu.VMEM((SIDE, 2 * SIDE), F32),
        ] + axis_sum_scratch() * 2 + sum_scratch(),
        compiler_params=pltpu.CompilerParams(collective_id=1, has_side_effects=True, vmem_limit_bytes=LIMIT),
        name="up_to_last_gram",
    )(count, modes, stiffness, connect, send)


def second_kernel(scale, g22, low, r11, q1, rest, q_out, r_out, work):
    lower = low[...]
    factor_start(work, unpack(g22[...]) - dot(lower, lower, 1, 1, HIGH))
    factor(work, 0, SIDE)
    r_out[0:SIDE, 0:SIDE] = r11[...] / scale
    r_out[0:SIDE, SIDE:] = lower.T / scale
    r_out[SIDE:, 0:SIDE] = jnp.zeros((SIDE, SIDE), F32)
    r_out[SIDE:, SIDE:] = upper(work[:, 0:SIDE]) / scale
    inv = work[:, SIDE:]
    for c in range(3):
        q_out[c, :, 0:SIDE] = q1[c] * scale
        q_out[c, :, SIDE:] = dot(rest[c], inv, 1, 1, HIGH) * scale


def second(scale, *operands):
    return pl.pallas_call(
        functools.partial(second_kernel, scale),
        out_shape=[jax.ShapeDtypeStruct((3, 256, 512), F32), jax.ShapeDtypeStruct((512, 512), F32)],
        in_specs=[VMEM] * len(operands),
        out_specs=[VMEM] * 2,
        scratch_shapes=[pltpu.VMEM((SIDE, 2 * SIDE), F32)],
        compiler_params=pltpu.CompilerParams(vmem_limit_bytes=LIMIT),
        name="second_factor",
    )(*operands)


def shards(modes, stiffness, connect, send_list, elem_count):
    modes = jnp.transpose(modes, (1, 0, 2))
    g22, low, rest, r11, q1 = up_to_last_gram(elem_count, modes, stiffness, connect, send_list[0])
    scale = float((3 * 256 * lax.axis_size("blk") * lax.axis_size("leaf")) ** 0.5)
    q, r = second(scale, g22, low, r11, q1, rest)
    return (jnp.transpose(q, (1, 0, 2)), r)


def solution(mesh):
    placed = (
        P(("blk", "leaf"), None, None),
        P(None, None, None, None, ("blk", "leaf")),
        P(None, ("blk", "leaf")),
        P(("blk", "leaf"), None, None),
        P(("blk", "leaf")),
    )
    return jax.shard_map(
        shards,
        mesh=mesh,
        in_specs=placed,
        out_specs=(P(("blk", "leaf"), None, None), P()),
        check_vma=False,
    )
```

```python
import functools

import jax
import jax.numpy as jnp
from jax import lax
from jax.experimental import pallas as pl
from jax.experimental.pallas import tpu as pltpu
from jax.sharding import PartitionSpec as P

HIGH = lax.Precision.HIGHEST
F32 = jnp.float32
BF16 = jnp.bfloat16
MESH = pl.DeviceIdType.MESH
VMEM = pl.BlockSpec(memory_space=pltpu.VMEM)
SMEM = pl.BlockSpec(memory_space=pltpu.SMEM)
LIMIT = 56 * 1024 * 1024


def dot(a, b, ca, cb, precision=None):
    return lax.dot_general(a, b, (((ca,), (cb,)), ((), ())), precision=precision, preferred_element_type=F32)


def split2(x):
    hi = x.astype(BF16)
    return hi, (x - hi.astype(F32)).astype(BF16)


def split3(x):
    hi = x.astype(BF16)
    rest = x - hi.astype(F32)
    mid = rest.astype(BF16)
    return hi, mid, (rest - mid.astype(F32)).astype(BF16)


def columns_of(rows, count):
    padded = jnp.concatenate([rows.astype(F32), jnp.zeros((16 - count, 128), F32)], axis=0)
    return padded.T


N_LEAF = 16
N_BLK = 8


def greet(leaf, blk):
    barrier = pltpu.get_barrier_semaphore()
    for k in range(1, N_LEAF):
        pl.semaphore_signal(barrier, inc=1, device_id={"leaf": lax.rem(leaf + k, N_LEAF)}, device_id_type=MESH)
    for k in range(1, N_BLK):
        pl.semaphore_signal(barrier, inc=1, device_id={"blk": lax.rem(blk + k, N_BLK)}, device_id_type=MESH)
    return barrier


class Sum:
    def __init__(self, leaf, blk, local, near, far, total, leaf_sems, blk_sems):
        size = local.shape[0] // N_LEAF
        self.blk = blk
        self.local, self.near, self.far, self.total = local, near, far, total
        mine = pl.ds(pl.multiple_of(leaf * size, 8), size)
        self.mine = mine
        self.spread, self.cross, self.collect = [], [], []
        for k in range(1, N_LEAF):
            peer = lax.rem(leaf + k, N_LEAF)
            self.spread.append(pltpu.make_async_remote_copy(
                src_ref=local.at[pl.ds(pl.multiple_of(peer * size, 8), size)], dst_ref=near.at[k],
                send_sem=leaf_sems.at[0, k], recv_sem=leaf_sems.at[1, k], device_id={"leaf": peer}, device_id_type=MESH))
            self.collect.append(pltpu.make_async_remote_copy(
                src_ref=total.at[mine], dst_ref=total.at[mine],
                send_sem=leaf_sems.at[2, k], recv_sem=leaf_sems.at[3, k], device_id={"leaf": peer}, device_id_type=MESH))
        for k in range(1, N_BLK):
            peer = lax.rem(blk + k, N_BLK)
            self.cross.append(pltpu.make_async_remote_copy(
                src_ref=far.at[blk], dst_ref=far.at[blk],
                send_sem=blk_sems.at[0, k], recv_sem=blk_sems.at[1, k], device_id={"blk": peer}, device_id_type=MESH))

    def begin(self, *parts):
        for n, part in enumerate(parts):
            self.local[128 * n : 128 * (n + 1), :] = part
        for copy in self.spread:
            copy.start()

    def across(self):
        part = self.local[self.mine, :]
        for k, copy in enumerate(self.spread):
            copy.wait_recv()
            part = part + self.near[k + 1]
        self.far[self.blk] = part
        for copy in self.cross:
            copy.start()

    def gather(self):
        for copy in self.cross:
            copy.wait_recv()
        part = self.far[0]
        for b in range(1, N_BLK):
            part = part + self.far[b]
        self.total[self.mine, :] = part
        for copy in self.collect:
            copy.start()

    def end(self):
        for copy in self.collect:
            copy.wait_recv()

    def drain(self):
        for copy in self.spread + self.cross + self.collect:
            copy.wait_send()


def sum_scratch(parts):
    size = 128 * parts // N_LEAF
    return [
        pltpu.VMEM((128 * parts, 128), F32),
        pltpu.VMEM((N_LEAF, size, 128), F32),
        pltpu.VMEM((N_BLK, size, 128), F32),
        pltpu.VMEM((128 * parts, 128), F32),
        pltpu.SemaphoreType.DMA((4, N_LEAF)),
        pltpu.SemaphoreType.DMA((2, N_BLK)),
    ]


SIDE = 128
BLOCK = 64


def factor_start(work, gram):
    work[:, 0:SIDE] = gram
    work[:, SIDE:] = (
        lax.broadcasted_iota(jnp.int32, (SIDE, SIDE), 0) == lax.broadcasted_iota(jnp.int32, (SIDE, SIDE), 1)
    ).astype(F32)


def factor(work, start):
    sub = lax.broadcasted_iota(jnp.int32, (8, 128), 0)
    if start:
        update = dot(work[0:start, start : start + BLOCK], work[0:start, :], 0, 0, HIGH)
        work[start : start + BLOCK, :] = work[start : start + BLOCK, :] - update
    count = BLOCK // 8
    tiles = 2
    x = [[work[start + 8 * t : start + 8 * t + 8, 128 * i : 128 * (i + 1)] for i in range(tiles)] for t in range(count)]
    for p in range(count):
        lane = start + 8 * p
        rest = range(p, count)
        col = [{t: jnp.broadcast_to(x[t][0][:, lane + j : lane + j + 1], (8, 128)) for t in rest} for j in range(8)]
        for j in range(8):
            inverse = lax.rsqrt(jnp.broadcast_to(col[j][p][j : j + 1, :], (8, 128)))
            low = {t: col[j][t] * inverse for t in rest}
            for k in range(j + 1, 8):
                pivot = jnp.broadcast_to(low[p][k : k + 1, :], (8, 128))
                for t in rest:
                    col[k][t] = col[k][t] - low[t] * pivot
            for i in range(tiles):
                row = jnp.broadcast_to(x[p][i][j : j + 1, :], (8, 128)) * inverse
                for t in rest:
                    moved = x[t][i] - low[t] * row
                    if t == p:
                        moved = jnp.where(sub > j, moved, jnp.where(sub == j, row, x[t][i]))
                    x[t][i] = moved
        for i in range(tiles):
            work[start + 8 * p : start + 8 * p + 8, 128 * i : 128 * (i + 1)] = x[p][i]


def factored(work):
    keep = lax.broadcasted_iota(jnp.int32, (SIDE, SIDE), 0) <= lax.broadcasted_iota(jnp.int32, (SIDE, SIDE), 1)
    return jnp.where(keep, work[:, 0:SIDE], 0.0), work[:, SIDE:]


def dot3(a, b, ca, cb):
    (ah, al), (bh, bl) = split2(a), split2(b)
    return dot(ah, bh, ca, cb) + (dot(ah, bl, ca, cb) + dot(al, bh, ca, cb))


TOTAL = N_LEAF * N_BLK
STEPS = (-1, 1)


class Exchange:
    def __init__(self, device, near, far, relay, near_to, far_to, sems):
        self.near_to, self.far_to = near_to, far_to
        self.direct, self.away, self.onward = [], [], []
        self.one, self.two, self.from_one, self.from_two = [], [], [], []
        self.between = (device >= 1) & (device < TOTAL - 1)
        for u, step in enumerate(STEPS):
            peer = lax.rem(device + step + TOTAL, TOTAL)
            there = (lax.div(peer, N_LEAF), lax.rem(peer, N_LEAF))

            def copy(kind, src, dst):
                return pltpu.make_async_remote_copy(
                    src_ref=src, dst_ref=dst, send_sem=sems.at[0, kind, u], recv_sem=sems.at[1, kind, u],
                    device_id=there, device_id_type=MESH)

            self.direct.append(copy(0, near[u], near_to[u]))
            self.away.append(copy(1, far[u], relay.at[u]))
            self.onward.append(copy(2, relay.at[u], far_to[u]))
            self.one.append(self.within(device + step))
            self.two.append(self.within(device + 2 * step))
            self.from_one.append(self.within(device - step))
            self.from_two.append(self.within(device - 2 * step))

    def within(self, device):
        return (device >= 0) & (device < TOTAL)

    def send_far(self):
        for u in range(2):
            pl.when(self.two[u])(self.away[u].start)

    def send_near(self):
        for u in range(2):
            pl.when(self.one[u])(self.direct[u].start)

    def forward(self):
        for u in range(2):
            @pl.when(self.between)
            def _():
                self.away[u].wait_recv()
                self.onward[u].start()

    def receive(self, arrives, copy, to):
        pl.when(arrives)(copy.wait_recv)

        @pl.when(jnp.logical_not(arrives))
        def _():
            to[...] = jnp.zeros(to.shape, F32)

    def receive_near(self):
        for u in range(2):
            self.receive(self.from_one[u], self.direct[u], self.near_to[u])

    def receive_far(self):
        for u in range(2):
            self.receive(self.from_two[u], self.onward[u], self.far_to[u])

    def drain(self):
        for u in range(2):
            pl.when(self.two[u])(self.away[u].wait_send)
            pl.when(self.one[u])(self.direct[u].wait_send)
            pl.when(self.between)(self.onward[u].wait_send)


STORED = (512, 256, 384, 640)
NEAR_OUT, FAR_OUT = (1, 2), (0, 3)
NEAR_BACK, FAR_BACK = (2, 1), (3, 0)


def main_kernel(scale, count, modes, stiffness, connect, send, bottom_out, low_out, rest_out, r_out, top_out, inv_out, q_out,
                outgoing, table, relay, acc, incoming, relay_back, halo_sems, back_sems,
                ext_hi, ext_lo, pick, place, taken, blocks, matrix_hi, matrix_lo, product, stiff, work, *sums):
    leaf, blk = lax.axis_index("leaf"), lax.axis_index("blk")
    device = blk * N_LEAF + leaf
    barrier = greet(leaf, blk)

    def rows_of(ref, h, j):
        return ref.at[h, pl.ds(STORED[j], 128)]

    halo, back = [], []
    for h in range(2):
        halo.append(Exchange(
            device, [outgoing.at[h, j] for j in NEAR_OUT], [outgoing.at[h, j] for j in FAR_OUT], relay.at[h],
            [rows_of(table, h, j) for j in NEAR_OUT], [rows_of(table, h, j) for j in FAR_OUT], halo_sems.at[h]))
        back.append(Exchange(
            device, [rows_of(acc, h, j) for j in NEAR_BACK], [rows_of(acc, h, j) for j in FAR_BACK], relay_back.at[h],
            [incoming.at[h, j] for j in NEAR_BACK], [incoming.at[h, j] for j in FAR_BACK], back_sems.at[h]))
    greeted = N_LEAF + N_BLK - 2
    for u, step in enumerate(STEPS):
        peer = lax.rem(device + step + TOTAL, TOTAL)
        there = (lax.div(peer, N_LEAF), lax.rem(peer, N_LEAF))
        greeted = greeted + halo[0].from_one[u].astype(jnp.int32)

        @pl.when(halo[0].one[u])
        def _():
            pl.semaphore_signal(barrier, inc=1, device_id=there, device_id_type=MESH)

    first, cross, top, bottom = (Sum(leaf, blk, *sums[6 * i : 6 * i + 6]) for i in range(4))

    chosen = send[...]
    columns = columns_of(chosen, 4)
    nodes = lax.broadcasted_iota(jnp.int32, (128, 256), 1).astype(F32)
    choosers = [(columns[:, j : j + 1] == nodes).astype(BF16) for j in range(4)]

    def prepare(h):
        wide = jnp.concatenate([modes[c, :, 128 * h : 128 * (h + 1)] for c in range(3)], axis=1)
        parts = split3(wide)
        for j in FAR_OUT + NEAR_OUT:
            outgoing[h, j] = sum(dot(choosers[j], part, 1, 0) for part in parts)
        table[h, 0:256, :] = wide
        ext_hi[h, 0:256, :], ext_lo[h, 0:256, :] = parts[0], parts[1]

    prepare(0)
    pl.semaphore_wait(barrier, greeted)
    halo[0].send_far()
    halo[0].send_near()
    prepare(1)
    gram = sum(dot3(modes[c].T, modes[c], 1, 0) for c in range(3))
    first.begin(gram[0:128, 0:128], gram[128:256, 0:128], gram[128:256, 128:256])

    conn = connect[...]
    columns = columns_of(conn, 10)

    def table_id(at):
        return jnp.where(at < 256, at, jnp.where(at < 512, at + 128, jnp.where(at < 640, at - 256, at)))

    lanes = table_id(lax.broadcasted_iota(jnp.int32, (128, 768), 1)).astype(F32)
    rows = table_id(lax.broadcasted_iota(jnp.int32, (768, 128), 0))
    for k in range(10):
        pick[128 * k : 128 * (k + 1), :] = (columns[:, k : k + 1] == lanes).astype(BF16)
        place[:, 128 * k : 128 * (k + 1)] = (rows == conn[k : k + 1, :]).astype(BF16)

    halo[0].forward()
    halo[1].send_far()
    halo[1].send_near()

    def gather(h, part):
        span = slice(256 * part, 256 * (part + 1))
        if part:
            ext_hi[h, span, :], ext_lo[h, span, :] = split2(table[h, span, :])

        def body(step, carry):
            at = pl.ds(pl.multiple_of(step * 320, 320), 320)
            picked = pick[at, span]
            found = dot(picked, ext_hi[h, span, :], 1, 0) + dot(picked, ext_lo[h, span, :], 1, 0)
            taken[h, at, :] = found if part == 0 else taken[h, at, :] + found
            return carry

        lax.fori_loop(0, 4, body, 0)

    gather(0, 0)
    gather(1, 0)

    live = lax.broadcasted_iota(jnp.int32, (30, 128), 1) < count[0]
    source = lax.broadcasted_iota(jnp.int32, (30, 256), 0)
    target = lax.broadcasted_iota(jnp.int32, (30, 256), 1)
    wanted = lax.rem(source, 3) * 10 + lax.div(source, 3)
    spread = (lax.shift_right_logical(target, 3) == wanted).astype(BF16)
    for k in range(10):
        for c in range(3):
            block = jnp.concatenate([stiffness[k, c, l] for l in range(10)], axis=0)
            hi, lo = split2(jnp.where(live, block, 0.0))
            blocks[10 * c + k] = dot(hi, spread, 0, 0) + dot(lo, spread, 0, 0)

    keep = lax.broadcasted_iota(jnp.int32, (8, 256), 0) == lax.rem(lax.broadcasted_iota(jnp.int32, (8, 256), 1), 8)

    def assemble(g, carry):
        at = pl.ds(pl.multiple_of(g * 8, 8), 8)
        matrix = jnp.concatenate([jnp.where(keep, blocks[n, at, :], 0.0) for n in range(30)], axis=0)
        matrix_hi[g], matrix_lo[g] = split2(matrix)
        return carry

    lax.fori_loop(0, 16, assemble, 0)

    def multiply(h):
        def group(g, carry):
            spans = [pl.ds(pl.multiple_of(128 * k + g * 8, 8), 8) for k in range(10)]
            vectors = jnp.concatenate(
                [taken[h, spans[l], 128 * d : 128 * (d + 1)] for d in range(3) for l in range(10)]
                + [jnp.zeros((16, 128), F32)],
                axis=0,
            )
            v_hi, v_lo = split2(vectors)
            m_hi, m_lo = matrix_hi[g], matrix_lo[g]
            result = dot(m_hi, v_hi, 1, 0) + (dot(m_hi, v_lo, 1, 0) + dot(m_lo, v_hi, 1, 0))
            for c in range(3):
                for k in range(10):
                    n = 10 * c + k
                    product[spans[k], 128 * c : 128 * (c + 1)] = result[8 * n : 8 * n + 8, :]
            return carry

        lax.fori_loop(0, 16, group, 0, unroll=2)
        return split2(product[...])

    def scatter(h, halves, span):
        where = place[span, :]
        acc[h, span, :] = dot(where, halves[0], 1, 0) + dot(where, halves[1], 1, 0)

    OWN, NEAR, FAR = slice(0, 256), slice(256, 512), slice(512, 768)

    halo[0].receive_near()
    gather(0, 1)
    halo[0].receive_far()
    gather(0, 2)
    halves = multiply(0)
    first.across()
    scatter(0, halves, FAR)
    back[0].send_far()
    halo[1].forward()
    scatter(0, halves, NEAR)
    back[0].send_near()
    scatter(0, halves, OWN)
    halo[1].receive_near()
    gather(1, 1)
    halo[1].receive_far()
    gather(1, 2)
    first.gather()
    halves = multiply(1)
    scatter(1, halves, FAR)
    back[1].send_far()
    back[0].forward()
    scatter(1, halves, NEAR)
    back[1].send_near()
    scatter(1, halves, OWN)

    lower, diagonal = [], 0.0
    for c in range(3):
        at = slice(128 * c, 128 * (c + 1))
        tables = [jnp.concatenate([ext[0, :, at], ext[1, :, at]], axis=1) for ext in (ext_hi, ext_lo)]
        for h in range(2):
            hi, lo = split2(acc[h, :, at].T)
            t_hi, t_lo = (t if h else t[:, 0:128] for t in tables)
            found = dot(hi, t_hi, 1, 0) + (dot(hi, t_lo, 1, 0) + dot(lo, t_hi, 1, 0))
            if h:
                lower.append(found)
            else:
                diagonal = diagonal + found
    lower = sum(lower)
    cross.begin(diagonal, lower[:, 0:128], lower[:, 128:256])

    rows = lax.broadcasted_iota(jnp.int32, (256, 128), 0)
    to_own = jnp.concatenate([(rows == chosen[j : j + 1, :]).astype(BF16) for j in range(4)], axis=1)

    def complete(h):
        back[h].receive_near()
        back[h].receive_far()
        parts = split2(jnp.concatenate([incoming[h, j] for j in range(4)], axis=0))
        whole = acc[h, OWN, :] + sum(dot(to_own, part, 1, 0) for part in parts)
        for c in range(3):
            stiff[c, :, 128 * h : 128 * (h + 1)] = whole[:, 128 * c : 128 * (c + 1)]

    first.end()
    factor_start(work, first.total[0:128, :])
    factor(work, 0)
    back[1].forward()
    factor(work, 64)
    r00, i00 = factored(work)
    complete(0)
    top.begin(sum(dot3(stiff[c, :, 0:128].T, stiff[c, :, 0:128], 1, 0) for c in range(3)))
    r01 = dot(i00, first.total[128:256, :], 1, 1, HIGH)
    factor_start(work, first.total[256:384, :] - dot(r01, r01, 0, 0, HIGH))
    factor(work, 0)
    factor(work, 64)
    r11, i11 = factored(work)
    r_out[0:128, 0:128], r_out[0:128, 128:256] = r00, r01
    r_out[128:256, 0:128], r_out[128:256, 128:256] = jnp.zeros((SIDE, SIDE), F32), r11
    i10 = dot(i11, dot(r01, i00, 0, 0, HIGH), 1, 0, HIGH)
    inv = jnp.concatenate(
        [jnp.concatenate([i00, jnp.zeros((SIDE, SIDE), F32)], axis=1), jnp.concatenate([-i10, i11], axis=1)], axis=0)
    cross.across()
    for c in range(3):
        q_out[c, :, 0:256] = dot3(modes[c], inv, 1, 1) * scale

    complete(1)
    both = sum(dot3(stiff[c, :, 128:256].T, stiff[c], 1, 0) for c in range(3))
    bottom.begin(both[:, 0:128], both[:, 128:256])
    cross.gather()
    top.across()
    top.gather()
    cross.end()
    crossed = cross.total
    gram = jnp.concatenate(
        [jnp.concatenate([crossed[0:128, :], crossed[128:256, :].T], axis=1),
         jnp.concatenate([crossed[128:256, :], crossed[256:384, :]], axis=1)], axis=0)
    low = dot(gram, inv, 1, 1, HIGH)
    low_out[...] = low
    top.end()
    factor_start(work, top.total[...] - dot(low[0:128, :], low[0:128, :], 1, 1, HIGH))
    factor(work, 0)
    bottom.across()
    factor(work, 64)
    bottom.gather()
    r22, i22 = factored(work)
    top_out[...] = r22
    inv_out[...] = i22
    for c in range(3):
        rest = stiff[c] - dot3(q_out[c, :, 0:256], low / scale, 1, 1)
        q_out[c, :, 256:384] = dot3(rest[:, 0:128], i22, 1, 1) * scale
        rest_out[c] = rest[:, 128:256]
    for h in range(2):
        halo[h].drain()
        back[h].drain()
    first.drain()
    cross.drain()
    top.drain()
    bottom.end()
    bottom.drain()
    bottom_out[...] = bottom.total[...]


def up_to_last_gram(scale, count, modes, stiffness, connect, send):
    shapes = ((256, 128), (256, 256), (3, 256, 128), (256, 256), (128, 128), (128, 128), (3, 256, 384))
    rows = pltpu.VMEM((2, 4, 128, 384), F32)
    table = pltpu.VMEM((2, 768, 384), F32)
    relay = pltpu.VMEM((2, 2, 128, 384), F32)
    sems = pltpu.SemaphoreType.DMA((2, 2, 3, 2))
    return pl.pallas_call(
        functools.partial(main_kernel, scale),
        out_shape=[jax.ShapeDtypeStruct(shape, F32) for shape in shapes],
        in_specs=[SMEM] + [VMEM] * 4,
        out_specs=[VMEM] * len(shapes),
        scratch_shapes=[
            rows, table, relay, table, rows, relay, sems, sems,
            pltpu.VMEM((2, 768, 384), BF16),
            pltpu.VMEM((2, 768, 384), BF16),
            pltpu.VMEM((1280, 768), BF16),
            pltpu.VMEM((768, 1280), BF16),
            pltpu.VMEM((2, 1280, 384), F32),
            pltpu.VMEM((30, 128, 256), F32),
            pltpu.VMEM((16, 240, 256), BF16),
            pltpu.VMEM((16, 240, 256), BF16),
            pltpu.VMEM((1280, 384), F32),
            pltpu.VMEM((3, 256, 256), F32),
            pltpu.VMEM((SIDE, 2 * SIDE), F32),
        ] + sum_scratch(3) + sum_scratch(3) + sum_scratch(1) + sum_scratch(2),
        compiler_params=pltpu.CompilerParams(collective_id=1, has_side_effects=True, vmem_limit_bytes=LIMIT),
        name="up_to_last_gram",
    )(count, modes, stiffness, connect, send)


def second_kernel(scale, bottom, low, r_first, r_top, i_top, rest, q_in, q_out, r_out, work, top_columns, last, sems):
    done = pltpu.make_async_copy(q_in, q_out.at[:, :, pl.ds(0, 384)], sems.at[0])
    fetch = pltpu.make_async_copy(q_in.at[:, :, pl.ds(256, 128)], top_columns, sems.at[1])
    done.start()
    fetch.start()
    low0, low1 = low[0:128, :], low[128:256, :]
    side = bottom[0:128, :] - dot(low1, low0, 1, 1, HIGH)
    r01 = dot(i_top[...], side, 1, 1, HIGH)
    factor_start(work, bottom[128:256, :] - dot(low1, low1, 1, 1, HIGH) - dot(r01, r01, 0, 0, HIGH))
    factor(work, 0)
    r_out[0:256, 0:256] = r_first[...] / scale
    r_out[0:256, 256:512] = low[...].T / scale
    r_out[256:512, 0:256] = jnp.zeros((256, 256), F32)
    r_out[256:384, 256:384] = r_top[...] / scale
    r_out[256:384, 384:512] = r01 / scale
    r_out[384:512, 256:384] = jnp.zeros((128, 128), F32)
    factor(work, 64)
    r11, i11 = factored(work)
    r_out[384:512, 384:512] = r11 / scale
    fetch.wait()
    for c in range(3):
        left = rest[c] - dot3(top_columns[c], r01 / scale, 1, 0)
        last[c] = dot3(left, i11, 1, 1) * scale
    place = pltpu.make_async_copy(last, q_out.at[:, :, pl.ds(384, 128)], sems.at[2])
    place.start()
    place.wait()
    done.wait()


def second(scale, *operands):
    anywhere = pl.BlockSpec(memory_space=pl.ANY)
    return pl.pallas_call(
        functools.partial(second_kernel, scale),
        out_shape=[jax.ShapeDtypeStruct((3, 256, 512), F32), jax.ShapeDtypeStruct((512, 512), F32)],
        in_specs=[VMEM] * 6 + [anywhere],
        out_specs=[anywhere, VMEM],
        scratch_shapes=[
            pltpu.VMEM((SIDE, 2 * SIDE), F32),
            pltpu.VMEM((3, 256, 128), F32),
            pltpu.VMEM((3, 256, 128), F32),
            pltpu.SemaphoreType.DMA((3,)),
        ],
        compiler_params=pltpu.CompilerParams(vmem_limit_bytes=LIMIT),
        name="second_factor",
    )(*operands)


def shards(modes, stiffness, connect, send_list, elem_count):
    modes = jnp.transpose(modes, (1, 0, 2))
    scale = float((3 * 256 * lax.axis_size("blk") * lax.axis_size("leaf")) ** 0.5)
    bottom, low, rest, r_first, r_top, i_top, q = up_to_last_gram(
        scale, elem_count, modes, stiffness, connect, send_list[0])
    q, r = second(scale, bottom, low, r_first, r_top, i_top, rest, q)
    return (jnp.transpose(q, (1, 0, 2)), r)


def solution(mesh):
    placed = (
        P(("blk", "leaf"), None, None),
        P(None, None, None, None, ("blk", "leaf")),
        P(None, ("blk", "leaf")),
        P(("blk", "leaf"), None, None),
        P(("blk", "leaf")),
    )
    return jax.shard_map(
        shards,
        mesh=mesh,
        in_specs=placed,
        out_specs=(P(("blk", "leaf"), None, None), P()),
        check_vma=False,
    )
```

```python
import functools

import jax
import jax.numpy as jnp
from jax import lax
from jax.experimental import pallas as pl
from jax.experimental.pallas import tpu as pltpu
from jax.sharding import PartitionSpec as P

HIGH = lax.Precision.HIGHEST
F32 = jnp.float32
BF16 = jnp.bfloat16
MESH = pl.DeviceIdType.MESH
VMEM = pl.BlockSpec(memory_space=pltpu.VMEM)
SMEM = pl.BlockSpec(memory_space=pltpu.SMEM)
LIMIT = 56 * 1024 * 1024


def dot(a, b, ca, cb, precision=None):
    return lax.dot_general(a, b, (((ca,), (cb,)), ((), ())), precision=precision, preferred_element_type=F32)


def split2(x):
    hi = x.astype(BF16)
    return hi, (x - hi.astype(F32)).astype(BF16)


def split3(x):
    hi = x.astype(BF16)
    rest = x - hi.astype(F32)
    mid = rest.astype(BF16)
    return hi, mid, (rest - mid.astype(F32)).astype(BF16)


def columns_of(rows, count):
    padded = jnp.concatenate([rows.astype(F32), jnp.zeros((16 - count, 128), F32)], axis=0)
    return padded.T


N_LEAF = 16
N_BLK = 8


def greet(leaf, blk):
    barrier = pltpu.get_barrier_semaphore()
    for k in range(1, N_LEAF):
        pl.semaphore_signal(barrier, inc=1, device_id={"leaf": lax.rem(leaf + k, N_LEAF)}, device_id_type=MESH)
    for k in range(1, N_BLK):
        pl.semaphore_signal(barrier, inc=1, device_id={"blk": lax.rem(blk + k, N_BLK)}, device_id_type=MESH)
    return barrier


class Sum:
    def __init__(self, leaf, blk, local, near, far, total, leaf_sems, blk_sems):
        size = local.shape[0] // N_LEAF
        self.blk = blk
        self.local, self.near, self.far, self.total = local, near, far, total
        mine = pl.ds(pl.multiple_of(leaf * size, 8), size)
        self.mine = mine
        self.spread, self.cross, self.collect = [], [], []
        for k in range(1, N_LEAF):
            peer = lax.rem(leaf + k, N_LEAF)
            self.spread.append(pltpu.make_async_remote_copy(
                src_ref=local.at[pl.ds(pl.multiple_of(peer * size, 8), size)], dst_ref=near.at[k],
                send_sem=leaf_sems.at[0, k], recv_sem=leaf_sems.at[1, k], device_id={"leaf": peer}, device_id_type=MESH))
            self.collect.append(pltpu.make_async_remote_copy(
                src_ref=total.at[mine], dst_ref=total.at[mine],
                send_sem=leaf_sems.at[2, k], recv_sem=leaf_sems.at[3, k], device_id={"leaf": peer}, device_id_type=MESH))
        for k in range(1, N_BLK):
            peer = lax.rem(blk + k, N_BLK)
            self.cross.append(pltpu.make_async_remote_copy(
                src_ref=far.at[blk], dst_ref=far.at[blk],
                send_sem=blk_sems.at[0, k], recv_sem=blk_sems.at[1, k], device_id={"blk": peer}, device_id_type=MESH))

    def begin(self, *parts):
        for n, part in enumerate(parts):
            self.local[128 * n : 128 * (n + 1), :] = part
        for copy in self.spread:
            copy.start()

    def across(self):
        part = self.local[self.mine, :]
        for k, copy in enumerate(self.spread):
            copy.wait_recv()
            part = part + self.near[k + 1]
        self.far[self.blk] = part
        for copy in self.cross:
            copy.start()

    def gather(self):
        for copy in self.cross:
            copy.wait_recv()
        part = self.far[0]
        for b in range(1, N_BLK):
            part = part + self.far[b]
        self.total[self.mine, :] = part
        for copy in self.collect:
            copy.start()

    def end(self):
        for copy in self.collect:
            copy.wait_recv()

    def drain(self):
        for copy in self.spread + self.cross + self.collect:
            copy.wait_send()


def sum_scratch(parts):
    size = 128 * parts // N_LEAF
    return [
        pltpu.VMEM((128 * parts, 128), F32),
        pltpu.VMEM((N_LEAF, size, 128), F32),
        pltpu.VMEM((N_BLK, size, 128), F32),
        pltpu.VMEM((128 * parts, 128), F32),
        pltpu.SemaphoreType.DMA((4, N_LEAF)),
        pltpu.SemaphoreType.DMA((2, N_BLK)),
    ]


SIDE = 128
BLOCK = 64


def factor_start(work, gram):
    work[:, 0:SIDE] = gram
    work[:, SIDE:] = (
        lax.broadcasted_iota(jnp.int32, (SIDE, SIDE), 0) == lax.broadcasted_iota(jnp.int32, (SIDE, SIDE), 1)
    ).astype(F32)


def factor(work, start):
    sub = lax.broadcasted_iota(jnp.int32, (8, 128), 0)
    if start:
        update = dot(work[0:start, start : start + BLOCK], work[0:start, :], 0, 0, HIGH)
        work[start : start + BLOCK, :] = work[start : start + BLOCK, :] - update
    count = BLOCK // 8
    tiles = 2
    x = [[work[start + 8 * t : start + 8 * t + 8, 128 * i : 128 * (i + 1)] for i in range(tiles)] for t in range(count)]
    for p in range(count):
        lane = start + 8 * p
        rest = range(p, count)
        col = [{t: jnp.broadcast_to(x[t][0][:, lane + j : lane + j + 1], (8, 128)) for t in rest} for j in range(8)]
        for j in range(8):
            inverse = lax.rsqrt(jnp.broadcast_to(col[j][p][j : j + 1, :], (8, 128)))
            low = {t: col[j][t] * inverse for t in rest}
            for k in range(j + 1, 8):
                pivot = jnp.broadcast_to(low[p][k : k + 1, :], (8, 128))
                for t in rest:
                    col[k][t] = col[k][t] - low[t] * pivot
            for i in range(tiles):
                row = jnp.broadcast_to(x[p][i][j : j + 1, :], (8, 128)) * inverse
                for t in rest:
                    moved = x[t][i] - low[t] * row
                    if t == p:
                        moved = jnp.where(sub > j, moved, jnp.where(sub == j, row, x[t][i]))
                    x[t][i] = moved
        for i in range(tiles):
            work[start + 8 * p : start + 8 * p + 8, 128 * i : 128 * (i + 1)] = x[p][i]


def factored(work):
    keep = lax.broadcasted_iota(jnp.int32, (SIDE, SIDE), 0) <= lax.broadcasted_iota(jnp.int32, (SIDE, SIDE), 1)
    return jnp.where(keep, work[:, 0:SIDE], 0.0), work[:, SIDE:]


def dot3(a, b, ca, cb):
    (ah, al), (bh, bl) = split2(a), split2(b)
    return dot(ah, bh, ca, cb) + (dot(ah, bl, ca, cb) + dot(al, bh, ca, cb))


TOTAL = N_LEAF * N_BLK
STEPS = (-1, 1)
ONE, TWO = 0, 1


class Exchange:
    def __init__(self, device, near, far, near_to, far_to, sems):
        self.to = (near_to, far_to)
        self.copies, self.sends, self.arrives, self.peers = ([], []), ([], []), ([], []), []
        for kind, (src, dst) in enumerate(((near, near_to), (far, far_to))):
            for u, step in enumerate(STEPS):
                step = step * (kind + 1)
                peer = lax.rem(device + step + TOTAL, TOTAL)
                there = (lax.div(peer, N_LEAF), lax.rem(peer, N_LEAF))
                self.copies[kind].append(pltpu.make_async_remote_copy(
                    src_ref=src[u], dst_ref=dst[u], send_sem=sems.at[0, kind, u], recv_sem=sems.at[1, kind, u],
                    device_id=there, device_id_type=MESH))
                self.sends[kind].append(self.within(device + step))
                self.arrives[kind].append(self.within(device - step))
                self.peers.append((self.sends[kind][u], self.arrives[kind][u], there))

    def within(self, device):
        return (device >= 0) & (device < TOTAL)

    def send(self, kind):
        for u in range(2):
            pl.when(self.sends[kind][u])(self.copies[kind][u].start)

    def receive(self, kind):
        for u in range(2):
            to = self.to[kind][u]
            pl.when(self.arrives[kind][u])(self.copies[kind][u].wait_recv)

            @pl.when(jnp.logical_not(self.arrives[kind][u]))
            def _():
                to[...] = jnp.zeros(to.shape, F32)

    def drain(self):
        for kind in range(2):
            for u in range(2):
                pl.when(self.sends[kind][u])(self.copies[kind][u].wait_send)


STORED = (512, 256, 384, 640)
NEAR_OUT, FAR_OUT = (1, 2), (0, 3)
NEAR_BACK, FAR_BACK = (2, 1), (3, 0)


def main_kernel(scale, count, modes, stiffness, connect, send, bottom_out, low_out, rest_out, r_out, top_out, inv_out, q_out,
                outgoing, table, acc, incoming, halo_sems, back_sems,
                ext_hi, ext_lo, pick, place, taken, blocks, matrix_hi, matrix_lo, product, stiff, work, *sums):
    leaf, blk = lax.axis_index("leaf"), lax.axis_index("blk")
    device = blk * N_LEAF + leaf
    barrier = greet(leaf, blk)

    def rows_of(ref, h, j):
        return ref.at[h, pl.ds(STORED[j], 128)]

    halo, back = [], []
    for h in range(2):
        halo.append(Exchange(
            device, [outgoing.at[h, j] for j in NEAR_OUT], [outgoing.at[h, j] for j in FAR_OUT],
            [rows_of(table, h, j) for j in NEAR_OUT], [rows_of(table, h, j) for j in FAR_OUT], halo_sems.at[h]))
        back.append(Exchange(
            device, [rows_of(acc, h, j) for j in NEAR_BACK], [rows_of(acc, h, j) for j in FAR_BACK],
            [incoming.at[h, j] for j in NEAR_BACK], [incoming.at[h, j] for j in FAR_BACK], back_sems.at[h]))
    greeted = N_LEAF + N_BLK - 2
    for sends, arrives, there in halo[0].peers:
        greeted = greeted + arrives.astype(jnp.int32)

        @pl.when(sends)
        def _():
            pl.semaphore_signal(barrier, inc=1, device_id=there, device_id_type=MESH)

    first, cross, top, bottom = (Sum(leaf, blk, *sums[6 * i : 6 * i + 6]) for i in range(4))

    chosen = send[...]
    columns = columns_of(chosen, 4)
    nodes = lax.broadcasted_iota(jnp.int32, (128, 256), 1).astype(F32)
    choosers = [(columns[:, j : j + 1] == nodes).astype(BF16) for j in range(4)]

    def prepare(h):
        wide = jnp.concatenate([modes[c, :, 128 * h : 128 * (h + 1)] for c in range(3)], axis=1)
        parts = split3(wide)
        for j in FAR_OUT + NEAR_OUT:
            outgoing[h, j] = sum(dot(choosers[j], part, 1, 0) for part in parts)
        table[h, 0:256, :] = wide
        ext_hi[h, 0:256, :], ext_lo[h, 0:256, :] = parts[0], parts[1]

    prepare(0)
    pl.semaphore_wait(barrier, greeted)
    halo[0].send(TWO)
    halo[0].send(ONE)
    prepare(1)
    gram = sum(dot3(modes[c].T, modes[c], 1, 0) for c in range(3))
    first.begin(gram[0:128, 0:128], gram[128:256, 0:128], gram[128:256, 128:256])

    conn = connect[...]
    columns = columns_of(conn, 10)

    def table_id(at):
        return jnp.where(at < 256, at, jnp.where(at < 512, at + 128, jnp.where(at < 640, at - 256, at)))

    lanes = table_id(lax.broadcasted_iota(jnp.int32, (128, 768), 1)).astype(F32)
    rows = table_id(lax.broadcasted_iota(jnp.int32, (768, 128), 0))
    for k in range(10):
        pick[128 * k : 128 * (k + 1), :] = (columns[:, k : k + 1] == lanes).astype(BF16)
        place[:, 128 * k : 128 * (k + 1)] = (rows == conn[k : k + 1, :]).astype(BF16)

    halo[1].send(TWO)
    halo[1].send(ONE)

    def gather(h, part):
        span = slice(256 * part, 256 * (part + 1))
        if part:
            ext_hi[h, span, :], ext_lo[h, span, :] = split2(table[h, span, :])

        def body(step, carry):
            at = pl.ds(pl.multiple_of(step * 320, 320), 320)
            picked = pick[at, span]
            found = dot(picked, ext_hi[h, span, :], 1, 0) + dot(picked, ext_lo[h, span, :], 1, 0)
            taken[h, at, :] = found if part == 0 else taken[h, at, :] + found
            return carry

        lax.fori_loop(0, 4, body, 0)

    gather(0, 0)
    gather(1, 0)

    live = lax.broadcasted_iota(jnp.int32, (30, 128), 1) < count[0]
    source = lax.broadcasted_iota(jnp.int32, (30, 256), 0)
    target = lax.broadcasted_iota(jnp.int32, (30, 256), 1)
    wanted = lax.rem(source, 3) * 10 + lax.div(source, 3)
    spread = (lax.shift_right_logical(target, 3) == wanted).astype(BF16)
    for k in range(10):
        for c in range(3):
            block = jnp.concatenate([stiffness[k, c, l] for l in range(10)], axis=0)
            hi, lo = split2(jnp.where(live, block, 0.0))
            blocks[10 * c + k] = dot(hi, spread, 0, 0) + dot(lo, spread, 0, 0)

    keep = lax.broadcasted_iota(jnp.int32, (8, 256), 0) == lax.rem(lax.broadcasted_iota(jnp.int32, (8, 256), 1), 8)

    def assemble(g, carry):
        at = pl.ds(pl.multiple_of(g * 8, 8), 8)
        matrix = jnp.concatenate([jnp.where(keep, blocks[n, at, :], 0.0) for n in range(30)], axis=0)
        matrix_hi[g], matrix_lo[g] = split2(matrix)
        return carry

    lax.fori_loop(0, 16, assemble, 0)

    def multiply(h):
        def group(g, carry):
            spans = [pl.ds(pl.multiple_of(128 * k + g * 8, 8), 8) for k in range(10)]
            vectors = jnp.concatenate(
                [taken[h, spans[l], 128 * d : 128 * (d + 1)] for d in range(3) for l in range(10)]
                + [jnp.zeros((16, 128), F32)],
                axis=0,
            )
            v_hi, v_lo = split2(vectors)
            m_hi, m_lo = matrix_hi[g], matrix_lo[g]
            result = dot(m_hi, v_hi, 1, 0) + (dot(m_hi, v_lo, 1, 0) + dot(m_lo, v_hi, 1, 0))
            for c in range(3):
                for k in range(10):
                    n = 10 * c + k
                    product[spans[k], 128 * c : 128 * (c + 1)] = result[8 * n : 8 * n + 8, :]
            return carry

        lax.fori_loop(0, 16, group, 0, unroll=2)
        return split2(product[...])

    def scatter(h, halves, span):
        where = place[span, :]
        acc[h, span, :] = dot(where, halves[0], 1, 0) + dot(where, halves[1], 1, 0)

    OWN, NEAR, FAR = slice(0, 256), slice(256, 512), slice(512, 768)

    halo[0].receive(ONE)
    gather(0, 1)
    halo[0].receive(TWO)
    gather(0, 2)
    halves = multiply(0)
    first.across()
    scatter(0, halves, FAR)
    back[0].send(TWO)
    scatter(0, halves, NEAR)
    back[0].send(ONE)
    scatter(0, halves, OWN)
    halo[1].receive(ONE)
    gather(1, 1)
    halo[1].receive(TWO)
    gather(1, 2)
    first.gather()
    halves = multiply(1)
    scatter(1, halves, FAR)
    back[1].send(TWO)
    scatter(1, halves, NEAR)
    back[1].send(ONE)
    scatter(1, halves, OWN)

    lower, diagonal = [], 0.0
    for c in range(3):
        at = slice(128 * c, 128 * (c + 1))
        tables = [jnp.concatenate([ext[0, :, at], ext[1, :, at]], axis=1) for ext in (ext_hi, ext_lo)]
        for h in range(2):
            hi, lo = split2(acc[h, :, at].T)
            t_hi, t_lo = (t if h else t[:, 0:128] for t in tables)
            found = dot(hi, t_hi, 1, 0) + (dot(hi, t_lo, 1, 0) + dot(lo, t_hi, 1, 0))
            if h:
                lower.append(found)
            else:
                diagonal = diagonal + found
    lower = sum(lower)
    cross.begin(diagonal, lower[:, 0:128], lower[:, 128:256])

    rows = lax.broadcasted_iota(jnp.int32, (256, 128), 0)
    to_own = jnp.concatenate([(rows == chosen[j : j + 1, :]).astype(BF16) for j in range(4)], axis=1)

    def complete(h):
        back[h].receive(ONE)
        back[h].receive(TWO)
        parts = split2(jnp.concatenate([incoming[h, j] for j in range(4)], axis=0))
        whole = acc[h, OWN, :] + sum(dot(to_own, part, 1, 0) for part in parts)
        for c in range(3):
            stiff[c, :, 128 * h : 128 * (h + 1)] = whole[:, 128 * c : 128 * (c + 1)]

    first.end()
    factor_start(work, first.total[0:128, :])
    factor(work, 0)
    factor(work, 64)
    r00, i00 = factored(work)
    complete(0)
    top.begin(sum(dot3(stiff[c, :, 0:128].T, stiff[c, :, 0:128], 1, 0) for c in range(3)))
    r01 = dot(i00, first.total[128:256, :], 1, 1, HIGH)
    factor_start(work, first.total[256:384, :] - dot(r01, r01, 0, 0, HIGH))
    factor(work, 0)
    factor(work, 64)
    r11, i11 = factored(work)
    r_out[0:128, 0:128], r_out[0:128, 128:256] = r00, r01
    r_out[128:256, 0:128], r_out[128:256, 128:256] = jnp.zeros((SIDE, SIDE), F32), r11
    i10 = dot(i11, dot(r01, i00, 0, 0, HIGH), 1, 0, HIGH)
    inv = jnp.concatenate(
        [jnp.concatenate([i00, jnp.zeros((SIDE, SIDE), F32)], axis=1), jnp.concatenate([-i10, i11], axis=1)], axis=0)
    cross.across()
    for c in range(3):
        q_out[c, :, 0:256] = dot3(modes[c], inv, 1, 1) * scale

    complete(1)
    both = sum(dot3(stiff[c, :, 128:256].T, stiff[c], 1, 0) for c in range(3))
    bottom.begin(both[:, 0:128], both[:, 128:256])
    cross.gather()
    top.across()
    top.gather()
    cross.end()
    crossed = cross.total
    gram = jnp.concatenate(
        [jnp.concatenate([crossed[0:128, :], crossed[128:256, :].T], axis=1),
         jnp.concatenate([crossed[128:256, :], crossed[256:384, :]], axis=1)], axis=0)
    low = dot(gram, inv, 1, 1, HIGH)
    low_out[...] = low
    top.end()
    factor_start(work, top.total[...] - dot(low[0:128, :], low[0:128, :], 1, 1, HIGH))
    factor(work, 0)
    bottom.across()
    factor(work, 64)
    bottom.gather()
    r22, i22 = factored(work)
    top_out[...] = r22
    inv_out[...] = i22
    for c in range(3):
        rest = stiff[c] - dot3(q_out[c, :, 0:256], low / scale, 1, 1)
        q_out[c, :, 256:384] = dot3(rest[:, 0:128], i22, 1, 1) * scale
        rest_out[c] = rest[:, 128:256]
    for h in range(2):
        halo[h].drain()
        back[h].drain()
    first.drain()
    cross.drain()
    top.drain()
    bottom.end()
    bottom.drain()
    bottom_out[...] = bottom.total[...]


def up_to_last_gram(scale, count, modes, stiffness, connect, send):
    shapes = ((256, 128), (256, 256), (3, 256, 128), (256, 256), (128, 128), (128, 128), (3, 256, 384))
    rows = pltpu.VMEM((2, 4, 128, 384), F32)
    table = pltpu.VMEM((2, 768, 384), F32)
    sems = pltpu.SemaphoreType.DMA((2, 2, 2, 2))
    return pl.pallas_call(
        functools.partial(main_kernel, scale),
        out_shape=[jax.ShapeDtypeStruct(shape, F32) for shape in shapes],
        in_specs=[SMEM] + [VMEM] * 4,
        out_specs=[VMEM] * len(shapes),
        scratch_shapes=[
            rows, table, table, rows, sems, sems,
            pltpu.VMEM((2, 768, 384), BF16),
            pltpu.VMEM((2, 768, 384), BF16),
            pltpu.VMEM((1280, 768), BF16),
            pltpu.VMEM((768, 1280), BF16),
            pltpu.VMEM((2, 1280, 384), F32),
            pltpu.VMEM((30, 128, 256), F32),
            pltpu.VMEM((16, 240, 256), BF16),
            pltpu.VMEM((16, 240, 256), BF16),
            pltpu.VMEM((1280, 384), F32),
            pltpu.VMEM((3, 256, 256), F32),
            pltpu.VMEM((SIDE, 2 * SIDE), F32),
        ] + sum_scratch(3) + sum_scratch(3) + sum_scratch(1) + sum_scratch(2),
        compiler_params=pltpu.CompilerParams(collective_id=1, has_side_effects=True, vmem_limit_bytes=LIMIT),
        name="up_to_last_gram",
    )(count, modes, stiffness, connect, send)


def second_kernel(scale, bottom, low, r_first, r_top, i_top, rest, q_in, q_out, r_out, work, columns, last, sems):
    fetch = pltpu.make_async_copy(q_in, columns, sems.at[0])
    done = pltpu.make_async_copy(columns, q_out.at[:, :, pl.ds(0, 384)], sems.at[1])
    fetch.start()
    low0, low1 = low[0:128, :], low[128:256, :]
    side = bottom[0:128, :] - dot(low1, low0, 1, 1, HIGH)
    r01 = dot(i_top[...], side, 1, 1, HIGH)
    factor_start(work, bottom[128:256, :] - dot(low1, low1, 1, 1, HIGH) - dot(r01, r01, 0, 0, HIGH))
    factor(work, 0)
    fetch.wait()
    done.start()
    r_out[0:256, 0:256] = r_first[...] / scale
    r_out[0:256, 256:512] = low[...].T / scale
    r_out[256:512, 0:256] = jnp.zeros((256, 256), F32)
    r_out[256:384, 256:384] = r_top[...] / scale
    r_out[256:384, 384:512] = r01 / scale
    r_out[384:512, 256:384] = jnp.zeros((128, 128), F32)
    factor(work, 64)
    r11, i11 = factored(work)
    r_out[384:512, 384:512] = r11 / scale
    for c in range(3):
        left = rest[c] - dot3(columns[c, :, 256:384], r01 / scale, 1, 0)
        last[c] = dot3(left, i11, 1, 1) * scale
    place = pltpu.make_async_copy(last, q_out.at[:, :, pl.ds(384, 128)], sems.at[2])
    place.start()
    place.wait()
    done.wait()


def second(scale, *operands):
    anywhere = pl.BlockSpec(memory_space=pl.ANY)
    return pl.pallas_call(
        functools.partial(second_kernel, scale),
        out_shape=[jax.ShapeDtypeStruct((3, 256, 512), F32), jax.ShapeDtypeStruct((512, 512), F32)],
        in_specs=[VMEM] * 6 + [anywhere],
        out_specs=[anywhere, VMEM],
        scratch_shapes=[
            pltpu.VMEM((SIDE, 2 * SIDE), F32),
            pltpu.VMEM((3, 256, 384), F32),
            pltpu.VMEM((3, 256, 128), F32),
            pltpu.SemaphoreType.DMA((3,)),
        ],
        compiler_params=pltpu.CompilerParams(vmem_limit_bytes=LIMIT),
        name="second_factor",
    )(*operands)


def shards(modes, stiffness, connect, send_list, elem_count):
    modes = jnp.transpose(modes, (1, 0, 2))
    scale = float((3 * 256 * lax.axis_size("blk") * lax.axis_size("leaf")) ** 0.5)
    bottom, low, rest, r_first, r_top, i_top, q = up_to_last_gram(
        scale, elem_count, modes, stiffness, connect, send_list[0])
    q, r = second(scale, bottom, low, r_first, r_top, i_top, rest, q)
    return (jnp.transpose(q, (1, 0, 2)), r)


def solution(mesh):
    placed = (
        P(("blk", "leaf"), None, None),
        P(None, None, None, None, ("blk", "leaf")),
        P(None, ("blk", "leaf")),
        P(("blk", "leaf"), None, None),
        P(("blk", "leaf")),
    )
    return jax.shard_map(
        shards,
        mesh=mesh,
        in_specs=placed,
        out_specs=(P(("blk", "leaf"), None, None), P()),
        check_vma=False,
    )
```

```python
import functools

import jax
import jax.numpy as jnp
from jax import lax
from jax.experimental import pallas as pl
from jax.experimental.pallas import tpu as pltpu
from jax.sharding import PartitionSpec as P

HIGH = lax.Precision.HIGHEST
F32 = jnp.float32
BF16 = jnp.bfloat16
MESH = pl.DeviceIdType.MESH
VMEM = pl.BlockSpec(memory_space=pltpu.VMEM)
SMEM = pl.BlockSpec(memory_space=pltpu.SMEM)
LIMIT = 56 * 1024 * 1024


def dot(a, b, ca, cb, precision=None):
    return lax.dot_general(a, b, (((ca,), (cb,)), ((), ())), precision=precision, preferred_element_type=F32)


def split2(x):
    hi = x.astype(BF16)
    return hi, (x - hi.astype(F32)).astype(BF16)


def split3(x):
    hi = x.astype(BF16)
    rest = x - hi.astype(F32)
    mid = rest.astype(BF16)
    return hi, mid, (rest - mid.astype(F32)).astype(BF16)


def columns_of(rows, count):
    padded = jnp.concatenate([rows.astype(F32), jnp.zeros((16 - count, 128), F32)], axis=0)
    return padded.T


N_LEAF = 16
N_BLK = 8


def greet(leaf, blk):
    barrier = pltpu.get_barrier_semaphore()
    for k in range(1, N_LEAF):
        pl.semaphore_signal(barrier, inc=1, device_id={"leaf": lax.rem(leaf + k, N_LEAF)}, device_id_type=MESH)
    for k in range(1, N_BLK):
        pl.semaphore_signal(barrier, inc=1, device_id={"blk": lax.rem(blk + k, N_BLK)}, device_id_type=MESH)
    return barrier


class Sum:
    def __init__(self, leaf, blk, local, near, far, total, leaf_sems, blk_sems):
        size = local.shape[0] // N_LEAF
        self.blk = blk
        self.local, self.near, self.far, self.total = local, near, far, total
        mine = pl.ds(pl.multiple_of(leaf * size, 8), size)
        self.mine = mine
        self.spread, self.cross, self.collect = [], [], []
        for k in range(1, N_LEAF):
            peer = lax.rem(leaf + k, N_LEAF)
            self.spread.append(pltpu.make_async_remote_copy(
                src_ref=local.at[pl.ds(pl.multiple_of(peer * size, 8), size)], dst_ref=near.at[k],
                send_sem=leaf_sems.at[0, k], recv_sem=leaf_sems.at[1, k], device_id={"leaf": peer}, device_id_type=MESH))
            self.collect.append(pltpu.make_async_remote_copy(
                src_ref=total.at[mine], dst_ref=total.at[mine],
                send_sem=leaf_sems.at[2, k], recv_sem=leaf_sems.at[3, k], device_id={"leaf": peer}, device_id_type=MESH))
        for k in range(1, N_BLK):
            peer = lax.rem(blk + k, N_BLK)
            self.cross.append(pltpu.make_async_remote_copy(
                src_ref=far.at[blk], dst_ref=far.at[blk],
                send_sem=blk_sems.at[0, k], recv_sem=blk_sems.at[1, k], device_id={"blk": peer}, device_id_type=MESH))

    def begin(self, *parts):
        for n, part in enumerate(parts):
            self.local[128 * n : 128 * (n + 1), :] = part
        for copy in self.spread:
            copy.start()

    def across(self):
        part = self.local[self.mine, :]
        for k, copy in enumerate(self.spread):
            copy.wait_recv()
            part = part + self.near[k + 1]
        self.far[self.blk] = part
        for copy in self.cross:
            copy.start()

    def gather(self):
        for copy in self.cross:
            copy.wait_recv()
        part = self.far[0]
        for b in range(1, N_BLK):
            part = part + self.far[b]
        self.total[self.mine, :] = part
        for copy in self.collect:
            copy.start()

    def end(self):
        for copy in self.collect:
            copy.wait_recv()

    def drain(self):
        for copy in self.spread + self.cross + self.collect:
            copy.wait_send()


def sum_scratch(parts):
    size = 128 * parts // N_LEAF
    return [
        pltpu.VMEM((128 * parts, 128), F32),
        pltpu.VMEM((N_LEAF, size, 128), F32),
        pltpu.VMEM((N_BLK, size, 128), F32),
        pltpu.VMEM((128 * parts, 128), F32),
        pltpu.SemaphoreType.DMA((4, N_LEAF)),
        pltpu.SemaphoreType.DMA((2, N_BLK)),
    ]


CHUNK = 24


class AxisSum:
    def __init__(self, leaf, blk, local, along_x, part, along_y, far, total, sems, blk_sems):
        self.blk, self.local, self.part, self.total = blk, local, part, total
        self.along_x, self.along_y, self.far = along_x, along_y, far
        x, y = lax.div(leaf, 4), lax.rem(leaf, 4)
        wide, slim = 4 * CHUNK, CHUNK
        self.wide = pl.ds(pl.multiple_of(x * wide, 8), wide)
        self.slim = pl.ds(pl.multiple_of(y * slim, 8), slim)
        self.mine = pl.ds(pl.multiple_of(leaf * slim, 8), slim)
        self.stages = [[], [], [], [], []]

        def copy(stage, k, src, dst, sem, peer):
            self.stages[stage].append(pltpu.make_async_remote_copy(
                src_ref=src, dst_ref=dst, send_sem=sem.at[0, k], recv_sem=sem.at[1, k],
                device_id=peer, device_id_type=MESH))

        for k in range(1, 4):
            px, py = lax.rem(x + k, 4), lax.rem(y + k, 4)
            beside, above = {"leaf": px * 4 + y}, {"leaf": x * 4 + py}
            copy(0, k, local.at[pl.ds(pl.multiple_of(px * wide, 8), wide)], along_x.at[k], sems.at[0], beside)
            copy(1, k, part.at[pl.ds(pl.multiple_of(py * slim, 8), slim)], along_y.at[k], sems.at[1], above)
            copy(3, k, total.at[self.mine], total.at[self.mine], sems.at[2], above)
            copy(4, k, total.at[self.wide], total.at[self.wide], sems.at[3], beside)
        for k in range(1, N_BLK):
            copy(2, k, far.at[blk], far.at[blk], blk_sems, {"blk": lax.rem(blk + k, N_BLK)})

    def start(self, stage):
        for copy in self.stages[stage]:
            copy.start()

    def wait(self, stage):
        for copy in self.stages[stage]:
            copy.wait_recv()

    def begin(self, gram):
        self.local[0:128, :] = gram[0:128, 0:128]
        self.local[128:256, :] = gram[128:256, 0:128]
        self.local[256:384, :] = gram[128:256, 128:256]
        self.start(0)

    def second(self):
        self.wait(0)
        part = self.local[self.wide, :]
        for k in range(1, 4):
            part = part + self.along_x[k]
        self.part[...] = part
        self.start(1)

    def third(self):
        self.wait(1)
        part = self.part[self.slim, :]
        for k in range(1, 4):
            part = part + self.along_y[k]
        self.far[self.blk] = part
        self.start(2)

    def fourth(self):
        self.wait(2)
        part = self.far[0]
        for b in range(1, N_BLK):
            part = part + self.far[b]
        self.total[self.mine, :] = part
        self.start(3)

    def fifth(self):
        self.wait(3)
        self.start(4)

    def end(self):
        self.wait(4)

    def drain(self):
        for stage in self.stages:
            for copy in stage:
                copy.wait_send()


def axis_sum_scratch():
    return [
        pltpu.VMEM((384, 128), F32),
        pltpu.VMEM((4, 4 * CHUNK, 128), F32),
        pltpu.VMEM((4 * CHUNK, 128), F32),
        pltpu.VMEM((4, CHUNK, 128), F32),
        pltpu.VMEM((N_BLK, CHUNK, 128), F32),
        pltpu.VMEM((384, 128), F32),
        pltpu.SemaphoreType.DMA((4, 2, 4)),
        pltpu.SemaphoreType.DMA((2, N_BLK)),
    ]


SIDE = 128
BLOCK = 64


def factor_start(work, gram):
    work[:, 0:SIDE] = gram
    work[:, SIDE:] = (
        lax.broadcasted_iota(jnp.int32, (SIDE, SIDE), 0) == lax.broadcasted_iota(jnp.int32, (SIDE, SIDE), 1)
    ).astype(F32)


def factor(work, start):
    sub = lax.broadcasted_iota(jnp.int32, (8, 128), 0)
    if start:
        update = dot(work[0:start, start : start + BLOCK], work[0:start, :], 0, 0, HIGH)
        work[start : start + BLOCK, :] = work[start : start + BLOCK, :] - update
    count = BLOCK // 8
    tiles = 2
    x = [[work[start + 8 * t : start + 8 * t + 8, 128 * i : 128 * (i + 1)] for i in range(tiles)] for t in range(count)]
    for p in range(count):
        lane = start + 8 * p
        rest = range(p, count)
        col = [{t: jnp.broadcast_to(x[t][0][:, lane + j : lane + j + 1], (8, 128)) for t in rest} for j in range(8)]
        for j in range(8):
            inverse = lax.rsqrt(jnp.broadcast_to(col[j][p][j : j + 1, :], (8, 128)))
            low = {t: col[j][t] * inverse for t in rest}
            for k in range(j + 1, 8):
                pivot = jnp.broadcast_to(low[p][k : k + 1, :], (8, 128))
                for t in rest:
                    col[k][t] = col[k][t] - low[t] * pivot
            for i in range(tiles):
                row = jnp.broadcast_to(x[p][i][j : j + 1, :], (8, 128)) * inverse
                for t in rest:
                    moved = x[t][i] - low[t] * row
                    if t == p:
                        moved = jnp.where(sub > j, moved, jnp.where(sub == j, row, x[t][i]))
                    x[t][i] = moved
        for i in range(tiles):
            work[start + 8 * p : start + 8 * p + 8, 128 * i : 128 * (i + 1)] = x[p][i]


def factored(work):
    keep = lax.broadcasted_iota(jnp.int32, (SIDE, SIDE), 0) <= lax.broadcasted_iota(jnp.int32, (SIDE, SIDE), 1)
    return jnp.where(keep, work[:, 0:SIDE], 0.0), work[:, SIDE:]


def dot3(a, b, ca, cb):
    (ah, al), (bh, bl) = split2(a), split2(b)
    return dot(ah, bh, ca, cb) + (dot(ah, bl, ca, cb) + dot(al, bh, ca, cb))


TOTAL = N_LEAF * N_BLK
STEPS = (-1, 1)


class Exchange:
    def __init__(self, device, near, far, relay, near_to, far_to, sems):
        self.near_to, self.far_to = near_to, far_to
        self.direct, self.away, self.onward = [], [], []
        self.one, self.two, self.from_one, self.from_two = [], [], [], []
        self.between = (device >= 1) & (device < TOTAL - 1)
        for u, step in enumerate(STEPS):
            peer = lax.rem(device + step + TOTAL, TOTAL)
            there = (lax.div(peer, N_LEAF), lax.rem(peer, N_LEAF))

            def copy(kind, src, dst):
                return pltpu.make_async_remote_copy(
                    src_ref=src, dst_ref=dst, send_sem=sems.at[0, kind, u], recv_sem=sems.at[1, kind, u],
                    device_id=there, device_id_type=MESH)

            self.direct.append(copy(0, near[u], near_to[u]))
            self.away.append(copy(1, far[u], relay.at[u]))
            self.onward.append(copy(2, relay.at[u], far_to[u]))
            self.one.append(self.within(device + step))
            self.two.append(self.within(device + 2 * step))
            self.from_one.append(self.within(device - step))
            self.from_two.append(self.within(device - 2 * step))

    def within(self, device):
        return (device >= 0) & (device < TOTAL)

    def send_far(self, u):
        pl.when(self.two[u])(self.away[u].start)

    def send_near(self, u):
        pl.when(self.one[u])(self.direct[u].start)

    def forward(self):
        for u in range(2):
            @pl.when(self.between)
            def _():
                self.away[u].wait_recv()
                self.onward[u].start()

    def receive(self, arrives, copy, to):
        pl.when(arrives)(copy.wait_recv)

        @pl.when(jnp.logical_not(arrives))
        def _():
            to[...] = jnp.zeros(to.shape, F32)

    def receive_near(self):
        for u in range(2):
            self.receive(self.from_one[u], self.direct[u], self.near_to[u])

    def receive_far(self):
        for u in range(2):
            self.receive(self.from_two[u], self.onward[u], self.far_to[u])

    def drain(self):
        for u in range(2):
            pl.when(self.two[u])(self.away[u].wait_send)
            pl.when(self.one[u])(self.direct[u].wait_send)
            pl.when(self.between)(self.onward[u].wait_send)


STORED = (512, 256, 384, 640)
NEAR_OUT, FAR_OUT = (1, 2), (0, 3)
NEAR_BACK, FAR_BACK = (2, 1), (3, 0)
OWN, NEAR, FAR = slice(0, 256), slice(256, 512), slice(512, 768)
COMPONENTS = [slice(256 * c, 256 * (c + 1)) for c in range(3)]


def main_kernel(scale, count, modes, stiffness, connect, send, bottom_out, low_out, rest_out, r_out, top_out, inv_out, q_out,
                outgoing, table, relay, acc, incoming, relay_back, halo_sems, back_sems,
                ext_hi, ext_lo, pick, place, taken, blocks, matrix_hi, matrix_lo, product, stiff, work, *sums):
    leaf, blk = lax.axis_index("leaf"), lax.axis_index("blk")
    device = blk * N_LEAF + leaf
    barrier = greet(leaf, blk)

    def rows_of(ref, j):
        return ref.at[pl.ds(STORED[j], 128)]

    halo = Exchange(
        device, [outgoing.at[j] for j in NEAR_OUT], [outgoing.at[j] for j in FAR_OUT], relay,
        [rows_of(table, j) for j in NEAR_OUT], [rows_of(table, j) for j in FAR_OUT], halo_sems)
    back = Exchange(
        device, [rows_of(acc, j) for j in NEAR_BACK], [rows_of(acc, j) for j in FAR_BACK], relay_back,
        [incoming.at[j] for j in NEAR_BACK], [incoming.at[j] for j in FAR_BACK], back_sems)
    greeted = N_LEAF + N_BLK - 2
    for u, step in enumerate(STEPS):
        peer = lax.rem(device + step + TOTAL, TOTAL)
        there = (lax.div(peer, N_LEAF), lax.rem(peer, N_LEAF))
        greeted = greeted + halo.from_one[u].astype(jnp.int32)

        @pl.when(halo.one[u])
        def _():
            pl.semaphore_signal(barrier, inc=1, device_id=there, device_id_type=MESH)

    first, cross = (AxisSum(leaf, blk, *sums[8 * i : 8 * i + 8]) for i in range(2))
    top, bottom = (Sum(leaf, blk, *sums[16 + 6 * i : 22 + 6 * i]) for i in range(2))

    chosen = send[...]
    columns = columns_of(chosen, 4)
    nodes = lax.broadcasted_iota(jnp.int32, (128, 256), 1).astype(F32)
    wide = jnp.concatenate([modes[c] for c in range(3)], axis=1)
    parts = split3(wide)

    def prepare(j):
        chooser = (columns[:, j : j + 1] == nodes).astype(BF16)
        outgoing[j] = sum(dot(chooser, part, 1, 0) for part in parts)

    prepare(FAR_OUT[0])
    pl.semaphore_wait(barrier, greeted)
    halo.send_far(0)
    prepare(FAR_OUT[1])
    halo.send_far(1)
    for u in range(2):
        prepare(NEAR_OUT[u])
        halo.send_near(u)
    table[OWN, :] = wide
    ext_hi[OWN, :], ext_lo[OWN, :] = parts[0], parts[1]
    first.begin(sum(dot3(modes[c].T, modes[c], 1, 0) for c in range(3)))

    conn = connect[...]
    columns = columns_of(conn, 10)

    def table_id(at):
        return jnp.where(at < 256, at, jnp.where(at < 512, at + 128, jnp.where(at < 640, at - 256, at)))

    lanes = table_id(lax.broadcasted_iota(jnp.int32, (128, 768), 1)).astype(F32)
    rows = table_id(lax.broadcasted_iota(jnp.int32, (768, 128), 0))
    for k in range(10):
        pick[128 * k : 128 * (k + 1), :] = (columns[:, k : k + 1] == lanes).astype(BF16)
        place[:, 128 * k : 128 * (k + 1)] = (rows == conn[k : k + 1, :]).astype(BF16)

    def gather(span):
        if span is not OWN:
            ext_hi[span, :], ext_lo[span, :] = split2(table[span, :])

        def body(step, carry):
            at = pl.ds(pl.multiple_of(step * 320, 320), 320)
            picked = pick[at, span]
            found = dot(picked, ext_hi[span, :], 1, 0) + dot(picked, ext_lo[span, :], 1, 0)
            taken[at, :] = found if span is OWN else taken[at, :] + found
            return carry

        lax.fori_loop(0, 4, body, 0)

    gather(OWN)

    live = lax.broadcasted_iota(jnp.int32, (30, 128), 1) < count[0]
    source = lax.broadcasted_iota(jnp.int32, (30, 256), 0)
    target = lax.broadcasted_iota(jnp.int32, (30, 256), 1)
    wanted = lax.rem(source, 3) * 10 + lax.div(source, 3)
    spread = (lax.shift_right_logical(target, 3) == wanted).astype(BF16)
    for k in range(10):
        for c in range(3):
            block = jnp.concatenate([stiffness[k, c, l] for l in range(10)], axis=0)
            hi, lo = split2(jnp.where(live, block, 0.0))
            blocks[10 * c + k] = dot(hi, spread, 0, 0) + dot(lo, spread, 0, 0)

    halo.forward()
    keep = lax.broadcasted_iota(jnp.int32, (8, 256), 0) == lax.rem(lax.broadcasted_iota(jnp.int32, (8, 256), 1), 8)

    def assemble(g, carry):
        at = pl.ds(pl.multiple_of(g * 8, 8), 8)
        matrix = jnp.concatenate([jnp.where(keep, blocks[n, at, :], 0.0) for n in range(30)], axis=0)
        matrix_hi[g], matrix_lo[g] = split2(matrix)
        return carry

    lax.fori_loop(0, 16, assemble, 0)
    halo.receive_near()
    gather(NEAR)
    first.second()
    halo.receive_far()
    first.third()
    gather(FAR)
    first.fourth()

    def group(g, carry):
        spans = [pl.ds(pl.multiple_of(128 * k + g * 8, 8), 8) for k in range(10)]
        vectors = jnp.concatenate(
            [taken[spans[l], COMPONENTS[d]] for d in range(3) for l in range(10)] + [jnp.zeros((16, 256), F32)], axis=0)
        v_hi, v_lo = split2(vectors)
        m_hi, m_lo = matrix_hi[g], matrix_lo[g]
        result = dot(m_hi, v_hi, 1, 0) + (dot(m_hi, v_lo, 1, 0) + dot(m_lo, v_hi, 1, 0))
        for c in range(3):
            for k in range(10):
                n = 10 * c + k
                product[spans[k], COMPONENTS[c]] = result[8 * n : 8 * n + 8, :]
        return carry

    lax.fori_loop(0, 16, group, 0, unroll=2)
    first.fifth()
    halves = [split2(product[:, at]) for at in COMPONENTS]

    def scatter(span):
        where = place[span, :]
        for c, at in enumerate(COMPONENTS):
            acc[span, at] = dot(where, halves[c][0], 1, 0) + dot(where, halves[c][1], 1, 0)

    scatter(FAR)
    back.send_far(0)
    back.send_far(1)
    scatter(NEAR)
    back.send_near(0)
    back.send_near(1)
    scatter(OWN)

    gram = jnp.zeros((256, 256), F32)
    for at in COMPONENTS:
        hi, lo = split2(acc[:, at].T)
        t_hi, t_lo = ext_hi[:, at], ext_lo[:, at]
        gram = gram + (dot(hi, t_hi, 1, 0) + (dot(hi, t_lo, 1, 0) + dot(lo, t_hi, 1, 0)))
    cross.begin(gram)

    first.end()
    factor_start(work, first.total[0:128, :])
    factor(work, 0)
    factor(work, 64)
    back.forward()
    r00, i00 = factored(work)
    r01 = dot(i00, first.total[128:256, :], 1, 1, HIGH)
    factor_start(work, first.total[256:384, :] - dot(r01, r01, 0, 0, HIGH))
    factor(work, 0)
    factor(work, 64)
    r11, i11 = factored(work)
    cross.second()
    r_out[0:128, 0:128], r_out[0:128, 128:256] = r00, r01
    r_out[128:256, 0:128], r_out[128:256, 128:256] = jnp.zeros((SIDE, SIDE), F32), r11
    i10 = dot(i11, dot(r01, i00, 0, 0, HIGH), 1, 0, HIGH)
    inv = jnp.concatenate(
        [jnp.concatenate([i00, jnp.zeros((SIDE, SIDE), F32)], axis=1), jnp.concatenate([-i10, i11], axis=1)], axis=0)
    for c in range(3):
        q_out[c, :, 0:256] = dot3(modes[c], inv, 1, 1) * scale
    cross.third()

    rows = lax.broadcasted_iota(jnp.int32, (256, 128), 0)
    to_own = jnp.concatenate([(rows == chosen[j : j + 1, :]).astype(BF16) for j in range(4)], axis=1)
    back.receive_near()
    cross.fourth()
    back.receive_far()
    cross.fifth()
    gram = jnp.zeros((256, 256), F32)
    for c, at in enumerate(COMPONENTS):
        halves = split2(jnp.concatenate([incoming[j, :, at] for j in range(4)], axis=0))
        whole = acc[OWN, at] + sum(dot(to_own, half, 1, 0) for half in halves)
        stiff[c] = whole
        gram = gram + dot3(whole.T, whole, 1, 0)
    top.begin(gram[0:128, 0:128])
    bottom.begin(gram[128:256, 0:128], gram[128:256, 128:256])
    cross.end()
    crossed = cross.total
    gram = jnp.concatenate(
        [jnp.concatenate([crossed[0:128, :], crossed[128:256, :].T], axis=1),
         jnp.concatenate([crossed[128:256, :], crossed[256:384, :]], axis=1)], axis=0)
    low = dot(gram, inv, 1, 1, HIGH)
    low_out[...] = low
    top.across()
    bottom.across()
    for c in range(3):
        stiff[c] = stiff[c] - dot3(q_out[c, :, 0:256], low / scale, 1, 1)
    top.gather()
    bottom.gather()
    halo.drain()
    back.drain()
    first.drain()
    cross.drain()
    top.end()
    factor_start(work, top.total[...] - dot(low[0:128, :], low[0:128, :], 1, 1, HIGH))
    factor(work, 0)
    factor(work, 64)
    r22, i22 = factored(work)
    top_out[...] = r22
    inv_out[...] = i22
    for c in range(3):
        q_out[c, :, 256:384] = dot3(stiff[c, :, 0:128], i22, 1, 1) * scale
        rest_out[c] = stiff[c, :, 128:256]
    top.drain()
    bottom.end()
    bottom.drain()
    bottom_out[...] = bottom.total[...]


def up_to_last_gram(scale, count, modes, stiffness, connect, send):
    shapes = ((256, 128), (256, 256), (3, 256, 128), (256, 256), (128, 128), (128, 128), (3, 256, 384))
    rows = pltpu.VMEM((4, 128, 768), F32)
    table = pltpu.VMEM((768, 768), F32)
    relay = pltpu.VMEM((2, 128, 768), F32)
    sems = pltpu.SemaphoreType.DMA((2, 3, 2))
    return pl.pallas_call(
        functools.partial(main_kernel, scale),
        out_shape=[jax.ShapeDtypeStruct(shape, F32) for shape in shapes],
        in_specs=[SMEM] + [VMEM] * 4,
        out_specs=[VMEM] * len(shapes),
        scratch_shapes=[
            rows, table, relay, table, rows, relay, sems, sems,
            pltpu.VMEM((768, 768), BF16),
            pltpu.VMEM((768, 768), BF16),
            pltpu.VMEM((1280, 768), BF16),
            pltpu.VMEM((768, 1280), BF16),
            pltpu.VMEM((1280, 768), F32),
            pltpu.VMEM((30, 128, 256), F32),
            pltpu.VMEM((16, 240, 256), BF16),
            pltpu.VMEM((16, 240, 256), BF16),
            pltpu.VMEM((1280, 768), F32),
            pltpu.VMEM((3, 256, 256), F32),
            pltpu.VMEM((SIDE, 2 * SIDE), F32),
        ] + axis_sum_scratch() + axis_sum_scratch() + sum_scratch(1) + sum_scratch(2),
        compiler_params=pltpu.CompilerParams(collective_id=1, has_side_effects=True, vmem_limit_bytes=LIMIT),
        name="up_to_last_gram",
    )(count, modes, stiffness, connect, send)


def second_kernel(scale, bottom, low, r_first, r_top, i_top, rest, q_in, q_out, r_out, work, columns, last, sems):
    fetch = pltpu.make_async_copy(q_in, columns, sems.at[0])
    done = pltpu.make_async_copy(columns, q_out.at[:, :, pl.ds(0, 384)], sems.at[1])
    fetch.start()
    low0, low1 = low[0:128, :], low[128:256, :]
    side = bottom[0:128, :] - dot(low1, low0, 1, 1, HIGH)
    r01 = dot(i_top[...], side, 1, 1, HIGH)
    factor_start(work, bottom[128:256, :] - dot(low1, low1, 1, 1, HIGH) - dot(r01, r01, 0, 0, HIGH))
    factor(work, 0)
    fetch.wait()
    done.start()
    r_out[0:256, 0:256] = r_first[...] / scale
    r_out[0:256, 256:512] = low[...].T / scale
    r_out[256:512, 0:256] = jnp.zeros((256, 256), F32)
    r_out[256:384, 256:384] = r_top[...] / scale
    r_out[256:384, 384:512] = r01 / scale
    r_out[384:512, 256:384] = jnp.zeros((128, 128), F32)
    factor(work, 64)
    r11, i11 = factored(work)
    r_out[384:512, 384:512] = r11 / scale
    for c in range(3):
        left = rest[c] - dot3(columns[c, :, 256:384], r01 / scale, 1, 0)
        last[c] = dot3(left, i11, 1, 1) * scale
    place = pltpu.make_async_copy(last, q_out.at[:, :, pl.ds(384, 128)], sems.at[2])
    place.start()
    place.wait()
    done.wait()


def second(scale, *operands):
    anywhere = pl.BlockSpec(memory_space=pl.ANY)
    return pl.pallas_call(
        functools.partial(second_kernel, scale),
        out_shape=[jax.ShapeDtypeStruct((3, 256, 512), F32), jax.ShapeDtypeStruct((512, 512), F32)],
        in_specs=[VMEM] * 6 + [anywhere],
        out_specs=[anywhere, VMEM],
        scratch_shapes=[
            pltpu.VMEM((SIDE, 2 * SIDE), F32),
            pltpu.VMEM((3, 256, 384), F32),
            pltpu.VMEM((3, 256, 128), F32),
            pltpu.SemaphoreType.DMA((3,)),
        ],
        compiler_params=pltpu.CompilerParams(vmem_limit_bytes=LIMIT),
        name="second_factor",
    )(*operands)


def shards(modes, stiffness, connect, send_list, elem_count):
    modes = jnp.transpose(modes, (1, 0, 2))
    scale = float((3 * 256 * lax.axis_size("blk") * lax.axis_size("leaf")) ** 0.5)
    bottom, low, rest, r_first, r_top, i_top, q = up_to_last_gram(
        scale, elem_count, modes, stiffness, connect, send_list[0])
    q, r = second(scale, bottom, low, r_first, r_top, i_top, rest, q)
    return (jnp.transpose(q, (1, 0, 2)), r)


def solution(mesh):
    placed = (
        P(("blk", "leaf"), None, None),
        P(None, None, None, None, ("blk", "leaf")),
        P(None, ("blk", "leaf")),
        P(("blk", "leaf"), None, None),
        P(("blk", "leaf")),
    )
    return jax.shard_map(
        shards,
        mesh=mesh,
        in_specs=placed,
        out_specs=(P(("blk", "leaf"), None, None), P()),
        check_vma=False,
    )
```

```python
import functools

import jax
import jax.numpy as jnp
from jax import lax
from jax.experimental import pallas as pl
from jax.experimental.pallas import tpu as pltpu
from jax.sharding import PartitionSpec as P

HIGH = lax.Precision.HIGHEST
F32 = jnp.float32
BF16 = jnp.bfloat16
MESH = pl.DeviceIdType.MESH
VMEM = pl.BlockSpec(memory_space=pltpu.VMEM)
SMEM = pl.BlockSpec(memory_space=pltpu.SMEM)
LIMIT = 56 * 1024 * 1024


def dot(a, b, ca, cb, precision=None):
    return lax.dot_general(a, b, (((ca,), (cb,)), ((), ())), precision=precision, preferred_element_type=F32)


def split2(x):
    hi = x.astype(BF16)
    return hi, (x - hi.astype(F32)).astype(BF16)


def split3(x):
    hi = x.astype(BF16)
    rest = x - hi.astype(F32)
    mid = rest.astype(BF16)
    return hi, mid, (rest - mid.astype(F32)).astype(BF16)


def columns_of(rows, count):
    padded = jnp.concatenate([rows.astype(F32), jnp.zeros((16 - count, 128), F32)], axis=0)
    return padded.T


N_LEAF = 16
N_BLK = 8


def greet(leaf, blk):
    barrier = pltpu.get_barrier_semaphore()
    for k in range(1, N_LEAF):
        pl.semaphore_signal(barrier, inc=1, device_id={"leaf": lax.rem(leaf + k, N_LEAF)}, device_id_type=MESH)
    for k in range(1, N_BLK):
        pl.semaphore_signal(barrier, inc=1, device_id={"blk": lax.rem(blk + k, N_BLK)}, device_id_type=MESH)
    return barrier


class Sum:
    def __init__(self, leaf, blk, local, near, far, total, leaf_sems, blk_sems):
        size = local.shape[0] // N_LEAF
        self.blk = blk
        self.local, self.near, self.far, self.total = local, near, far, total
        mine = pl.ds(pl.multiple_of(leaf * size, 8), size)
        self.mine = mine
        self.spread, self.cross, self.collect = [], [], []
        for k in range(1, N_LEAF):
            peer = lax.rem(leaf + k, N_LEAF)
            self.spread.append(pltpu.make_async_remote_copy(
                src_ref=local.at[pl.ds(pl.multiple_of(peer * size, 8), size)], dst_ref=near.at[k],
                send_sem=leaf_sems.at[0, k], recv_sem=leaf_sems.at[1, k], device_id={"leaf": peer}, device_id_type=MESH))
            self.collect.append(pltpu.make_async_remote_copy(
                src_ref=total.at[mine], dst_ref=total.at[mine],
                send_sem=leaf_sems.at[2, k], recv_sem=leaf_sems.at[3, k], device_id={"leaf": peer}, device_id_type=MESH))
        for k in range(1, N_BLK):
            peer = lax.rem(blk + k, N_BLK)
            self.cross.append(pltpu.make_async_remote_copy(
                src_ref=far.at[blk], dst_ref=far.at[blk],
                send_sem=blk_sems.at[0, k], recv_sem=blk_sems.at[1, k], device_id={"blk": peer}, device_id_type=MESH))

    def begin(self, *parts):
        for n, part in enumerate(parts):
            self.local[128 * n : 128 * (n + 1), :] = part
        for copy in self.spread:
            copy.start()

    def across(self):
        part = self.local[self.mine, :]
        for k, copy in enumerate(self.spread):
            copy.wait_recv()
            part = part + self.near[k + 1]
        self.far[self.blk] = part
        for copy in self.cross:
            copy.start()

    def gather(self):
        for copy in self.cross:
            copy.wait_recv()
        part = self.far[0]
        for b in range(1, N_BLK):
            part = part + self.far[b]
        self.total[self.mine, :] = part
        for copy in self.collect:
            copy.start()

    def end(self):
        for copy in self.collect:
            copy.wait_recv()

    def drain(self):
        for copy in self.spread + self.cross + self.collect:
            copy.wait_send()


def sum_scratch(parts):
    size = 128 * parts // N_LEAF
    return [
        pltpu.VMEM((128 * parts, 128), F32),
        pltpu.VMEM((N_LEAF, size, 128), F32),
        pltpu.VMEM((N_BLK, size, 128), F32),
        pltpu.VMEM((128 * parts, 128), F32),
        pltpu.SemaphoreType.DMA((4, N_LEAF)),
        pltpu.SemaphoreType.DMA((2, N_BLK)),
    ]


class BlkSum:
    def __init__(self, leaf, blk, local, along_blk, along_y, along_x, total, sems, blk_sems):
        size = local.shape[0] // N_BLK
        x, y = lax.div(leaf, 4), lax.rem(leaf, 4)
        self.x, self.y, self.local, self.total = x, y, local, total
        self.along_blk, self.along_y, self.along_x = along_blk, along_y, along_x
        self.mine = pl.ds(pl.multiple_of(blk * size, 8), size)
        self.stages = [[], [], [], []]

        def copy(stage, k, src, dst, sem, peer):
            self.stages[stage].append(pltpu.make_async_remote_copy(
                src_ref=src, dst_ref=dst, send_sem=sem.at[0, k], recv_sem=sem.at[1, k],
                device_id=peer, device_id_type=MESH))

        for k in range(1, N_BLK):
            peer = lax.rem(blk + k, N_BLK)
            copy(0, k, local.at[pl.ds(pl.multiple_of(peer * size, 8), size)], along_blk.at[k], blk_sems.at[0], {"blk": peer})
            copy(3, k, total.at[self.mine], total.at[self.mine], blk_sems.at[1], {"blk": peer})
        for k in range(1, 4):
            copy(1, k, along_y.at[y], along_y.at[y], sems.at[0], {"leaf": x * 4 + lax.rem(y + k, 4)})
            copy(2, k, along_x.at[x], along_x.at[x], sems.at[1], {"leaf": lax.rem(x + k, 4) * 4 + y})

    def start(self, stage):
        for copy in self.stages[stage]:
            copy.start()

    def wait(self, stage):
        for copy in self.stages[stage]:
            copy.wait_recv()

    def begin(self, *parts):
        for n, part in enumerate(parts):
            self.local[128 * n : 128 * (n + 1), :] = part
        self.start(0)

    def second(self):
        self.wait(0)
        part = self.local[self.mine, :]
        for k in range(1, N_BLK):
            part = part + self.along_blk[k]
        self.along_y[self.y] = part
        self.start(1)

    def third(self):
        self.wait(1)
        part = self.along_y[0]
        for k in range(1, 4):
            part = part + self.along_y[k]
        self.along_x[self.x] = part
        self.start(2)

    def fourth(self):
        self.wait(2)
        part = self.along_x[0]
        for k in range(1, 4):
            part = part + self.along_x[k]
        self.total[self.mine, :] = part
        self.start(3)

    def end(self):
        self.wait(3)

    def drain(self):
        for stage in self.stages:
            for copy in stage:
                copy.wait_send()


def blk_sum_scratch():
    return [
        pltpu.VMEM((384, 128), F32),
        pltpu.VMEM((N_BLK, 48, 128), F32),
        pltpu.VMEM((4, 48, 128), F32),
        pltpu.VMEM((4, 48, 128), F32),
        pltpu.VMEM((384, 128), F32),
        pltpu.SemaphoreType.DMA((2, 2, 4)),
        pltpu.SemaphoreType.DMA((2, 2, N_BLK)),
    ]


SIDE = 128
BLOCK = 64


def factor_start(work, gram):
    work[:, 0:SIDE] = gram
    work[:, SIDE:] = (
        lax.broadcasted_iota(jnp.int32, (SIDE, SIDE), 0) == lax.broadcasted_iota(jnp.int32, (SIDE, SIDE), 1)
    ).astype(F32)


def factor(work, start):
    sub = lax.broadcasted_iota(jnp.int32, (8, 128), 0)
    if start:
        update = dot(work[0:start, start : start + BLOCK], work[0:start, :], 0, 0, HIGH)
        work[start : start + BLOCK, :] = work[start : start + BLOCK, :] - update
    count = BLOCK // 8
    tiles = 2
    x = [[work[start + 8 * t : start + 8 * t + 8, 128 * i : 128 * (i + 1)] for i in range(tiles)] for t in range(count)]
    for p in range(count):
        lane = start + 8 * p
        rest = range(p, count)
        col = [{t: jnp.broadcast_to(x[t][0][:, lane + j : lane + j + 1], (8, 128)) for t in rest} for j in range(8)]
        for j in range(8):
            inverse = lax.rsqrt(jnp.broadcast_to(col[j][p][j : j + 1, :], (8, 128)))
            low = {t: col[j][t] * inverse for t in rest}
            for k in range(j + 1, 8):
                pivot = jnp.broadcast_to(low[p][k : k + 1, :], (8, 128))
                for t in rest:
                    col[k][t] = col[k][t] - low[t] * pivot
            for i in range(tiles):
                row = jnp.broadcast_to(x[p][i][j : j + 1, :], (8, 128)) * inverse
                for t in rest:
                    moved = x[t][i] - low[t] * row
                    if t == p:
                        moved = jnp.where(sub > j, moved, jnp.where(sub == j, row, x[t][i]))
                    x[t][i] = moved
        for i in range(tiles):
            work[start + 8 * p : start + 8 * p + 8, 128 * i : 128 * (i + 1)] = x[p][i]


def factored(work):
    keep = lax.broadcasted_iota(jnp.int32, (SIDE, SIDE), 0) <= lax.broadcasted_iota(jnp.int32, (SIDE, SIDE), 1)
    return jnp.where(keep, work[:, 0:SIDE], 0.0), work[:, SIDE:]


def dot3(a, b, ca, cb):
    (ah, al), (bh, bl) = split2(a), split2(b)
    return dot(ah, bh, ca, cb) + (dot(ah, bl, ca, cb) + dot(al, bh, ca, cb))


TOTAL = N_LEAF * N_BLK
STEPS = (-1, 1)


class Exchange:
    def __init__(self, device, near, far, relay, near_to, far_to, sems):
        self.near_to, self.far_to = near_to, far_to
        self.direct, self.away, self.onward = [], [], []
        self.one, self.two, self.from_one, self.from_two = [], [], [], []
        self.between = (device >= 1) & (device < TOTAL - 1)
        for u, step in enumerate(STEPS):
            peer = lax.rem(device + step + TOTAL, TOTAL)
            there = (lax.div(peer, N_LEAF), lax.rem(peer, N_LEAF))

            def copy(kind, src, dst):
                return pltpu.make_async_remote_copy(
                    src_ref=src, dst_ref=dst, send_sem=sems.at[0, kind, u], recv_sem=sems.at[1, kind, u],
                    device_id=there, device_id_type=MESH)

            self.direct.append(copy(0, near[u], near_to[u]))
            self.away.append(copy(1, far[u], relay.at[u]))
            self.onward.append(copy(2, relay.at[u], far_to[u]))
            self.one.append(self.within(device + step))
            self.two.append(self.within(device + 2 * step))
            self.from_one.append(self.within(device - step))
            self.from_two.append(self.within(device - 2 * step))

    def within(self, device):
        return (device >= 0) & (device < TOTAL)

    def send_far(self):
        for u in range(2):
            pl.when(self.two[u])(self.away[u].start)

    def send_near(self):
        for u in range(2):
            pl.when(self.one[u])(self.direct[u].start)

    def forward(self):
        for u in range(2):
            @pl.when(self.between)
            def _():
                self.away[u].wait_recv()
                self.onward[u].start()

    def receive(self, arrives, copy, to):
        pl.when(arrives)(copy.wait_recv)

        @pl.when(jnp.logical_not(arrives))
        def _():
            to[...] = jnp.zeros(to.shape, F32)

    def receive_near(self):
        for u in range(2):
            self.receive(self.from_one[u], self.direct[u], self.near_to[u])

    def receive_far(self):
        for u in range(2):
            self.receive(self.from_two[u], self.onward[u], self.far_to[u])

    def drain(self):
        for u in range(2):
            pl.when(self.two[u])(self.away[u].wait_send)
            pl.when(self.one[u])(self.direct[u].wait_send)
            pl.when(self.between)(self.onward[u].wait_send)


STORED = (512, 256, 384, 640)
NEAR_OUT, FAR_OUT = (1, 2), (0, 3)
NEAR_BACK, FAR_BACK = (2, 1), (3, 0)


def main_kernel(scale, count, modes, stiffness, connect, send, bottom_out, low_out, rest_out, r_out, top_out, inv_out, q_out,
                outgoing, table, relay, acc, incoming, relay_back, halo_sems, back_sems,
                ext_hi, ext_lo, pick, place, taken, blocks, matrix_hi, matrix_lo, product, stiff, work, *sums):
    leaf, blk = lax.axis_index("leaf"), lax.axis_index("blk")
    device = blk * N_LEAF + leaf
    barrier = greet(leaf, blk)

    def rows_of(ref, h, j):
        return ref.at[h, pl.ds(STORED[j], 128)]

    halo, back = [], []
    for h in range(2):
        halo.append(Exchange(
            device, [outgoing.at[h, j] for j in NEAR_OUT], [outgoing.at[h, j] for j in FAR_OUT], relay.at[h],
            [rows_of(table, h, j) for j in NEAR_OUT], [rows_of(table, h, j) for j in FAR_OUT], halo_sems.at[h]))
        back.append(Exchange(
            device, [rows_of(acc, h, j) for j in NEAR_BACK], [rows_of(acc, h, j) for j in FAR_BACK], relay_back.at[h],
            [incoming.at[h, j] for j in NEAR_BACK], [incoming.at[h, j] for j in FAR_BACK], back_sems.at[h]))
    greeted = N_LEAF + N_BLK - 2
    for u, step in enumerate(STEPS):
        peer = lax.rem(device + step + TOTAL, TOTAL)
        there = (lax.div(peer, N_LEAF), lax.rem(peer, N_LEAF))
        greeted = greeted + halo[0].from_one[u].astype(jnp.int32)

        @pl.when(halo[0].one[u])
        def _():
            pl.semaphore_signal(barrier, inc=1, device_id=there, device_id_type=MESH)

    first, cross = (BlkSum(leaf, blk, *sums[7 * i : 7 * i + 7]) for i in range(2))
    top, bottom = (Sum(leaf, blk, *sums[14 + 6 * i : 20 + 6 * i]) for i in range(2))

    chosen = send[...]
    columns = columns_of(chosen, 4)
    nodes = lax.broadcasted_iota(jnp.int32, (128, 256), 1).astype(F32)
    choosers = [(columns[:, j : j + 1] == nodes).astype(BF16) for j in range(4)]

    wides = [jnp.concatenate([modes[c, :, 128 * h : 128 * (h + 1)] for c in range(3)], axis=1) for h in range(2)]
    parts = [split3(wide) for wide in wides]

    def prepare(h, directions):
        for j in directions:
            outgoing[h, j] = sum(dot(choosers[j], part, 1, 0) for part in parts[h])

    prepare(0, FAR_OUT)
    pl.semaphore_wait(barrier, greeted)
    halo[0].send_far()
    prepare(0, NEAR_OUT)
    halo[0].send_near()
    gram = sum(dot3(modes[c].T, modes[c], 1, 0) for c in range(3))
    first.begin(gram[0:128, 0:128], gram[128:256, 0:128], gram[128:256, 128:256])
    prepare(1, FAR_OUT + NEAR_OUT)
    for h in range(2):
        table[h, 0:256, :] = wides[h]
        ext_hi[h, 0:256, :], ext_lo[h, 0:256, :] = parts[h][0], parts[h][1]

    conn = connect[...]
    columns = columns_of(conn, 10)

    def table_id(at):
        return jnp.where(at < 256, at, jnp.where(at < 512, at + 128, jnp.where(at < 640, at - 256, at)))

    lanes = table_id(lax.broadcasted_iota(jnp.int32, (128, 768), 1)).astype(F32)
    rows = table_id(lax.broadcasted_iota(jnp.int32, (768, 128), 0))
    for k in range(10):
        pick[128 * k : 128 * (k + 1), :] = (columns[:, k : k + 1] == lanes).astype(BF16)
        place[:, 128 * k : 128 * (k + 1)] = (rows == conn[k : k + 1, :]).astype(BF16)

    halo[0].forward()
    first.second()
    halo[1].send_far()
    halo[1].send_near()

    def gather(h, part):
        span = slice(256 * part, 256 * (part + 1))
        if part:
            ext_hi[h, span, :], ext_lo[h, span, :] = split2(table[h, span, :])

        def body(step, carry):
            at = pl.ds(pl.multiple_of(step * 320, 320), 320)
            picked = pick[at, span]
            found = dot(picked, ext_hi[h, span, :], 1, 0) + dot(picked, ext_lo[h, span, :], 1, 0)
            taken[h, at, :] = found if part == 0 else taken[h, at, :] + found
            return carry

        lax.fori_loop(0, 4, body, 0)

    gather(0, 0)
    gather(1, 0)

    live = lax.broadcasted_iota(jnp.int32, (30, 128), 1) < count[0]
    source = lax.broadcasted_iota(jnp.int32, (30, 256), 0)
    target = lax.broadcasted_iota(jnp.int32, (30, 256), 1)
    wanted = lax.rem(source, 3) * 10 + lax.div(source, 3)
    spread = (lax.shift_right_logical(target, 3) == wanted).astype(BF16)
    for k in range(10):
        for c in range(3):
            block = jnp.concatenate([stiffness[k, c, l] for l in range(10)], axis=0)
            hi, lo = split2(jnp.where(live, block, 0.0))
            blocks[10 * c + k] = dot(hi, spread, 0, 0) + dot(lo, spread, 0, 0)

    keep = lax.broadcasted_iota(jnp.int32, (8, 256), 0) == lax.rem(lax.broadcasted_iota(jnp.int32, (8, 256), 1), 8)

    def assemble(g, carry):
        at = pl.ds(pl.multiple_of(g * 8, 8), 8)
        matrix = jnp.concatenate([jnp.where(keep, blocks[n, at, :], 0.0) for n in range(30)], axis=0)
        matrix_hi[g], matrix_lo[g] = split2(matrix)
        return carry

    lax.fori_loop(0, 16, assemble, 0)
    first.third()

    def multiply(h):
        def group(g, carry):
            spans = [pl.ds(pl.multiple_of(128 * k + g * 8, 8), 8) for k in range(10)]
            vectors = jnp.concatenate(
                [taken[h, spans[l], 128 * d : 128 * (d + 1)] for d in range(3) for l in range(10)]
                + [jnp.zeros((16, 128), F32)],
                axis=0,
            )
            v_hi, v_lo = split2(vectors)
            m_hi, m_lo = matrix_hi[g], matrix_lo[g]
            result = dot(m_hi, v_hi, 1, 0) + (dot(m_hi, v_lo, 1, 0) + dot(m_lo, v_hi, 1, 0))
            for c in range(3):
                for k in range(10):
                    n = 10 * c + k
                    product[spans[k], 128 * c : 128 * (c + 1)] = result[8 * n : 8 * n + 8, :]
            return carry

        lax.fori_loop(0, 16, group, 0, unroll=2)
        return split2(product[...])

    def scatter(h, halves, span):
        where = place[span, :]
        acc[h, span, :] = dot(where, halves[0], 1, 0) + dot(where, halves[1], 1, 0)

    OWN, NEAR, FAR = slice(0, 256), slice(256, 512), slice(512, 768)

    halo[0].receive_near()
    gather(0, 1)
    halo[0].receive_far()
    gather(0, 2)
    halves = multiply(0)
    halo[1].forward()
    scatter(0, halves, FAR)
    back[0].send_far()
    scatter(0, halves, NEAR)
    back[0].send_near()
    scatter(0, halves, OWN)
    halo[1].receive_near()
    gather(1, 1)
    halo[1].receive_far()
    gather(1, 2)
    halves = multiply(1)
    back[0].forward()
    scatter(1, halves, FAR)
    back[1].send_far()
    scatter(1, halves, NEAR)
    back[1].send_near()
    first.fourth()
    scatter(1, halves, OWN)

    lower, diagonal = [], 0.0
    for c in range(3):
        at = slice(128 * c, 128 * (c + 1))
        tables = [jnp.concatenate([ext[0, :, at], ext[1, :, at]], axis=1) for ext in (ext_hi, ext_lo)]
        for h in range(2):
            hi, lo = split2(acc[h, :, at].T)
            t_hi, t_lo = (t if h else t[:, 0:128] for t in tables)
            found = dot(hi, t_hi, 1, 0) + (dot(hi, t_lo, 1, 0) + dot(lo, t_hi, 1, 0))
            if h:
                lower.append(found)
            else:
                diagonal = diagonal + found
    lower = sum(lower)
    cross.begin(diagonal, lower[:, 0:128], lower[:, 128:256])

    rows = lax.broadcasted_iota(jnp.int32, (256, 128), 0)
    to_own = jnp.concatenate([(rows == chosen[j : j + 1, :]).astype(BF16) for j in range(4)], axis=1)

    def complete(h):
        back[h].receive_near()
        back[h].receive_far()
        parts = split2(jnp.concatenate([incoming[h, j] for j in range(4)], axis=0))
        whole = acc[h, OWN, :] + sum(dot(to_own, part, 1, 0) for part in parts)
        for c in range(3):
            stiff[c, :, 128 * h : 128 * (h + 1)] = whole[:, 128 * c : 128 * (c + 1)]

    first.end()
    factor_start(work, first.total[0:128, :])
    factor(work, 0)
    back[1].forward()
    factor(work, 64)
    r00, i00 = factored(work)
    complete(0)
    top.begin(sum(dot3(stiff[c, :, 0:128].T, stiff[c, :, 0:128], 1, 0) for c in range(3)))
    r01 = dot(i00, first.total[128:256, :], 1, 1, HIGH)
    factor_start(work, first.total[256:384, :] - dot(r01, r01, 0, 0, HIGH))
    factor(work, 0)
    cross.second()
    factor(work, 64)
    r11, i11 = factored(work)
    r_out[0:128, 0:128], r_out[0:128, 128:256] = r00, r01
    r_out[128:256, 0:128], r_out[128:256, 128:256] = jnp.zeros((SIDE, SIDE), F32), r11
    i10 = dot(i11, dot(r01, i00, 0, 0, HIGH), 1, 0, HIGH)
    inv = jnp.concatenate(
        [jnp.concatenate([i00, jnp.zeros((SIDE, SIDE), F32)], axis=1), jnp.concatenate([-i10, i11], axis=1)], axis=0)
    cross.third()
    for c in range(3):
        q_out[c, :, 0:256] = dot3(modes[c], inv, 1, 1) * scale

    cross.fourth()
    complete(1)
    both = sum(dot3(stiff[c, :, 128:256].T, stiff[c], 1, 0) for c in range(3))
    bottom.begin(both[:, 0:128], both[:, 128:256])
    top.across()
    cross.end()
    crossed = cross.total
    gram = jnp.concatenate(
        [jnp.concatenate([crossed[0:128, :], crossed[128:256, :].T], axis=1),
         jnp.concatenate([crossed[128:256, :], crossed[256:384, :]], axis=1)], axis=0)
    low = dot(gram, inv, 1, 1, HIGH)
    low_out[...] = low
    top.gather()
    for c in range(3):
        stiff[c] = stiff[c] - dot3(q_out[c, :, 0:256], low / scale, 1, 1)
    bottom.across()
    top.end()
    factor_start(work, top.total[...] - dot(low[0:128, :], low[0:128, :], 1, 1, HIGH))
    factor(work, 0)
    bottom.gather()
    factor(work, 64)
    r22, i22 = factored(work)
    top_out[...] = r22
    inv_out[...] = i22
    for c in range(3):
        q_out[c, :, 256:384] = dot3(stiff[c, :, 0:128], i22, 1, 1) * scale
        rest_out[c] = stiff[c, :, 128:256]
    for h in range(2):
        halo[h].drain()
        back[h].drain()
    first.drain()
    cross.drain()
    top.drain()
    bottom.end()
    bottom.drain()
    bottom_out[...] = bottom.total[...]


def up_to_last_gram(scale, count, modes, stiffness, connect, send):
    shapes = ((256, 128), (256, 256), (3, 256, 128), (256, 256), (128, 128), (128, 128), (3, 256, 384))
    rows = pltpu.VMEM((2, 4, 128, 384), F32)
    table = pltpu.VMEM((2, 768, 384), F32)
    relay = pltpu.VMEM((2, 2, 128, 384), F32)
    sems = pltpu.SemaphoreType.DMA((2, 2, 3, 2))
    return pl.pallas_call(
        functools.partial(main_kernel, scale),
        out_shape=[jax.ShapeDtypeStruct(shape, F32) for shape in shapes],
        in_specs=[SMEM] + [VMEM] * 4,
        out_specs=[VMEM] * len(shapes),
        scratch_shapes=[
            rows, table, relay, table, rows, relay, sems, sems,
            pltpu.VMEM((2, 768, 384), BF16),
            pltpu.VMEM((2, 768, 384), BF16),
            pltpu.VMEM((1280, 768), BF16),
            pltpu.VMEM((768, 1280), BF16),
            pltpu.VMEM((2, 1280, 384), F32),
            pltpu.VMEM((30, 128, 256), F32),
            pltpu.VMEM((16, 240, 256), BF16),
            pltpu.VMEM((16, 240, 256), BF16),
            pltpu.VMEM((1280, 384), F32),
            pltpu.VMEM((3, 256, 256), F32),
            pltpu.VMEM((SIDE, 2 * SIDE), F32),
        ] + blk_sum_scratch() + blk_sum_scratch() + sum_scratch(1) + sum_scratch(2),
        compiler_params=pltpu.CompilerParams(collective_id=1, has_side_effects=True, vmem_limit_bytes=LIMIT),
        name="up_to_last_gram",
    )(count, modes, stiffness, connect, send)


def second_kernel(scale, bottom, low, r_first, r_top, i_top, rest, q_in, q_out, r_out, work, columns, last, sems):
    fetch = pltpu.make_async_copy(q_in, columns, sems.at[0])
    done = pltpu.make_async_copy(columns, q_out.at[:, :, pl.ds(0, 384)], sems.at[1])
    fetch.start()
    low0, low1 = low[0:128, :], low[128:256, :]
    side = bottom[0:128, :] - dot(low1, low0, 1, 1, HIGH)
    r01 = dot(i_top[...], side, 1, 1, HIGH)
    factor_start(work, bottom[128:256, :] - dot(low1, low1, 1, 1, HIGH) - dot(r01, r01, 0, 0, HIGH))
    factor(work, 0)
    fetch.wait()
    done.start()
    r_out[0:256, 0:256] = r_first[...] / scale
    r_out[0:256, 256:512] = low[...].T / scale
    r_out[256:512, 0:256] = jnp.zeros((256, 256), F32)
    r_out[256:384, 256:384] = r_top[...] / scale
    r_out[256:384, 384:512] = r01 / scale
    r_out[384:512, 256:384] = jnp.zeros((128, 128), F32)
    factor(work, 64)
    r11, i11 = factored(work)
    r_out[384:512, 384:512] = r11 / scale
    for c in range(3):
        left = rest[c] - dot3(columns[c, :, 256:384], r01 / scale, 1, 0)
        last[c] = dot3(left, i11, 1, 1) * scale
    place = pltpu.make_async_copy(last, q_out.at[:, :, pl.ds(384, 128)], sems.at[2])
    place.start()
    place.wait()
    done.wait()


def second(scale, *operands):
    anywhere = pl.BlockSpec(memory_space=pl.ANY)
    return pl.pallas_call(
        functools.partial(second_kernel, scale),
        out_shape=[jax.ShapeDtypeStruct((3, 256, 512), F32), jax.ShapeDtypeStruct((512, 512), F32)],
        in_specs=[VMEM] * 6 + [anywhere],
        out_specs=[anywhere, VMEM],
        scratch_shapes=[
            pltpu.VMEM((SIDE, 2 * SIDE), F32),
            pltpu.VMEM((3, 256, 384), F32),
            pltpu.VMEM((3, 256, 128), F32),
            pltpu.SemaphoreType.DMA((3,)),
        ],
        compiler_params=pltpu.CompilerParams(vmem_limit_bytes=LIMIT),
        name="second_factor",
    )(*operands)


def shards(modes, stiffness, connect, send_list, elem_count):
    modes = jnp.transpose(modes, (1, 0, 2))
    scale = float((3 * 256 * lax.axis_size("blk") * lax.axis_size("leaf")) ** 0.5)
    bottom, low, rest, r_first, r_top, i_top, q = up_to_last_gram(
        scale, elem_count, modes, stiffness, connect, send_list[0])
    q, r = second(scale, bottom, low, r_first, r_top, i_top, rest, q)
    return (jnp.transpose(q, (1, 0, 2)), r)


def solution(mesh):
    placed = (
        P(("blk", "leaf"), None, None),
        P(None, None, None, None, ("blk", "leaf")),
        P(None, ("blk", "leaf")),
        P(("blk", "leaf"), None, None),
        P(("blk", "leaf")),
    )
    return jax.shard_map(
        shards,
        mesh=mesh,
        in_specs=placed,
        out_specs=(P(("blk", "leaf"), None, None), P()),
        check_vma=False,
    )
```

```python
import functools

import jax
import jax.numpy as jnp
from jax import lax
from jax.experimental import pallas as pl
from jax.experimental.pallas import tpu as pltpu
from jax.sharding import PartitionSpec as P

HIGH = lax.Precision.HIGHEST
F32 = jnp.float32
BF16 = jnp.bfloat16
MESH = pl.DeviceIdType.MESH
VMEM = pl.BlockSpec(memory_space=pltpu.VMEM)
SMEM = pl.BlockSpec(memory_space=pltpu.SMEM)
LIMIT = 56 * 1024 * 1024


def dot(a, b, ca, cb, precision=None):
    return lax.dot_general(a, b, (((ca,), (cb,)), ((), ())), precision=precision, preferred_element_type=F32)


def split2(x):
    hi = x.astype(BF16)
    return hi, (x - hi.astype(F32)).astype(BF16)


def split3(x):
    hi = x.astype(BF16)
    rest = x - hi.astype(F32)
    mid = rest.astype(BF16)
    return hi, mid, (rest - mid.astype(F32)).astype(BF16)


def columns_of(rows, count):
    padded = jnp.concatenate([rows.astype(F32), jnp.zeros((16 - count, 128), F32)], axis=0)
    return padded.T


N_LEAF = 16
N_BLK = 8


def greet(leaf, blk):
    barrier = pltpu.get_barrier_semaphore()
    for k in range(1, N_LEAF):
        pl.semaphore_signal(barrier, inc=1, device_id={"leaf": lax.rem(leaf + k, N_LEAF)}, device_id_type=MESH)
    for k in range(1, N_BLK):
        pl.semaphore_signal(barrier, inc=1, device_id={"blk": lax.rem(blk + k, N_BLK)}, device_id_type=MESH)
    return barrier


class Sum:
    def __init__(self, leaf, blk, local, near, far, total, leaf_sems, blk_sems):
        size = local.shape[0] // N_LEAF
        self.blk = blk
        self.local, self.near, self.far, self.total = local, near, far, total
        mine = pl.ds(pl.multiple_of(leaf * size, 8), size)
        self.mine = mine
        self.spread, self.cross, self.collect = [], [], []
        for k in range(1, N_LEAF):
            peer = lax.rem(leaf + k, N_LEAF)
            self.spread.append(pltpu.make_async_remote_copy(
                src_ref=local.at[pl.ds(pl.multiple_of(peer * size, 8), size)], dst_ref=near.at[k],
                send_sem=leaf_sems.at[0, k], recv_sem=leaf_sems.at[1, k], device_id={"leaf": peer}, device_id_type=MESH))
            self.collect.append(pltpu.make_async_remote_copy(
                src_ref=total.at[mine], dst_ref=total.at[mine],
                send_sem=leaf_sems.at[2, k], recv_sem=leaf_sems.at[3, k], device_id={"leaf": peer}, device_id_type=MESH))
        for k in range(1, N_BLK):
            peer = lax.rem(blk + k, N_BLK)
            self.cross.append(pltpu.make_async_remote_copy(
                src_ref=far.at[blk], dst_ref=far.at[blk],
                send_sem=blk_sems.at[0, k], recv_sem=blk_sems.at[1, k], device_id={"blk": peer}, device_id_type=MESH))

    def begin(self, *parts):
        for n, part in enumerate(parts):
            self.local[128 * n : 128 * (n + 1), :] = part
        for copy in self.spread:
            copy.start()

    def across(self):
        part = self.local[self.mine, :]
        for k, copy in enumerate(self.spread):
            copy.wait_recv()
            part = part + self.near[k + 1]
        self.far[self.blk] = part
        for copy in self.cross:
            copy.start()

    def gather(self):
        for copy in self.cross:
            copy.wait_recv()
        part = self.far[0]
        for b in range(1, N_BLK):
            part = part + self.far[b]
        self.total[self.mine, :] = part
        for copy in self.collect:
            copy.start()

    def end(self):
        for copy in self.collect:
            copy.wait_recv()

    def drain(self):
        for copy in self.spread + self.cross + self.collect:
            copy.wait_send()


def sum_scratch(parts):
    size = 128 * parts // N_LEAF
    return [
        pltpu.VMEM((128 * parts, 128), F32),
        pltpu.VMEM((N_LEAF, size, 128), F32),
        pltpu.VMEM((N_BLK, size, 128), F32),
        pltpu.VMEM((128 * parts, 128), F32),
        pltpu.SemaphoreType.DMA((4, N_LEAF)),
        pltpu.SemaphoreType.DMA((2, N_BLK)),
    ]


SIDE = 128
BLOCK = 64


def factor_start(work, gram):
    work[:, 0:SIDE] = gram
    work[:, SIDE:] = (
        lax.broadcasted_iota(jnp.int32, (SIDE, SIDE), 0) == lax.broadcasted_iota(jnp.int32, (SIDE, SIDE), 1)
    ).astype(F32)


def factor(work, start):
    sub = lax.broadcasted_iota(jnp.int32, (8, 128), 0)
    if start:
        update = dot(work[0:start, start : start + BLOCK], work[0:start, :], 0, 0, HIGH)
        work[start : start + BLOCK, :] = work[start : start + BLOCK, :] - update
    count = BLOCK // 8
    tiles = 2
    x = [[work[start + 8 * t : start + 8 * t + 8, 128 * i : 128 * (i + 1)] for i in range(tiles)] for t in range(count)]
    for p in range(count):
        lane = start + 8 * p
        rest = range(p, count)
        col = [{t: jnp.broadcast_to(x[t][0][:, lane + j : lane + j + 1], (8, 128)) for t in rest} for j in range(8)]
        diagonal = [jnp.broadcast_to(col[k][p][k : k + 1, :], (8, 128)) for k in range(8)]
        for j in range(8):
            below = {k: jnp.broadcast_to(col[j][p][k : k + 1, :], (8, 128)) for k in range(j + 1, 8)}
            inverse = lax.rsqrt(diagonal[j])
            low = {t: col[j][t] * inverse for t in rest}
            for k in range(j + 1, 8):
                pivot = below[k] * inverse
                diagonal[k] = diagonal[k] - pivot * pivot
                for t in rest:
                    col[k][t] = col[k][t] - low[t] * pivot
            for i in range(tiles):
                row = jnp.broadcast_to(x[p][i][j : j + 1, :], (8, 128)) * inverse
                for t in rest:
                    moved = x[t][i] - low[t] * row
                    if t == p:
                        moved = jnp.where(sub > j, moved, jnp.where(sub == j, row, x[t][i]))
                    x[t][i] = moved
        for i in range(tiles):
            work[start + 8 * p : start + 8 * p + 8, 128 * i : 128 * (i + 1)] = x[p][i]


def factored(work):
    keep = lax.broadcasted_iota(jnp.int32, (SIDE, SIDE), 0) <= lax.broadcasted_iota(jnp.int32, (SIDE, SIDE), 1)
    return jnp.where(keep, work[:, 0:SIDE], 0.0), work[:, SIDE:]


def dot3(a, b, ca, cb):
    (ah, al), (bh, bl) = split2(a), split2(b)
    return dot(ah, bh, ca, cb) + (dot(ah, bl, ca, cb) + dot(al, bh, ca, cb))


TOTAL = N_LEAF * N_BLK
STEPS = (-1, 1)


class Exchange:
    def __init__(self, device, near, far, relay, near_to, far_to, sems):
        self.near_to, self.far_to = near_to, far_to
        self.direct, self.away, self.onward = [], [], []
        self.one, self.two, self.from_one, self.from_two = [], [], [], []
        self.between = (device >= 1) & (device < TOTAL - 1)
        for u, step in enumerate(STEPS):
            peer = lax.rem(device + step + TOTAL, TOTAL)
            there = (lax.div(peer, N_LEAF), lax.rem(peer, N_LEAF))

            def copy(kind, src, dst):
                return pltpu.make_async_remote_copy(
                    src_ref=src, dst_ref=dst, send_sem=sems.at[0, kind, u], recv_sem=sems.at[1, kind, u],
                    device_id=there, device_id_type=MESH)

            self.direct.append(copy(0, near[u], near_to[u]))
            self.away.append(copy(1, far[u], relay.at[u]))
            self.onward.append(copy(2, relay.at[u], far_to[u]))
            self.one.append(self.within(device + step))
            self.two.append(self.within(device + 2 * step))
            self.from_one.append(self.within(device - step))
            self.from_two.append(self.within(device - 2 * step))

    def within(self, device):
        return (device >= 0) & (device < TOTAL)

    def send_far(self):
        for u in range(2):
            pl.when(self.two[u])(self.away[u].start)

    def send_near(self):
        for u in range(2):
            pl.when(self.one[u])(self.direct[u].start)

    def forward(self):
        for u in range(2):
            @pl.when(self.between)
            def _():
                self.away[u].wait_recv()
                self.onward[u].start()

    def receive(self, arrives, copy, to):
        pl.when(arrives)(copy.wait_recv)

        @pl.when(jnp.logical_not(arrives))
        def _():
            to[...] = jnp.zeros(to.shape, F32)

    def receive_near(self):
        for u in range(2):
            self.receive(self.from_one[u], self.direct[u], self.near_to[u])

    def receive_far(self):
        for u in range(2):
            self.receive(self.from_two[u], self.onward[u], self.far_to[u])

    def drain(self):
        for u in range(2):
            pl.when(self.two[u])(self.away[u].wait_send)
            pl.when(self.one[u])(self.direct[u].wait_send)
            pl.when(self.between)(self.onward[u].wait_send)


STORED = (512, 256, 384, 640)
NEAR_OUT, FAR_OUT = (1, 2), (0, 3)
NEAR_BACK, FAR_BACK = (2, 1), (3, 0)


def main_kernel(scale, count, modes, stiffness, connect, send, bottom_out, low_out, rest_out, r_out, top_out, inv_out, q_out,
                outgoing, table, relay, acc, incoming, relay_back, halo_sems, back_sems,
                ext, pick, place, taken, blocks, matrix_hi, matrix_lo, product, stiff, work, *sums):
    leaf, blk = lax.axis_index("leaf"), lax.axis_index("blk")
    device = blk * N_LEAF + leaf
    barrier = greet(leaf, blk)

    def rows_of(ref, h, j):
        return ref.at[h, pl.ds(STORED[j], 128)]

    halo, back = [], []
    for h in range(2):
        halo.append(Exchange(
            device, [outgoing.at[h, j] for j in NEAR_OUT], [outgoing.at[h, j] for j in FAR_OUT], relay.at[h],
            [rows_of(table, h, j) for j in NEAR_OUT], [rows_of(table, h, j) for j in FAR_OUT], halo_sems.at[h]))
        back.append(Exchange(
            device, [rows_of(acc, h, j) for j in NEAR_BACK], [rows_of(acc, h, j) for j in FAR_BACK], relay_back.at[h],
            [incoming.at[h, j] for j in NEAR_BACK], [incoming.at[h, j] for j in FAR_BACK], back_sems.at[h]))
    greeted = N_LEAF + N_BLK - 2
    for u, step in enumerate(STEPS):
        peer = lax.rem(device + step + TOTAL, TOTAL)
        there = (lax.div(peer, N_LEAF), lax.rem(peer, N_LEAF))
        greeted = greeted + halo[0].from_one[u].astype(jnp.int32)

        @pl.when(halo[0].one[u])
        def _():
            pl.semaphore_signal(barrier, inc=1, device_id=there, device_id_type=MESH)

    first, cross, top, bottom = (Sum(leaf, blk, *sums[6 * i : 6 * i + 6]) for i in range(4))

    chosen = send[...]
    columns = columns_of(chosen, 4)
    nodes = lax.broadcasted_iota(jnp.int32, (128, 256), 1).astype(F32)
    choosers = [(columns[:, j : j + 1] == nodes).astype(BF16) for j in range(4)]

    wides = [jnp.concatenate([modes[c, :, 128 * h : 128 * (h + 1)] for c in range(3)], axis=1) for h in range(2)]
    parts = [split3(wide) for wide in wides]
    sent = [jnp.concatenate(part, axis=1) for part in parts]

    def prepare(h, directions):
        for j in directions:
            found = dot(choosers[j], sent[h], 1, 0)
            outgoing[h, j] = found[:, 0:384] + (found[:, 384:768] + found[:, 768:1152])

    prepare(0, FAR_OUT)
    pl.semaphore_wait(barrier, greeted)
    halo[0].send_far()
    prepare(0, NEAR_OUT)
    halo[0].send_near()
    gram = sum(dot3(modes[c].T, modes[c], 1, 0) for c in range(3))
    first.begin(gram[0:128, 0:128], gram[128:256, 0:128], gram[128:256, 128:256])
    prepare(1, FAR_OUT + NEAR_OUT)
    for h in range(2):
        table[h, 0:256, :] = wides[h]
        ext[h, 0:256, 0:384], ext[h, 0:256, 384:768] = parts[h][0], parts[h][1]

    conn = connect[...]
    columns = columns_of(conn, 10)

    def table_id(at):
        return jnp.where(at < 256, at, jnp.where(at < 512, at + 128, jnp.where(at < 640, at - 256, at)))

    lanes = table_id(lax.broadcasted_iota(jnp.int32, (128, 768), 1)).astype(F32)
    rows = table_id(lax.broadcasted_iota(jnp.int32, (768, 128), 0))
    for k in range(10):
        pick[128 * k : 128 * (k + 1), :] = (columns[:, k : k + 1] == lanes).astype(BF16)
        place[:, 128 * k : 128 * (k + 1)] = (rows == conn[k : k + 1, :]).astype(BF16)

    halo[0].forward()
    halo[1].send_far()
    halo[1].send_near()

    def gather(h, part):
        span = slice(256 * part, 256 * (part + 1))
        if part:
            ext[h, span, 0:384], ext[h, span, 384:768] = split2(table[h, span, :])

        def body(step, carry):
            at = pl.ds(pl.multiple_of(step * 320, 320), 320)
            picked = pick[at, span]
            found = dot(picked, ext[h, span, :], 1, 0)
            found = found[:, 0:384] + found[:, 384:768]
            taken[h, at, :] = found if part == 0 else taken[h, at, :] + found
            return carry

        lax.fori_loop(0, 4, body, 0)

    gather(0, 0)
    gather(1, 0)

    live = lax.broadcasted_iota(jnp.int32, (30, 128), 1) < count[0]
    source = lax.broadcasted_iota(jnp.int32, (30, 256), 0)
    target = lax.broadcasted_iota(jnp.int32, (30, 256), 1)
    wanted = lax.rem(source, 3) * 10 + lax.div(source, 3)
    spread = (lax.shift_right_logical(target, 3) == wanted).astype(BF16)
    for k in range(10):
        for c in range(3):
            block = jnp.concatenate([stiffness[k, c, l] for l in range(10)], axis=0)
            hi, lo = split2(jnp.where(live, block, 0.0))
            blocks[10 * c + k] = dot(hi, spread, 0, 0) + dot(lo, spread, 0, 0)

    keep = lax.broadcasted_iota(jnp.int32, (8, 256), 0) == lax.rem(lax.broadcasted_iota(jnp.int32, (8, 256), 1), 8)

    def assemble(g, carry):
        at = pl.ds(pl.multiple_of(g * 8, 8), 8)
        matrix = jnp.concatenate([jnp.where(keep, blocks[n, at, :], 0.0) for n in range(30)], axis=0)
        matrix_hi[g], matrix_lo[g] = split2(matrix)
        return carry

    lax.fori_loop(0, 16, assemble, 0)

    def multiply(h):
        def group(g, carry):
            spans = [pl.ds(pl.multiple_of(128 * k + g * 8, 8), 8) for k in range(10)]
            vectors = jnp.concatenate(
                [taken[h, spans[l], 128 * d : 128 * (d + 1)] for d in range(3) for l in range(10)]
                + [jnp.zeros((16, 128), F32)],
                axis=0,
            )
            v_hi, v_lo = split2(vectors)
            m_hi, m_lo = matrix_hi[g], matrix_lo[g]
            result = dot(m_hi, jnp.concatenate([v_hi, v_lo], axis=1), 1, 0)
            result = result[:, 0:128] + (result[:, 128:256] + dot(m_lo, v_hi, 1, 0))
            for c in range(3):
                for k in range(10):
                    n = 10 * c + k
                    product[spans[k], 128 * c : 128 * (c + 1)] = result[8 * n : 8 * n + 8, :]
            return carry

        lax.fori_loop(0, 16, group, 0, unroll=4)
        return jnp.concatenate(split2(product[...]), axis=1)

    def scatter(h, halves, span):
        where = place[span, :]
        found = dot(where, halves, 1, 0)
        acc[h, span, :] = found[:, 0:384] + found[:, 384:768]

    OWN, NEAR, FAR = slice(0, 256), slice(256, 512), slice(512, 768)

    halo[0].receive_near()
    gather(0, 1)
    halo[0].receive_far()
    gather(0, 2)
    halves = multiply(0)
    halo[1].forward()
    scatter(0, halves, FAR)
    back[0].send_far()
    scatter(0, halves, NEAR)
    back[0].send_near()
    first.across()
    scatter(0, halves, OWN)
    halo[1].receive_near()
    gather(1, 1)
    halo[1].receive_far()
    gather(1, 2)
    first.gather()
    halves = multiply(1)
    back[0].forward()
    scatter(1, halves, FAR)
    back[1].send_far()
    scatter(1, halves, NEAR)
    back[1].send_near()
    scatter(1, halves, OWN)

    lower, diagonal = [], 0.0
    for c in range(3):
        at = slice(128 * c, 128 * (c + 1))
        low_at = slice(384 + 128 * c, 512 + 128 * c)
        tables = [jnp.concatenate([ext[0, :, lanes], ext[1, :, lanes]], axis=1) for lanes in (at, low_at)]
        for h in range(2):
            hi, lo = split2(acc[h, :, at].T)
            t_hi, t_lo = (t if h else t[:, 0:128] for t in tables)
            found = dot(hi, t_hi, 1, 0) + (dot(hi, t_lo, 1, 0) + dot(lo, t_hi, 1, 0))
            if h:
                lower.append(found)
            else:
                diagonal = diagonal + found
    lower = sum(lower)
    cross.begin(diagonal, lower[:, 0:128], lower[:, 128:256])

    rows = lax.broadcasted_iota(jnp.int32, (256, 128), 0)
    to_own = jnp.concatenate([(rows == chosen[j : j + 1, :]).astype(BF16) for j in range(4)], axis=1)

    def complete(h):
        back[h].receive_near()
        back[h].receive_far()
        parts = split2(jnp.concatenate([incoming[h, j] for j in range(4)], axis=0))
        found = dot(to_own, jnp.concatenate(parts, axis=1), 1, 0)
        whole = acc[h, OWN, :] + (found[:, 0:384] + found[:, 384:768])
        for c in range(3):
            stiff[c, :, 128 * h : 128 * (h + 1)] = whole[:, 128 * c : 128 * (c + 1)]

    first.end()
    factor_start(work, first.total[0:128, :])
    factor(work, 0)
    back[1].forward()
    factor(work, 64)
    r00, i00 = factored(work)
    complete(0)
    top.begin(sum(dot3(stiff[c, :, 0:128].T, stiff[c, :, 0:128], 1, 0) for c in range(3)))
    r01 = dot(i00, first.total[128:256, :], 1, 1, HIGH)
    factor_start(work, first.total[256:384, :] - dot(r01, r01, 0, 0, HIGH))
    factor(work, 0)
    factor(work, 64)
    r11, i11 = factored(work)
    r_out[0:128, 0:128], r_out[0:128, 128:256] = r00, r01
    r_out[128:256, 0:128], r_out[128:256, 128:256] = jnp.zeros((SIDE, SIDE), F32), r11
    i10 = dot(i11, dot(r01, i00, 0, 0, HIGH), 1, 0, HIGH)
    inv = jnp.concatenate(
        [jnp.concatenate([i00, jnp.zeros((SIDE, SIDE), F32)], axis=1), jnp.concatenate([-i10, i11], axis=1)], axis=0)
    cross.across()
    for c in range(3):
        q_out[c, :, 0:256] = dot3(modes[c], inv, 1, 1) * scale

    cross.gather()
    complete(1)
    both = sum(dot3(stiff[c, :, 128:256].T, stiff[c], 1, 0) for c in range(3))
    bottom.begin(both[:, 0:128], both[:, 128:256])
    top.across()
    cross.end()
    crossed = cross.total
    gram = jnp.concatenate(
        [jnp.concatenate([crossed[0:128, :], crossed[128:256, :].T], axis=1),
         jnp.concatenate([crossed[128:256, :], crossed[256:384, :]], axis=1)], axis=0)
    low = dot(gram, inv, 1, 1, HIGH)
    low_out[...] = low
    top.gather()
    for c in range(3):
        stiff[c] = stiff[c] - dot3(q_out[c, :, 0:256], low / scale, 1, 1)
    bottom.across()
    top.end()
    factor_start(work, top.total[...] - dot(low[0:128, :], low[0:128, :], 1, 1, HIGH))
    factor(work, 0)
    bottom.gather()
    factor(work, 64)
    r22, i22 = factored(work)
    top_out[...] = r22
    inv_out[...] = i22
    for c in range(3):
        q_out[c, :, 256:384] = dot3(stiff[c, :, 0:128], i22, 1, 1) * scale
        rest_out[c] = stiff[c, :, 128:256]
    for h in range(2):
        halo[h].drain()
        back[h].drain()
    first.drain()
    cross.drain()
    top.drain()
    bottom.end()
    bottom.drain()
    bottom_out[...] = bottom.total[...]


def up_to_last_gram(scale, count, modes, stiffness, connect, send):
    shapes = ((256, 128), (256, 256), (3, 256, 128), (256, 256), (128, 128), (128, 128), (3, 256, 384))
    rows = pltpu.VMEM((2, 4, 128, 384), F32)
    table = pltpu.VMEM((2, 768, 384), F32)
    relay = pltpu.VMEM((2, 2, 128, 384), F32)
    sems = pltpu.SemaphoreType.DMA((2, 2, 3, 2))
    return pl.pallas_call(
        functools.partial(main_kernel, scale),
        out_shape=[jax.ShapeDtypeStruct(shape, F32) for shape in shapes],
        in_specs=[SMEM] + [VMEM] * 4,
        out_specs=[VMEM] * len(shapes),
        scratch_shapes=[
            rows, table, relay, table, rows, relay, sems, sems,
            pltpu.VMEM((2, 768, 768), BF16),
            pltpu.VMEM((1280, 768), BF16),
            pltpu.VMEM((768, 1280), BF16),
            pltpu.VMEM((2, 1280, 384), F32),
            pltpu.VMEM((30, 128, 256), F32),
            pltpu.VMEM((16, 240, 256), BF16),
            pltpu.VMEM((16, 240, 256), BF16),
            pltpu.VMEM((1280, 384), F32),
            pltpu.VMEM((3, 256, 256), F32),
            pltpu.VMEM((SIDE, 2 * SIDE), F32),
        ] + sum_scratch(3) + sum_scratch(3) + sum_scratch(1) + sum_scratch(2),
        compiler_params=pltpu.CompilerParams(collective_id=1, has_side_effects=True, vmem_limit_bytes=LIMIT),
        name="up_to_last_gram",
    )(count, modes, stiffness, connect, send)


def second_kernel(scale, bottom, low, r_first, r_top, i_top, rest, q_in, q_out, r_out, work, columns, last, sems):
    fetch = pltpu.make_async_copy(q_in, columns, sems.at[0])
    done = pltpu.make_async_copy(columns, q_out.at[:, :, pl.ds(0, 384)], sems.at[1])
    fetch.start()
    low0, low1 = low[0:128, :], low[128:256, :]
    side = bottom[0:128, :] - dot(low1, low0, 1, 1, HIGH)
    r01 = dot(i_top[...], side, 1, 1, HIGH)
    factor_start(work, bottom[128:256, :] - dot(low1, low1, 1, 1, HIGH) - dot(r01, r01, 0, 0, HIGH))
    factor(work, 0)
    fetch.wait()
    done.start()
    r_out[0:256, 0:256] = r_first[...] / scale
    r_out[0:256, 256:512] = low[...].T / scale
    r_out[256:512, 0:256] = jnp.zeros((256, 256), F32)
    r_out[256:384, 256:384] = r_top[...] / scale
    r_out[256:384, 384:512] = r01 / scale
    r_out[384:512, 256:384] = jnp.zeros((128, 128), F32)
    factor(work, 64)
    r11, i11 = factored(work)
    r_out[384:512, 384:512] = r11 / scale
    for c in range(3):
        left = rest[c] - dot3(columns[c, :, 256:384], r01 / scale, 1, 0)
        last[c] = dot3(left, i11, 1, 1) * scale
    place = pltpu.make_async_copy(last, q_out.at[:, :, pl.ds(384, 128)], sems.at[2])
    place.start()
    place.wait()
    done.wait()


def second(scale, *operands):
    anywhere = pl.BlockSpec(memory_space=pl.ANY)
    return pl.pallas_call(
        functools.partial(second_kernel, scale),
        out_shape=[jax.ShapeDtypeStruct((3, 256, 512), F32), jax.ShapeDtypeStruct((512, 512), F32)],
        in_specs=[VMEM] * 6 + [anywhere],
        out_specs=[anywhere, VMEM],
        scratch_shapes=[
            pltpu.VMEM((SIDE, 2 * SIDE), F32),
            pltpu.VMEM((3, 256, 384), F32),
            pltpu.VMEM((3, 256, 128), F32),
            pltpu.SemaphoreType.DMA((3,)),
        ],
        compiler_params=pltpu.CompilerParams(vmem_limit_bytes=LIMIT),
        name="second_factor",
    )(*operands)


def shards(modes, stiffness, connect, send_list, elem_count):
    modes = jnp.transpose(modes, (1, 0, 2))
    scale = float((3 * 256 * lax.axis_size("blk") * lax.axis_size("leaf")) ** 0.5)
    bottom, low, rest, r_first, r_top, i_top, q = up_to_last_gram(
        scale, elem_count, modes, stiffness, connect, send_list[0])
    q, r = second(scale, bottom, low, r_first, r_top, i_top, rest, q)
    return (jnp.transpose(q, (1, 0, 2)), r)


def solution(mesh):
    placed = (
        P(("blk", "leaf"), None, None),
        P(None, None, None, None, ("blk", "leaf")),
        P(None, ("blk", "leaf")),
        P(("blk", "leaf"), None, None),
        P(("blk", "leaf")),
    )
    return jax.shard_map(
        shards,
        mesh=mesh,
        in_specs=placed,
        out_specs=(P(("blk", "leaf"), None, None), P()),
        check_vma=False,
    )
```

```python
import functools

import jax
import jax.numpy as jnp
from jax import lax
from jax.experimental import pallas as pl
from jax.experimental.pallas import tpu as pltpu
from jax.sharding import PartitionSpec as P

HIGH = lax.Precision.HIGHEST
F32 = jnp.float32
BF16 = jnp.bfloat16
MESH = pl.DeviceIdType.MESH
VMEM = pl.BlockSpec(memory_space=pltpu.VMEM)
SMEM = pl.BlockSpec(memory_space=pltpu.SMEM)
LIMIT = 56 * 1024 * 1024


def dot(a, b, ca, cb, precision=None):
    return lax.dot_general(a, b, (((ca,), (cb,)), ((), ())), precision=precision, preferred_element_type=F32)


def split2(x):
    hi = x.astype(BF16)
    return hi, (x - hi.astype(F32)).astype(BF16)


def split3(x):
    hi = x.astype(BF16)
    rest = x - hi.astype(F32)
    mid = rest.astype(BF16)
    return hi, mid, (rest - mid.astype(F32)).astype(BF16)


def columns_of(rows, count):
    padded = jnp.concatenate([rows.astype(F32), jnp.zeros((16 - count, 128), F32)], axis=0)
    return padded.T


N_LEAF = 16
N_BLK = 8


def greet(leaf, blk):
    barrier = pltpu.get_barrier_semaphore()
    for k in range(1, N_LEAF):
        pl.semaphore_signal(barrier, inc=1, device_id={"leaf": lax.rem(leaf + k, N_LEAF)}, device_id_type=MESH)
    for k in range(1, N_BLK):
        pl.semaphore_signal(barrier, inc=1, device_id={"blk": lax.rem(blk + k, N_BLK)}, device_id_type=MESH)
    return barrier


class Sum:
    def __init__(self, leaf, blk, local, near, far, total, leaf_sems, blk_sems):
        size = local.shape[0] // N_LEAF
        self.blk = blk
        self.local, self.near, self.far, self.total = local, near, far, total
        mine = pl.ds(pl.multiple_of(leaf * size, 8), size)
        self.mine = mine
        self.spread, self.cross, self.collect = [], [], []
        for k in range(1, N_LEAF):
            peer = lax.rem(leaf + k, N_LEAF)
            self.spread.append(pltpu.make_async_remote_copy(
                src_ref=local.at[pl.ds(pl.multiple_of(peer * size, 8), size)], dst_ref=near.at[k],
                send_sem=leaf_sems.at[0, k], recv_sem=leaf_sems.at[1, k], device_id={"leaf": peer}, device_id_type=MESH))
            self.collect.append(pltpu.make_async_remote_copy(
                src_ref=total.at[mine], dst_ref=total.at[mine],
                send_sem=leaf_sems.at[2, k], recv_sem=leaf_sems.at[3, k], device_id={"leaf": peer}, device_id_type=MESH))
        for k in range(1, N_BLK):
            peer = lax.rem(blk + k, N_BLK)
            self.cross.append(pltpu.make_async_remote_copy(
                src_ref=far.at[blk], dst_ref=far.at[blk],
                send_sem=blk_sems.at[0, k], recv_sem=blk_sems.at[1, k], device_id={"blk": peer}, device_id_type=MESH))

    def begin(self, *parts):
        for n, part in enumerate(parts):
            self.local[128 * n : 128 * (n + 1), :] = part
        for copy in self.spread:
            copy.start()

    def across(self):
        part = self.local[self.mine, :]
        for k, copy in enumerate(self.spread):
            copy.wait_recv()
            part = part + self.near[k + 1]
        self.far[self.blk] = part
        for copy in self.cross:
            copy.start()

    def gather(self):
        for copy in self.cross:
            copy.wait_recv()
        part = self.far[0]
        for b in range(1, N_BLK):
            part = part + self.far[b]
        self.total[self.mine, :] = part
        for copy in self.collect:
            copy.start()

    def end(self):
        for copy in self.collect:
            copy.wait_recv()

    def drain(self):
        for copy in self.spread + self.cross + self.collect:
            copy.wait_send()


def sum_scratch(parts):
    size = 128 * parts // N_LEAF
    return [
        pltpu.VMEM((128 * parts, 128), F32),
        pltpu.VMEM((N_LEAF, size, 128), F32),
        pltpu.VMEM((N_BLK, size, 128), F32),
        pltpu.VMEM((128 * parts, 128), F32),
        pltpu.SemaphoreType.DMA((4, N_LEAF)),
        pltpu.SemaphoreType.DMA((2, N_BLK)),
    ]


SIDE = 128
BLOCK = 32


def factor_start(work, gram):
    work[:, 0:SIDE] = gram
    work[:, SIDE:] = (
        lax.broadcasted_iota(jnp.int32, (SIDE, SIDE), 0) == lax.broadcasted_iota(jnp.int32, (SIDE, SIDE), 1)
    ).astype(F32)


def factor(work, start):
    sub = lax.broadcasted_iota(jnp.int32, (8, 128), 0)
    if start:
        update = dot(work[0:start, start : start + BLOCK], work[0:start, :], 0, 0, HIGH)
        work[start : start + BLOCK, :] = work[start : start + BLOCK, :] - update
    count = BLOCK // 8
    tiles = 2
    x = [[work[start + 8 * t : start + 8 * t + 8, 128 * i : 128 * (i + 1)] for i in range(tiles)] for t in range(count)]
    for p in range(count):
        lane = start + 8 * p
        rest = range(p, count)
        col = [{t: jnp.broadcast_to(x[t][0][:, lane + j : lane + j + 1], (8, 128)) for t in rest} for j in range(8)]
        for j in range(8):
            inverse = lax.rsqrt(jnp.broadcast_to(col[j][p][j : j + 1, :], (8, 128)))
            low = {t: col[j][t] * inverse for t in rest}
            for k in range(j + 1, 8):
                pivot = jnp.broadcast_to(low[p][k : k + 1, :], (8, 128))
                for t in rest:
                    col[k][t] = col[k][t] - low[t] * pivot
            for i in range(tiles):
                row = jnp.broadcast_to(x[p][i][j : j + 1, :], (8, 128)) * inverse
                for t in rest:
                    moved = x[t][i] - low[t] * row
                    if t == p:
                        moved = jnp.where(sub > j, moved, jnp.where(sub == j, row, x[t][i]))
                    x[t][i] = moved
        for i in range(tiles):
            work[start + 8 * p : start + 8 * p + 8, 128 * i : 128 * (i + 1)] = x[p][i]


def factor_half(work, half):
    for start in range(64 * half, 64 * half + 64, BLOCK):
        factor(work, start)


def factored(work):
    keep = lax.broadcasted_iota(jnp.int32, (SIDE, SIDE), 0) <= lax.broadcasted_iota(jnp.int32, (SIDE, SIDE), 1)
    return jnp.where(keep, work[:, 0:SIDE], 0.0), work[:, SIDE:]


def dot3(a, b, ca, cb):
    (ah, al), (bh, bl) = split2(a), split2(b)
    return dot(ah, bh, ca, cb) + (dot(ah, bl, ca, cb) + dot(al, bh, ca, cb))


TOTAL = N_LEAF * N_BLK
STEPS = (-1, 1)


class Exchange:
    def __init__(self, device, near, far, relay, near_to, far_to, sems):
        self.near_to, self.far_to = near_to, far_to
        self.direct, self.away, self.onward = [], [], []
        self.one, self.two, self.from_one, self.from_two = [], [], [], []
        self.between = (device >= 1) & (device < TOTAL - 1)
        for u, step in enumerate(STEPS):
            peer = lax.rem(device + step + TOTAL, TOTAL)
            there = (lax.div(peer, N_LEAF), lax.rem(peer, N_LEAF))

            def copy(kind, src, dst):
                return pltpu.make_async_remote_copy(
                    src_ref=src, dst_ref=dst, send_sem=sems.at[0, kind, u], recv_sem=sems.at[1, kind, u],
                    device_id=there, device_id_type=MESH)

            self.direct.append(copy(0, near[u], near_to[u]))
            self.away.append(copy(1, far[u], relay.at[u]))
            self.onward.append(copy(2, relay.at[u], far_to[u]))
            self.one.append(self.within(device + step))
            self.two.append(self.within(device + 2 * step))
            self.from_one.append(self.within(device - step))
            self.from_two.append(self.within(device - 2 * step))

    def within(self, device):
        return (device >= 0) & (device < TOTAL)

    def send_far(self):
        for u in range(2):
            pl.when(self.two[u])(self.away[u].start)

    def send_near(self):
        for u in range(2):
            pl.when(self.one[u])(self.direct[u].start)

    def forward(self):
        for u in range(2):
            @pl.when(self.between)
            def _():
                self.away[u].wait_recv()
                self.onward[u].start()

    def receive(self, arrives, copy, to):
        pl.when(arrives)(copy.wait_recv)

        @pl.when(jnp.logical_not(arrives))
        def _():
            to[...] = jnp.zeros(to.shape, F32)

    def receive_near(self):
        for u in range(2):
            self.receive(self.from_one[u], self.direct[u], self.near_to[u])

    def receive_far(self):
        for u in range(2):
            self.receive(self.from_two[u], self.onward[u], self.far_to[u])

    def drain(self):
        for u in range(2):
            pl.when(self.two[u])(self.away[u].wait_send)
            pl.when(self.one[u])(self.direct[u].wait_send)
            pl.when(self.between)(self.onward[u].wait_send)


STORED = (512, 256, 384, 640)
NEAR_OUT, FAR_OUT = (1, 2), (0, 3)
NEAR_BACK, FAR_BACK = (2, 1), (3, 0)


def main_kernel(scale, count, modes, stiffness, connect, send, bottom_out, low_out, rest_out, r_out, top_out, inv_out, q_out,
                outgoing, table, relay, acc, incoming, relay_back, halo_sems, back_sems,
                ext, pick, place, taken, blocks, matrix_hi, matrix_lo, product, stiff, work, *sums):
    leaf, blk = lax.axis_index("leaf"), lax.axis_index("blk")
    device = blk * N_LEAF + leaf
    barrier = greet(leaf, blk)

    def rows_of(ref, h, j):
        return ref.at[h, pl.ds(STORED[j], 128)]

    halo, back = [], []
    for h in range(2):
        halo.append(Exchange(
            device, [outgoing.at[h, j] for j in NEAR_OUT], [outgoing.at[h, j] for j in FAR_OUT], relay.at[h],
            [rows_of(table, h, j) for j in NEAR_OUT], [rows_of(table, h, j) for j in FAR_OUT], halo_sems.at[h]))
        back.append(Exchange(
            device, [rows_of(acc, h, j) for j in NEAR_BACK], [rows_of(acc, h, j) for j in FAR_BACK], relay_back.at[h],
            [incoming.at[h, j] for j in NEAR_BACK], [incoming.at[h, j] for j in FAR_BACK], back_sems.at[h]))
    greeted = N_LEAF + N_BLK - 2
    for u, step in enumerate(STEPS):
        peer = lax.rem(device + step + TOTAL, TOTAL)
        there = (lax.div(peer, N_LEAF), lax.rem(peer, N_LEAF))
        greeted = greeted + halo[0].from_one[u].astype(jnp.int32)

        @pl.when(halo[0].one[u])
        def _():
            pl.semaphore_signal(barrier, inc=1, device_id=there, device_id_type=MESH)

    first, cross, top, bottom = (Sum(leaf, blk, *sums[6 * i : 6 * i + 6]) for i in range(4))

    chosen = send[...]
    columns = columns_of(chosen, 4)
    nodes = lax.broadcasted_iota(jnp.int32, (128, 256), 1).astype(F32)
    choosers = [(columns[:, j : j + 1] == nodes).astype(BF16) for j in range(4)]

    wides = [jnp.concatenate([modes[c, :, 128 * h : 128 * (h + 1)] for c in range(3)], axis=1) for h in range(2)]
    parts = [split3(wide) for wide in wides]
    sent = [jnp.concatenate(part, axis=1) for part in parts]

    def prepare(h, directions):
        for j in directions:
            found = dot(choosers[j], sent[h], 1, 0)
            outgoing[h, j] = found[:, 0:384] + (found[:, 384:768] + found[:, 768:1152])

    prepare(0, FAR_OUT)
    pl.semaphore_wait(barrier, greeted)
    halo[0].send_far()
    prepare(0, NEAR_OUT)
    halo[0].send_near()
    gram = sum(dot3(modes[c].T, modes[c], 1, 0) for c in range(3))
    first.begin(gram[0:128, 0:128], gram[128:256, 0:128], gram[128:256, 128:256])
    prepare(1, FAR_OUT + NEAR_OUT)
    for h in range(2):
        table[h, 0:256, :] = wides[h]
        ext[h, 0:256, 0:384], ext[h, 0:256, 384:768] = parts[h][0], parts[h][1]

    conn = connect[...]
    columns = columns_of(conn, 10)

    def table_id(at):
        return jnp.where(at < 256, at, jnp.where(at < 512, at + 128, jnp.where(at < 640, at - 256, at)))

    lanes = table_id(lax.broadcasted_iota(jnp.int32, (128, 768), 1)).astype(F32)
    rows = table_id(lax.broadcasted_iota(jnp.int32, (768, 128), 0))
    for k in range(10):
        pick[128 * k : 128 * (k + 1), :] = (columns[:, k : k + 1] == lanes).astype(BF16)
        place[:, 128 * k : 128 * (k + 1)] = (rows == conn[k : k + 1, :]).astype(BF16)

    halo[0].forward()
    halo[1].send_far()
    halo[1].send_near()

    def gather(h, part):
        span = slice(256 * part, 256 * (part + 1))
        if part:
            ext[h, span, 0:384], ext[h, span, 384:768] = split2(table[h, span, :])

        def body(step, carry):
            at = pl.ds(pl.multiple_of(step * 320, 320), 320)
            picked = pick[at, span]
            found = dot(picked, ext[h, span, :], 1, 0)
            found = found[:, 0:384] + found[:, 384:768]
            taken[h, at, :] = found if part == 0 else taken[h, at, :] + found
            return carry

        lax.fori_loop(0, 4, body, 0)

    gather(0, 0)
    gather(1, 0)

    live = lax.broadcasted_iota(jnp.int32, (30, 128), 1) < count[0]
    source = lax.broadcasted_iota(jnp.int32, (30, 256), 0)
    target = lax.broadcasted_iota(jnp.int32, (30, 256), 1)
    wanted = lax.rem(source, 3) * 10 + lax.div(source, 3)
    spread = (lax.shift_right_logical(target, 3) == wanted).astype(BF16)
    for k in range(10):
        for c in range(3):
            block = jnp.concatenate([stiffness[k, c, l] for l in range(10)], axis=0)
            hi, lo = split2(jnp.where(live, block, 0.0))
            blocks[10 * c + k] = dot(hi, spread, 0, 0) + dot(lo, spread, 0, 0)

    keep = lax.broadcasted_iota(jnp.int32, (8, 256), 0) == lax.rem(lax.broadcasted_iota(jnp.int32, (8, 256), 1), 8)

    def assemble(g, carry):
        at = pl.ds(pl.multiple_of(g * 8, 8), 8)
        matrix = jnp.concatenate([jnp.where(keep, blocks[n, at, :], 0.0) for n in range(30)], axis=0)
        matrix_hi[g], matrix_lo[g] = split2(matrix)
        return carry

    lax.fori_loop(0, 16, assemble, 0)

    def multiply(h):
        def group(g, carry):
            spans = [pl.ds(pl.multiple_of(128 * k + g * 8, 8), 8) for k in range(10)]
            vectors = jnp.concatenate(
                [taken[h, spans[l], 128 * d : 128 * (d + 1)] for d in range(3) for l in range(10)]
                + [jnp.zeros((16, 128), F32)],
                axis=0,
            )
            v_hi, v_lo = split2(vectors)
            m_hi, m_lo = matrix_hi[g], matrix_lo[g]
            result = dot(m_hi, jnp.concatenate([v_hi, v_lo], axis=1), 1, 0)
            result = result[:, 0:128] + (result[:, 128:256] + dot(m_lo, v_hi, 1, 0))
            for c in range(3):
                for k in range(10):
                    n = 10 * c + k
                    product[spans[k], 128 * c : 128 * (c + 1)] = result[8 * n : 8 * n + 8, :]
            return carry

        lax.fori_loop(0, 16, group, 0, unroll=4)
        return jnp.concatenate(split2(product[...]), axis=1)

    def scatter(h, halves, span):
        where = place[span, :]
        found = dot(where, halves, 1, 0)
        acc[h, span, :] = found[:, 0:384] + found[:, 384:768]

    OWN, NEAR, FAR = slice(0, 256), slice(256, 512), slice(512, 768)

    halo[0].receive_near()
    gather(0, 1)
    halo[0].receive_far()
    gather(0, 2)
    halves = multiply(0)
    halo[1].forward()
    scatter(0, halves, FAR)
    back[0].send_far()
    scatter(0, halves, NEAR)
    back[0].send_near()
    first.across()
    scatter(0, halves, OWN)
    halo[1].receive_near()
    gather(1, 1)
    halo[1].receive_far()
    gather(1, 2)
    first.gather()
    halves = multiply(1)
    back[0].forward()
    scatter(1, halves, FAR)
    back[1].send_far()
    scatter(1, halves, NEAR)
    back[1].send_near()
    scatter(1, halves, OWN)

    lower, diagonal = [], 0.0
    for c in range(3):
        at = slice(128 * c, 128 * (c + 1))
        low_at = slice(384 + 128 * c, 512 + 128 * c)
        tables = [jnp.concatenate([ext[0, :, lanes], ext[1, :, lanes]], axis=1) for lanes in (at, low_at)]
        for h in range(2):
            hi, lo = split2(acc[h, :, at].T)
            t_hi, t_lo = (t if h else t[:, 0:128] for t in tables)
            found = dot(hi, t_hi, 1, 0) + (dot(hi, t_lo, 1, 0) + dot(lo, t_hi, 1, 0))
            if h:
                lower.append(found)
            else:
                diagonal = diagonal + found
    lower = sum(lower)
    cross.begin(diagonal, lower[:, 0:128], lower[:, 128:256])

    rows = lax.broadcasted_iota(jnp.int32, (256, 128), 0)
    to_own = jnp.concatenate([(rows == chosen[j : j + 1, :]).astype(BF16) for j in range(4)], axis=1)

    def complete(h):
        back[h].receive_near()
        back[h].receive_far()
        parts = split2(jnp.concatenate([incoming[h, j] for j in range(4)], axis=0))
        found = dot(to_own, jnp.concatenate(parts, axis=1), 1, 0)
        whole = acc[h, OWN, :] + (found[:, 0:384] + found[:, 384:768])
        for c in range(3):
            stiff[c, :, 128 * h : 128 * (h + 1)] = whole[:, 128 * c : 128 * (c + 1)]

    first.end()
    factor_start(work, first.total[0:128, :])
    factor_half(work, 0)
    back[1].forward()
    factor_half(work, 1)
    r00, i00 = factored(work)
    complete(0)
    top.begin(sum(dot3(stiff[c, :, 0:128].T, stiff[c, :, 0:128], 1, 0) for c in range(3)))
    r01 = dot3(i00, first.total[128:256, :], 1, 1)
    factor_start(work, first.total[256:384, :] - dot(r01, r01, 0, 0, HIGH))
    factor_half(work, 0)
    factor_half(work, 1)
    r11, i11 = factored(work)
    r_out[0:128, 0:128], r_out[0:128, 128:256] = r00, r01
    r_out[128:256, 0:128], r_out[128:256, 128:256] = jnp.zeros((SIDE, SIDE), F32), r11
    i10 = dot3(i11, dot3(r01.T, i00, 1, 0), 1, 0)
    inv = jnp.concatenate(
        [jnp.concatenate([i00, jnp.zeros((SIDE, SIDE), F32)], axis=1), jnp.concatenate([-i10, i11], axis=1)], axis=0)
    cross.across()
    for c in range(3):
        q_out[c, :, 0:256] = dot3(modes[c], inv, 1, 1) * scale

    cross.gather()
    complete(1)
    both = sum(dot3(stiff[c, :, 128:256].T, stiff[c], 1, 0) for c in range(3))
    bottom.begin(both[:, 0:128], both[:, 128:256])
    top.across()
    cross.end()
    crossed = cross.total
    gram = jnp.concatenate(
        [jnp.concatenate([crossed[0:128, :], crossed[128:256, :].T], axis=1),
         jnp.concatenate([crossed[128:256, :], crossed[256:384, :]], axis=1)], axis=0)
    low = dot3(gram, inv, 1, 1)
    low_out[...] = low
    top.gather()
    for c in range(3):
        stiff[c] = stiff[c] - dot3(q_out[c, :, 0:256], low / scale, 1, 1)
    bottom.across()
    top.end()
    factor_start(work, top.total[...] - dot(low[0:128, :], low[0:128, :], 1, 1, HIGH))
    factor_half(work, 0)
    bottom.gather()
    factor_half(work, 1)
    r22, i22 = factored(work)
    top_out[...] = r22
    inv_out[...] = i22
    for c in range(3):
        q_out[c, :, 256:384] = dot3(stiff[c, :, 0:128], i22, 1, 1) * scale
        rest_out[c] = stiff[c, :, 128:256]
    for h in range(2):
        halo[h].drain()
        back[h].drain()
    first.drain()
    cross.drain()
    top.drain()
    bottom.end()
    bottom.drain()
    bottom_out[...] = bottom.total[...]


def up_to_last_gram(scale, count, modes, stiffness, connect, send):
    shapes = ((256, 128), (256, 256), (3, 256, 128), (256, 256), (128, 128), (128, 128), (3, 256, 384))
    rows = pltpu.VMEM((2, 4, 128, 384), F32)
    table = pltpu.VMEM((2, 768, 384), F32)
    relay = pltpu.VMEM((2, 2, 128, 384), F32)
    sems = pltpu.SemaphoreType.DMA((2, 2, 3, 2))
    return pl.pallas_call(
        functools.partial(main_kernel, scale),
        out_shape=[jax.ShapeDtypeStruct(shape, F32) for shape in shapes],
        in_specs=[SMEM] + [VMEM] * 4,
        out_specs=[VMEM] * len(shapes),
        scratch_shapes=[
            rows, table, relay, table, rows, relay, sems, sems,
            pltpu.VMEM((2, 768, 768), BF16),
            pltpu.VMEM((1280, 768), BF16),
            pltpu.VMEM((768, 1280), BF16),
            pltpu.VMEM((2, 1280, 384), F32),
            pltpu.VMEM((30, 128, 256), F32),
            pltpu.VMEM((16, 240, 256), BF16),
            pltpu.VMEM((16, 240, 256), BF16),
            pltpu.VMEM((1280, 384), F32),
            pltpu.VMEM((3, 256, 256), F32),
            pltpu.VMEM((SIDE, 2 * SIDE), F32),
        ] + sum_scratch(3) + sum_scratch(3) + sum_scratch(1) + sum_scratch(2),
        compiler_params=pltpu.CompilerParams(collective_id=1, has_side_effects=True, vmem_limit_bytes=LIMIT),
        name="up_to_last_gram",
    )(count, modes, stiffness, connect, send)


def second_kernel(scale, bottom, low, r_first, r_top, i_top, rest, q_in, q_out, r_out, work, columns, last, sems):
    fetch = pltpu.make_async_copy(q_in, columns, sems.at[0])
    done = pltpu.make_async_copy(columns, q_out.at[:, :, pl.ds(0, 384)], sems.at[1])
    fetch.start()
    low0, low1 = low[0:128, :], low[128:256, :]
    side = bottom[0:128, :] - dot3(low1, low0, 1, 1)
    r01 = dot3(i_top[...], side, 1, 1)
    factor_start(work, bottom[128:256, :] - dot(low1, low1, 1, 1, HIGH) - dot(r01, r01, 0, 0, HIGH))
    factor_half(work, 0)
    fetch.wait()
    done.start()
    r_out[0:256, 0:256] = r_first[...] / scale
    r_out[0:256, 256:512] = low[...].T / scale
    r_out[256:512, 0:256] = jnp.zeros((256, 256), F32)
    r_out[256:384, 256:384] = r_top[...] / scale
    r_out[256:384, 384:512] = r01 / scale
    r_out[384:512, 256:384] = jnp.zeros((128, 128), F32)
    factor_half(work, 1)
    r11, i11 = factored(work)
    r_out[384:512, 384:512] = r11 / scale
    for c in range(3):
        left = rest[c] - dot3(columns[c, :, 256:384], r01 / scale, 1, 0)
        last[c] = dot3(left, i11, 1, 1) * scale
    place = pltpu.make_async_copy(last, q_out.at[:, :, pl.ds(384, 128)], sems.at[2])
    place.start()
    place.wait()
    done.wait()


def second(scale, *operands):
    anywhere = pl.BlockSpec(memory_space=pl.ANY)
    return pl.pallas_call(
        functools.partial(second_kernel, scale),
        out_shape=[jax.ShapeDtypeStruct((3, 256, 512), F32), jax.ShapeDtypeStruct((512, 512), F32)],
        in_specs=[VMEM] * 6 + [anywhere],
        out_specs=[anywhere, VMEM],
        scratch_shapes=[
            pltpu.VMEM((SIDE, 2 * SIDE), F32),
            pltpu.VMEM((3, 256, 384), F32),
            pltpu.VMEM((3, 256, 128), F32),
            pltpu.SemaphoreType.DMA((3,)),
        ],
        compiler_params=pltpu.CompilerParams(vmem_limit_bytes=LIMIT),
        name="second_factor",
    )(*operands)


def shards(modes, stiffness, connect, send_list, elem_count):
    modes = jnp.transpose(modes, (1, 0, 2))
    scale = float((3 * 256 * lax.axis_size("blk") * lax.axis_size("leaf")) ** 0.5)
    bottom, low, rest, r_first, r_top, i_top, q = up_to_last_gram(
        scale, elem_count, modes, stiffness, connect, send_list[0])
    q, r = second(scale, bottom, low, r_first, r_top, i_top, rest, q)
    return (jnp.transpose(q, (1, 0, 2)), r)


def solution(mesh):
    placed = (
        P(("blk", "leaf"), None, None),
        P(None, None, None, None, ("blk", "leaf")),
        P(None, ("blk", "leaf")),
        P(("blk", "leaf"), None, None),
        P(("blk", "leaf")),
    )
    return jax.shard_map(
        shards,
        mesh=mesh,
        in_specs=placed,
        out_specs=(P(("blk", "leaf"), None, None), P()),
        check_vma=False,
    )
```

```python
import functools

import jax
import jax.numpy as jnp
from jax import lax
from jax.experimental import pallas as pl
from jax.experimental.pallas import tpu as pltpu
from jax.sharding import PartitionSpec as P

HIGH = lax.Precision.HIGHEST
F32 = jnp.float32
BF16 = jnp.bfloat16
MESH = pl.DeviceIdType.MESH
VMEM = pl.BlockSpec(memory_space=pltpu.VMEM)
SMEM = pl.BlockSpec(memory_space=pltpu.SMEM)
LIMIT = 56 * 1024 * 1024


def dot(a, b, ca, cb, precision=None):
    return lax.dot_general(a, b, (((ca,), (cb,)), ((), ())), precision=precision, preferred_element_type=F32)


def split2(x):
    hi = x.astype(BF16)
    return hi, (x - hi.astype(F32)).astype(BF16)


def split3(x):
    hi = x.astype(BF16)
    rest = x - hi.astype(F32)
    mid = rest.astype(BF16)
    return hi, mid, (rest - mid.astype(F32)).astype(BF16)


def columns_of(rows, count):
    padded = jnp.concatenate([rows.astype(F32), jnp.zeros((16 - count, 128), F32)], axis=0)
    return padded.T


N_LEAF = 16
N_BLK = 8


def greet(leaf, blk):
    barrier = pltpu.get_barrier_semaphore()
    for k in range(1, N_LEAF):
        pl.semaphore_signal(barrier, inc=1, device_id={"leaf": lax.rem(leaf + k, N_LEAF)}, device_id_type=MESH)
    for k in range(1, N_BLK):
        pl.semaphore_signal(barrier, inc=1, device_id={"blk": lax.rem(blk + k, N_BLK)}, device_id_type=MESH)
    return barrier


class Sum:
    def __init__(self, leaf, blk, local, near, far, total, leaf_sems, blk_sems):
        size = local.shape[0] // N_LEAF
        self.blk = blk
        self.local, self.near, self.far, self.total = local, near, far, total
        mine = pl.ds(pl.multiple_of(leaf * size, 8), size)
        self.mine = mine
        self.spread, self.cross, self.collect = [], [], []
        for k in range(1, N_LEAF):
            peer = lax.rem(leaf + k, N_LEAF)
            self.spread.append(pltpu.make_async_remote_copy(
                src_ref=local.at[pl.ds(pl.multiple_of(peer * size, 8), size)], dst_ref=near.at[k],
                send_sem=leaf_sems.at[0, k], recv_sem=leaf_sems.at[1, k], device_id={"leaf": peer}, device_id_type=MESH))
            self.collect.append(pltpu.make_async_remote_copy(
                src_ref=total.at[mine], dst_ref=total.at[mine],
                send_sem=leaf_sems.at[2, k], recv_sem=leaf_sems.at[3, k], device_id={"leaf": peer}, device_id_type=MESH))
        for k in range(1, N_BLK):
            peer = lax.rem(blk + k, N_BLK)
            self.cross.append(pltpu.make_async_remote_copy(
                src_ref=far.at[blk], dst_ref=far.at[blk],
                send_sem=blk_sems.at[0, k], recv_sem=blk_sems.at[1, k], device_id={"blk": peer}, device_id_type=MESH))

    def begin(self, *parts):
        for n, part in enumerate(parts):
            self.local[128 * n : 128 * (n + 1), :] = part
        for copy in self.spread:
            copy.start()

    def across(self):
        part = self.local[self.mine, :]
        for k, copy in enumerate(self.spread):
            copy.wait_recv()
            part = part + self.near[k + 1]
        self.far[self.blk] = part
        for copy in self.cross:
            copy.start()

    def gather(self):
        for copy in self.cross:
            copy.wait_recv()
        part = self.far[0]
        for b in range(1, N_BLK):
            part = part + self.far[b]
        self.total[self.mine, :] = part
        for copy in self.collect:
            copy.start()

    def end(self):
        for copy in self.collect:
            copy.wait_recv()

    def drain(self):
        for copy in self.spread + self.cross + self.collect:
            copy.wait_send()


def sum_scratch(parts):
    size = 128 * parts // N_LEAF
    return [
        pltpu.VMEM((128 * parts, 128), F32),
        pltpu.VMEM((N_LEAF, size, 128), F32),
        pltpu.VMEM((N_BLK, size, 128), F32),
        pltpu.VMEM((128 * parts, 128), F32),
        pltpu.SemaphoreType.DMA((4, N_LEAF)),
        pltpu.SemaphoreType.DMA((2, N_BLK)),
    ]


SIDE = 128
BLOCK = 32


def factor_start(work, gram):
    work[:, 0:SIDE] = gram
    work[:, SIDE:] = (
        lax.broadcasted_iota(jnp.int32, (SIDE, SIDE), 0) == lax.broadcasted_iota(jnp.int32, (SIDE, SIDE), 1)
    ).astype(F32)


def factor(work, start):
    sub = lax.broadcasted_iota(jnp.int32, (8, 128), 0)
    if start:
        update = dot(work[0:start, start : start + BLOCK], work[0:start, :], 0, 0, HIGH)
        work[start : start + BLOCK, :] = work[start : start + BLOCK, :] - update
    count = BLOCK // 8
    tiles = 2
    x = [[work[start + 8 * t : start + 8 * t + 8, 128 * i : 128 * (i + 1)] for i in range(tiles)] for t in range(count)]
    for p in range(count):
        lane = start + 8 * p
        rest = range(p, count)
        col = [{t: jnp.broadcast_to(x[t][0][:, lane + j : lane + j + 1], (8, 128)) for t in rest} for j in range(8)]
        for j in range(8):
            inverse = lax.rsqrt(jnp.broadcast_to(col[j][p][j : j + 1, :], (8, 128)))
            low = {t: col[j][t] * inverse for t in rest}
            for k in range(j + 1, 8):
                pivot = jnp.broadcast_to(low[p][k : k + 1, :], (8, 128))
                for t in rest:
                    col[k][t] = col[k][t] - low[t] * pivot
            for i in range(tiles):
                row = jnp.broadcast_to(x[p][i][j : j + 1, :], (8, 128)) * inverse
                for t in rest:
                    moved = x[t][i] - low[t] * row
                    if t == p:
                        moved = jnp.where(sub > j, moved, jnp.where(sub == j, row, x[t][i]))
                    x[t][i] = moved
        for i in range(tiles):
            work[start + 8 * p : start + 8 * p + 8, 128 * i : 128 * (i + 1)] = x[p][i]


def factor_half(work, half):
    for start in range(64 * half, 64 * half + 64, BLOCK):
        factor(work, start)


def factored(work):
    keep = lax.broadcasted_iota(jnp.int32, (SIDE, SIDE), 0) <= lax.broadcasted_iota(jnp.int32, (SIDE, SIDE), 1)
    return jnp.where(keep, work[:, 0:SIDE], 0.0), work[:, SIDE:]


def dot3(a, b, ca, cb):
    (ah, al), (bh, bl) = split2(a), split2(b)
    return dot(ah, bh, ca, cb) + (dot(ah, bl, ca, cb) + dot(al, bh, ca, cb))


TOTAL = N_LEAF * N_BLK
STEPS = (-1, 1)


class Exchange:
    def __init__(self, device, near, far, relay, near_to, far_to, sems):
        self.near_to, self.far_to = near_to, far_to
        self.direct, self.away, self.onward = [], [], []
        self.one, self.two, self.from_one, self.from_two = [], [], [], []
        self.between = (device >= 1) & (device < TOTAL - 1)
        for u, step in enumerate(STEPS):
            peer = lax.rem(device + step + TOTAL, TOTAL)
            there = (lax.div(peer, N_LEAF), lax.rem(peer, N_LEAF))

            def copy(kind, src, dst):
                return pltpu.make_async_remote_copy(
                    src_ref=src, dst_ref=dst, send_sem=sems.at[0, kind, u], recv_sem=sems.at[1, kind, u],
                    device_id=there, device_id_type=MESH)

            self.direct.append(copy(0, near[u], near_to[u]))
            self.away.append(copy(1, far[u], relay.at[u]))
            self.onward.append(copy(2, relay.at[u], far_to[u]))
            self.one.append(self.within(device + step))
            self.two.append(self.within(device + 2 * step))
            self.from_one.append(self.within(device - step))
            self.from_two.append(self.within(device - 2 * step))

    def within(self, device):
        return (device >= 0) & (device < TOTAL)

    def send_far(self):
        for u in range(2):
            pl.when(self.two[u])(self.away[u].start)

    def send_near(self):
        for u in range(2):
            pl.when(self.one[u])(self.direct[u].start)

    def forward(self):
        for u in range(2):
            @pl.when(self.between)
            def _():
                self.away[u].wait_recv()
                self.onward[u].start()

    def receive(self, arrives, copy, to):
        pl.when(arrives)(copy.wait_recv)

        @pl.when(jnp.logical_not(arrives))
        def _():
            to[...] = jnp.zeros(to.shape, F32)

    def receive_near(self):
        for u in range(2):
            self.receive(self.from_one[u], self.direct[u], self.near_to[u])

    def receive_far(self):
        for u in range(2):
            self.receive(self.from_two[u], self.onward[u], self.far_to[u])

    def drain(self):
        for u in range(2):
            pl.when(self.two[u])(self.away[u].wait_send)
            pl.when(self.one[u])(self.direct[u].wait_send)
            pl.when(self.between)(self.onward[u].wait_send)


STORED = (512, 256, 384, 640)
NEAR_OUT, FAR_OUT = (1, 2), (0, 3)
NEAR_BACK, FAR_BACK = (2, 1), (3, 0)


def main_kernel(scale, count, modes, stiffness, connect, send, bottom_out, low_out, rest_out, r_out, top_out, inv_out, q_out,
                outgoing, table, relay, acc, incoming, relay_back, halo_sems, back_sems,
                ext, pick, place, taken, blocks, matrix_hi, matrix_lo, product, stiff, work, *sums):
    leaf, blk = lax.axis_index("leaf"), lax.axis_index("blk")
    device = blk * N_LEAF + leaf
    barrier = greet(leaf, blk)

    def rows_of(ref, h, j):
        return ref.at[h, pl.ds(STORED[j], 128)]

    halo, back = [], []
    for h in range(2):
        halo.append(Exchange(
            device, [outgoing.at[h, j] for j in NEAR_OUT], [outgoing.at[h, j] for j in FAR_OUT], relay.at[h],
            [rows_of(table, h, j) for j in NEAR_OUT], [rows_of(table, h, j) for j in FAR_OUT], halo_sems.at[h]))
        back.append(Exchange(
            device, [rows_of(acc, h, j) for j in NEAR_BACK], [rows_of(acc, h, j) for j in FAR_BACK], relay_back.at[h],
            [incoming.at[h, j] for j in NEAR_BACK], [incoming.at[h, j] for j in FAR_BACK], back_sems.at[h]))
    greeted = N_LEAF + N_BLK - 2
    for u, step in enumerate(STEPS):
        peer = lax.rem(device + step + TOTAL, TOTAL)
        there = (lax.div(peer, N_LEAF), lax.rem(peer, N_LEAF))
        greeted = greeted + halo[0].from_one[u].astype(jnp.int32)

        @pl.when(halo[0].one[u])
        def _():
            pl.semaphore_signal(barrier, inc=1, device_id=there, device_id_type=MESH)

    first, cross, top, bottom = (Sum(leaf, blk, *sums[6 * i : 6 * i + 6]) for i in range(4))

    chosen = send[...]
    columns = columns_of(chosen, 4)
    nodes = lax.broadcasted_iota(jnp.int32, (128, 256), 1).astype(F32)
    choosers = [(columns[:, j : j + 1] == nodes).astype(BF16) for j in range(4)]

    wides = [jnp.concatenate([modes[c, :, 128 * h : 128 * (h + 1)] for c in range(3)], axis=1) for h in range(2)]
    parts = [split3(wide) for wide in wides]
    sent = [jnp.concatenate(part, axis=1) for part in parts]

    def prepare(h, directions):
        for j in directions:
            found = dot(choosers[j], sent[h], 1, 0)
            outgoing[h, j] = found[:, 0:384] + (found[:, 384:768] + found[:, 768:1152])

    prepare(0, FAR_OUT)
    pl.semaphore_wait(barrier, greeted)
    halo[0].send_far()
    prepare(0, NEAR_OUT)
    halo[0].send_near()
    gram = sum(dot3(modes[c].T, modes[c], 1, 0) for c in range(3))
    first.begin(gram[0:128, 0:128], gram[128:256, 0:128], gram[128:256, 128:256])
    prepare(1, FAR_OUT + NEAR_OUT)
    for h in range(2):
        table[h, 0:256, :] = wides[h]
        ext[h, 0:256, 0:384], ext[h, 0:256, 384:768] = parts[h][0], parts[h][1]

    conn = connect[...]
    columns = columns_of(conn, 10)

    def table_id(at):
        return jnp.where(at < 256, at, jnp.where(at < 512, at + 128, jnp.where(at < 640, at - 256, at)))

    lanes = table_id(lax.broadcasted_iota(jnp.int32, (128, 768), 1)).astype(F32)
    rows = table_id(lax.broadcasted_iota(jnp.int32, (768, 128), 0))
    for k in range(10):
        pick[128 * k : 128 * (k + 1), :] = (columns[:, k : k + 1] == lanes).astype(BF16)
        place[:, 128 * k : 128 * (k + 1)] = (rows == conn[k : k + 1, :]).astype(BF16)

    halo[0].forward()
    halo[1].send_far()
    halo[1].send_near()

    def gather(h, part):
        span = slice(256 * part, 256 * (part + 1))
        if part:
            ext[h, span, 0:384], ext[h, span, 384:768] = split2(table[h, span, :])

        def body(step, carry):
            at = pl.ds(pl.multiple_of(step * 320, 320), 320)
            picked = pick[at, span]
            found = dot(picked, ext[h, span, :], 1, 0)
            found = found[:, 0:384] + found[:, 384:768]
            taken[h, at, :] = found if part == 0 else taken[h, at, :] + found
            return carry

        lax.fori_loop(0, 4, body, 0)

    gather(0, 0)
    gather(1, 0)

    live = lax.broadcasted_iota(jnp.int32, (30, 128), 1) < count[0]
    source = lax.broadcasted_iota(jnp.int32, (30, 256), 0)
    target = lax.broadcasted_iota(jnp.int32, (30, 256), 1)
    wanted = lax.rem(source, 3) * 10 + lax.div(source, 3)
    spread = (lax.shift_right_logical(target, 3) == wanted).astype(BF16)
    for k in range(10):
        for c in range(3):
            block = jnp.concatenate([stiffness[k, c, l] for l in range(10)], axis=0)
            hi, lo = split2(jnp.where(live, block, 0.0))
            blocks[10 * c + k] = dot(hi, spread, 0, 0) + dot(lo, spread, 0, 0)

    keep = lax.broadcasted_iota(jnp.int32, (8, 256), 0) == lax.rem(lax.broadcasted_iota(jnp.int32, (8, 256), 1), 8)

    def assemble(g, carry):
        at = pl.ds(pl.multiple_of(g * 8, 8), 8)
        matrix = jnp.concatenate([jnp.where(keep, blocks[n, at, :], 0.0) for n in range(30)], axis=0)
        matrix_hi[g], matrix_lo[g] = split2(matrix)
        return carry

    lax.fori_loop(0, 16, assemble, 0)

    def multiply(h):
        def group(g, carry):
            spans = [pl.ds(pl.multiple_of(128 * k + g * 8, 8), 8) for k in range(10)]
            vectors = jnp.concatenate(
                [taken[h, spans[l], 128 * d : 128 * (d + 1)] for d in range(3) for l in range(10)]
                + [jnp.zeros((16, 128), F32)],
                axis=0,
            )
            v_hi, v_lo = split2(vectors)
            m_hi, m_lo = matrix_hi[g], matrix_lo[g]
            result = dot(m_hi, jnp.concatenate([v_hi, v_lo], axis=1), 1, 0)
            result = result[:, 0:128] + (result[:, 128:256] + dot(m_lo, v_hi, 1, 0))
            for c in range(3):
                for k in range(10):
                    n = 10 * c + k
                    product[spans[k], 128 * c : 128 * (c + 1)] = result[8 * n : 8 * n + 8, :]
            return carry

        lax.fori_loop(0, 16, group, 0, unroll=4)
        return jnp.concatenate(split2(product[...]), axis=1)

    def scatter(h, halves, span):
        where = place[span, :]
        found = dot(where, halves, 1, 0)
        acc[h, span, :] = found[:, 0:384] + found[:, 384:768]

    OWN, NEAR, FAR = slice(0, 256), slice(256, 512), slice(512, 768)

    halo[0].receive_near()
    gather(0, 1)
    halo[0].receive_far()
    gather(0, 2)
    halves = multiply(0)
    halo[1].forward()
    scatter(0, halves, FAR)
    back[0].send_far()
    scatter(0, halves, NEAR)
    back[0].send_near()
    first.across()
    scatter(0, halves, OWN)
    halo[1].receive_near()
    gather(1, 1)
    halo[1].receive_far()
    gather(1, 2)
    first.gather()
    halves = multiply(1)
    back[0].forward()
    scatter(1, halves, FAR)
    back[1].send_far()
    scatter(1, halves, NEAR)
    back[1].send_near()
    scatter(1, halves, OWN)

    lower, diagonal = [], 0.0
    for c in range(3):
        at = slice(128 * c, 128 * (c + 1))
        low_at = slice(384 + 128 * c, 512 + 128 * c)
        tables = [jnp.concatenate([ext[0, :, lanes], ext[1, :, lanes]], axis=1) for lanes in (at, low_at)]
        for h in range(2):
            hi, lo = split2(acc[h, :, at].T)
            t_hi, t_lo = (t if h else t[:, 0:128] for t in tables)
            found = dot(hi, t_hi, 1, 0) + (dot(hi, t_lo, 1, 0) + dot(lo, t_hi, 1, 0))
            if h:
                lower.append(found)
            else:
                diagonal = diagonal + found
    lower = sum(lower)
    cross.begin(diagonal, lower[:, 0:128], lower[:, 128:256])

    rows = lax.broadcasted_iota(jnp.int32, (256, 128), 0)
    to_own = jnp.concatenate([(rows == chosen[j : j + 1, :]).astype(BF16) for j in range(4)], axis=1)

    def complete(h):
        back[h].receive_near()
        back[h].receive_far()
        parts = split2(jnp.concatenate([incoming[h, j] for j in range(4)], axis=0))
        found = dot(to_own, jnp.concatenate(parts, axis=1), 1, 0)
        whole = acc[h, OWN, :] + (found[:, 0:384] + found[:, 384:768])
        for c in range(3):
            stiff[c, :, 128 * h : 128 * (h + 1)] = whole[:, 128 * c : 128 * (c + 1)]

    first.end()
    factor_start(work, first.total[0:128, :])
    factor_half(work, 0)
    back[1].forward()
    factor_half(work, 1)
    r00, i00 = factored(work)
    complete(0)
    top.begin(sum(dot3(stiff[c, :, 0:128].T, stiff[c, :, 0:128], 1, 0) for c in range(3)))
    r01 = dot3(i00, first.total[128:256, :], 1, 1)
    factor_start(work, first.total[256:384, :] - dot(r01, r01, 0, 0, HIGH))
    factor_half(work, 0)
    factor_half(work, 1)
    r11, i11 = factored(work)
    r_out[0:128, 0:128], r_out[0:128, 128:256] = r00, r01
    r_out[128:256, 0:128], r_out[128:256, 128:256] = jnp.zeros((SIDE, SIDE), F32), r11
    i10 = dot3(i11, dot3(r01.T, i00, 1, 0), 1, 0)
    inv = jnp.concatenate(
        [jnp.concatenate([i00, jnp.zeros((SIDE, SIDE), F32)], axis=1), jnp.concatenate([-i10, i11], axis=1)], axis=0)
    cross.across()
    top.across()
    for c in range(3):
        q_out[c, :, 0:256] = dot3(modes[c], inv, 1, 1) * scale

    cross.gather()
    top.gather()
    complete(1)
    both = sum(dot3(stiff[c, :, 128:256].T, stiff[c], 1, 0) for c in range(3))
    bottom.begin(both[:, 0:128], both[:, 128:256])
    cross.end()
    crossed = cross.total
    gram = jnp.concatenate(
        [jnp.concatenate([crossed[0:128, :], crossed[128:256, :].T], axis=1),
         jnp.concatenate([crossed[128:256, :], crossed[256:384, :]], axis=1)], axis=0)
    low = dot3(gram, inv, 1, 1)
    low_out[...] = low
    top.end()
    factor_start(work, top.total[...] - dot(low[0:128, :], low[0:128, :], 1, 1, HIGH))
    factor_half(work, 0)
    bottom.across()
    for c in range(3):
        stiff[c] = stiff[c] - dot3(q_out[c, :, 0:256], low / scale, 1, 1)
    factor_half(work, 1)
    bottom.gather()
    r22, i22 = factored(work)
    top_out[...] = r22
    inv_out[...] = i22
    for c in range(3):
        q_out[c, :, 256:384] = dot3(stiff[c, :, 0:128], i22, 1, 1) * scale
        rest_out[c] = stiff[c, :, 128:256]
    for h in range(2):
        halo[h].drain()
        back[h].drain()
    first.drain()
    cross.drain()
    top.drain()
    bottom.end()
    bottom.drain()
    bottom_out[...] = bottom.total[...]


def up_to_last_gram(scale, count, modes, stiffness, connect, send):
    shapes = ((256, 128), (256, 256), (3, 256, 128), (256, 256), (128, 128), (128, 128), (3, 256, 384))
    rows = pltpu.VMEM((2, 4, 128, 384), F32)
    table = pltpu.VMEM((2, 768, 384), F32)
    relay = pltpu.VMEM((2, 2, 128, 384), F32)
    sems = pltpu.SemaphoreType.DMA((2, 2, 3, 2))
    return pl.pallas_call(
        functools.partial(main_kernel, scale),
        out_shape=[jax.ShapeDtypeStruct(shape, F32) for shape in shapes],
        in_specs=[SMEM] + [VMEM] * 4,
        out_specs=[VMEM] * len(shapes),
        scratch_shapes=[
            rows, table, relay, table, rows, relay, sems, sems,
            pltpu.VMEM((2, 768, 768), BF16),
            pltpu.VMEM((1280, 768), BF16),
            pltpu.VMEM((768, 1280), BF16),
            pltpu.VMEM((2, 1280, 384), F32),
            pltpu.VMEM((30, 128, 256), F32),
            pltpu.VMEM((16, 240, 256), BF16),
            pltpu.VMEM((16, 240, 256), BF16),
            pltpu.VMEM((1280, 384), F32),
            pltpu.VMEM((3, 256, 256), F32),
            pltpu.VMEM((SIDE, 2 * SIDE), F32),
        ] + sum_scratch(3) + sum_scratch(3) + sum_scratch(1) + sum_scratch(2),
        compiler_params=pltpu.CompilerParams(collective_id=1, has_side_effects=True, vmem_limit_bytes=LIMIT),
        name="up_to_last_gram",
    )(count, modes, stiffness, connect, send)


def second_kernel(scale, bottom, low, r_first, r_top, i_top, rest, q_in, q_out, r_out, work, columns, last, sems):
    fetch = pltpu.make_async_copy(q_in, columns, sems.at[0])
    done = pltpu.make_async_copy(columns, q_out.at[:, :, pl.ds(0, 384)], sems.at[1])
    fetch.start()
    low0, low1 = low[0:128, :], low[128:256, :]
    side = bottom[0:128, :] - dot3(low1, low0, 1, 1)
    r01 = dot3(i_top[...], side, 1, 1)
    factor_start(work, bottom[128:256, :] - dot(low1, low1, 1, 1, HIGH) - dot(r01, r01, 0, 0, HIGH))
    factor_half(work, 0)
    fetch.wait()
    done.start()
    r_out[0:256, 0:256] = r_first[...] / scale
    r_out[0:256, 256:512] = low[...].T / scale
    r_out[256:512, 0:256] = jnp.zeros((256, 256), F32)
    r_out[256:384, 256:384] = r_top[...] / scale
    r_out[256:384, 384:512] = r01 / scale
    r_out[384:512, 256:384] = jnp.zeros((128, 128), F32)
    factor_half(work, 1)
    r11, i11 = factored(work)
    r_out[384:512, 384:512] = r11 / scale
    for c in range(3):
        left = rest[c] - dot3(columns[c, :, 256:384], r01 / scale, 1, 0)
        last[c] = dot3(left, i11, 1, 1) * scale
    place = pltpu.make_async_copy(last, q_out.at[:, :, pl.ds(384, 128)], sems.at[2])
    place.start()
    place.wait()
    done.wait()


def second(scale, *operands):
    anywhere = pl.BlockSpec(memory_space=pl.ANY)
    return pl.pallas_call(
        functools.partial(second_kernel, scale),
        out_shape=[jax.ShapeDtypeStruct((3, 256, 512), F32), jax.ShapeDtypeStruct((512, 512), F32)],
        in_specs=[VMEM] * 6 + [anywhere],
        out_specs=[anywhere, VMEM],
        scratch_shapes=[
            pltpu.VMEM((SIDE, 2 * SIDE), F32),
            pltpu.VMEM((3, 256, 384), F32),
            pltpu.VMEM((3, 256, 128), F32),
            pltpu.SemaphoreType.DMA((3,)),
        ],
        compiler_params=pltpu.CompilerParams(vmem_limit_bytes=LIMIT),
        name="second_factor",
    )(*operands)


def shards(modes, stiffness, connect, send_list, elem_count):
    modes = jnp.transpose(modes, (1, 0, 2))
    scale = float((3 * 256 * lax.axis_size("blk") * lax.axis_size("leaf")) ** 0.5)
    bottom, low, rest, r_first, r_top, i_top, q = up_to_last_gram(
        scale, elem_count, modes, stiffness, connect, send_list[0])
    q, r = second(scale, bottom, low, r_first, r_top, i_top, rest, q)
    return (jnp.transpose(q, (1, 0, 2)), r)


def solution(mesh):
    placed = (
        P(("blk", "leaf"), None, None),
        P(None, None, None, None, ("blk", "leaf")),
        P(None, ("blk", "leaf")),
        P(("blk", "leaf"), None, None),
        P(("blk", "leaf")),
    )
    return jax.shard_map(
        shards,
        mesh=mesh,
        in_specs=placed,
        out_specs=(P(("blk", "leaf"), None, None), P()),
        check_vma=False,
    )
```
